128 devices in a mesh: lat: 8 (over z, y_hi), lon: 16 (over x, y_lo, core).
Axes of the slice: x: 4, y: 4 (y_hi: 2, y_lo: 2; y = y_hi * 2 + y_lo), z: 4, core: 2. Of those that a mesh axis runs over, the one named last changes fastest.
Arguments:
- obs_values: bfloat16 [1048576, 24], P(('lat', 'lon')), may hold values from -6 to 6
- tile_ids: int32 [1048576, 1], P(('lat', 'lon')), may hold values from 0 to 127; in each aligned block of 8192 rows (0 to 8191, 8192 to 16383, ...) at most 128 rows name the same one
- obs_rows: float32 [1048576], P(('lat', 'lon')), may hold values from 0 to 16
- obs_cols: float32 [1048576], P(('lat', 'lon')), may hold values from 0 to 128
- w_embed: bfloat16 [24, 128], replicated, may hold values from -0.25 to 0.25
- w_first: bfloat16 [3, 3, 128, 128], replicated, may hold values from -0.1875 to 0.1875
- w_second: bfloat16 [3, 3, 128, 128], replicated, may hold values from -0.1875 to 0.1875
- cotangent: bfloat16 [128, 2048, 128], P('lat', 'lon'), may hold values from -0.01171875 to 0.01171875
Outputs:
- field: bfloat16 [128, 2048, 128], P('lat', 'lon')
- grad_embed: float32 [24, 128], replicated
- grad_first: float32 [3, 3, 128, 128], replicated
- grad_second: float32 [3, 3, 128, 128], replicated
The draws below stay inside these ranges and needn't reach their ends.
Inputs may be any that keep to these rules, and one draw needn't show every extreme that they name: `tile_ids`: within the rows of one device no tile is named by more than 128 rows, and in every draw some device names some tile exactly 128 times.
All inputs are finite; a program needn't handle non-finite values.
Results may differ from the reference program's by a relative error of at most 0.0083.
Values may be sent and summed in bfloat16 or wider, within the bound.
No kernel may reach another device: no remote copies, remote signals or barrier semaphores. Data moves between devices by JAX's collectives and lax.ppermute only.
A program may use at most 64 MiB of HBM per device.

```python
import math
import jax
import jax.numpy as jnp
import numpy as np
from jax import lax

C = 128
NVAL = 24
CH = 16
CW = 128
OBS_DEV = 8192
BANDS = 8
SECTORS = 16
ROWS = 128
COLS = 2048
CAP = 128
SLOTS = 16384
OBS = 1048576
N_LAT = 8
N_LON = 16


def level_of(stream_key, shape, split, smallest, largest):
    loudness, own = 1.0, jax.random.fold_in(stream_key, 6)
    for dim, shards_of in split:
        draws = jnp.exp(jax.random.uniform(jax.random.fold_in(own, dim), (shards_of,), jnp.float32, smallest / len(split), largest / len(split)))
        loudness = loudness * jnp.repeat(draws, shape[dim] // shards_of).reshape([-1 if axis == dim else 1 for axis in range(len(shape))])
    return loudness


def shared_out(own_key, own, number, rows, number_of, top, reach, slope):
    ranking = jax.random.permutation(own_key, number_of)
    crowded, common = shares(number_of, rows * top, reach, slope, True), shares(number_of, rows * top, reach, slope, False)
    places = jnp.arange(number_of)

    def named(lengths, offset_by):
        used = int((lengths > 0).sum())
        fixed = max(1, used // 4)
        shifted = fixed + (places - fixed + offset_by * (used - fixed)) % max(1, number_of - fixed)
        return jnp.zeros((number_of,), jnp.int32).at[ranking[jnp.where(places < fixed, places, shifted)]].set(jnp.asarray(lengths, jnp.int32))

    lengths = jnp.where(number % 4 == 0, named(crowded, number // 4), named(common, number - number // 4 - 1))
    mixed = jax.random.permutation(jax.random.fold_in(own, 3), number_of)
    source_of, taker = mixed[0:number_of // 2 * 2:2], mixed[1:number_of // 2 * 2:2]
    margin = jnp.minimum(lengths[source_of] - 1, reach - lengths[taker]) // 2
    margin = jnp.where((source_of == ranking[0]) | (taker == ranking[0]) | (lengths[taker] == 0), 0, jnp.maximum(margin, 0))
    shifted = jax.random.randint(jax.random.fold_in(own, 4), (number_of // 2,), 0, 1 << 20) % (margin + 1)
    lengths = lengths.at[source_of].add(-shifted).at[taker].add(shifted)
    items = jnp.searchsorted(jnp.cumsum(lengths), jnp.arange(rows * top), side="right").astype(jnp.int32)
    table = items.reshape(top, rows).T
    table = table[jax.random.permutation(jax.random.fold_in(own, 1), rows)]
    offset_by = jax.random.randint(jax.random.fold_in(own, 2), (rows, 1), 0, top)
    return jnp.take_along_axis(table, (jnp.arange(top)[None, :] + offset_by) % top, axis=1)


def shares(amount, total, reach, lean, full):
    portions = [(1 << 20) // math.isqrt(rank ** lean) + 1 for rank in range(1, amount + 1)]
    largest = reach if full else min(reach, max(-(-total // amount), total * portions[0] // sum(portions)))
    least = 1 if total - largest >= amount - 1 else 0
    holding, surplus = [largest] + [least] * (amount - 1), total - largest - least * (amount - 1)
    while surplus > 0:
        free = [i for i in range(1, amount) if holding[i] < largest] or [i for i in range(1, amount) if holding[i] < reach]
        pool, left = sum([portions[i] for i in free]), surplus
        for i in free:
            extra = min(reach - holding[i], max(1, left * portions[i] // pool), surplus)
            holding[i] = holding[i] + extra
            surplus = surplus - extra
    return np.array(holding)


def centred(stream_key, extent, scale, reach, shards=(), kind=jnp.bfloat16):
    drawn = jax.random.normal(stream_key, extent, jnp.float32) * scale
    if len(shards) > 0:
        drawn = level_of(stream_key, extent, shards, -0.22, 0.18) * drawn
    return jnp.clip(drawn, min=-reach, max=reach).astype(kind)


def setup_inputs(seed: int = 0) -> dict:
    keys = jax.random.split(jax.random.key(seed), 9)
    obs_values = centred(keys[0], (OBS, NVAL), 1.0, 6.0, ((0, 128),))
    tile_ids_keys = jax.random.split(jax.random.fold_in(keys[1], 1), OBS // OBS_DEV)
    tile_ids_turns = jax.random.permutation(jax.random.fold_in(keys[1], 3), OBS // OBS_DEV)
    tile_ids = jax.vmap(lambda own, number: shared_out(jax.random.fold_in(keys[1], 2), own, number, OBS_DEV, N_LAT * N_LON, 1, CAP, 2))(tile_ids_keys, tile_ids_turns).reshape((OBS, 1))
    obs_rows = jnp.clip(16.0 * jax.random.uniform(keys[2], (OBS,), jnp.float32) ** level_of(keys[2], (OBS,), ((0, 128),), -0.2, 0.2), 0.0, 16.0)
    obs_cols = jnp.clip(128.0 * jax.random.uniform(keys[3], (OBS,), jnp.float32) ** level_of(keys[3], (OBS,), ((0, 128),), -0.2, 0.2), 0.0, 128.0)
    w_embed = centred(keys[4], (NVAL, C), (25 * NVAL) ** -0.5, 0.25)
    w_first = centred(keys[5], (3, 3, C, C), (9 * C) ** -0.5, 0.1875)
    w_second = centred(keys[6], (3, 3, C, C), (9 * C) ** -0.5, 0.1875)
    cotangent = centred(keys[7], (ROWS, COLS, C), ((CH * CW * N_LAT * N_LON) ** -0.5), 0.01171875, ((0, 8), (1, 16)))
    return {"obs_values": obs_values, "tile_ids": tile_ids, "obs_rows": obs_rows, "obs_cols": obs_cols, "w_embed": w_embed, "w_first": w_first, "w_second": w_second, "cotangent": cotangent}


spread_cells = 1.0

def assign_slots(target):
    owners = jnp.arange(BANDS * SECTORS, dtype=jnp.int32)
    onehot = (target[:, None] == owners[None, :]).astype(jnp.int32)
    running = jnp.cumsum(onehot, axis=0) - 1
    return lax.optimization_barrier(jnp.sum(running * onehot, axis=1)).astype(jnp.int32)

def set_conv(packed):
    values, row_pos, col_pos = packed
    centre_row = jnp.arange(CH, dtype=jnp.float32) + 0.5
    centre_col = jnp.arange(CW, dtype=jnp.float32) + 0.5
    scale_two = 2.0 * spread_cells * spread_cells
    row_weight = jnp.exp(-jnp.square(row_pos[None, :] - centre_row[:, None]) / scale_two)
    col_weight = jnp.exp(-jnp.square(col_pos[None, :] - centre_col[:, None]) / scale_two).astype(jnp.bfloat16)
    weighted = (row_weight[:, None, :] * values.T.astype(jnp.float32)[None, :, :]).astype(jnp.bfloat16)
    summed = jnp.dot(weighted.reshape(CH * NVAL, SLOTS), col_weight.T, preferred_element_type=jnp.float32)
    return summed.astype(jnp.bfloat16).reshape(CH, NVAL, CW)

def to_tiles(field_grid):
    return field_grid.reshape(BANDS, CH, SECTORS, CW, -1).transpose(0, 2, 1, 3, 4)

def to_grid(tile_view):
    return tile_view.transpose(0, 2, 1, 3, 4).reshape(ROWS, COLS, -1)

def extend(field_grid):
    half_turn = COLS // 2
    upper_row = jnp.roll(field_grid[:1], -half_turn, axis=1)
    lower_row = jnp.roll(field_grid[-1:], -half_turn, axis=1)
    with_poles = jnp.concatenate([upper_row, field_grid, lower_row], axis=0)
    wrapped = jnp.concatenate([with_poles[:, -1:], with_poles, with_poles[:, :1]], axis=1)
    row_index = (jnp.arange(BANDS, dtype=jnp.int32)[:, None] * CH + jnp.arange(CH + 2, dtype=jnp.int32)[None, :]).reshape(-1)
    col_index = (jnp.arange(SECTORS, dtype=jnp.int32)[:, None] * CW + jnp.arange(CW + 2, dtype=jnp.int32)[None, :]).reshape(-1)
    picked = jnp.take(wrapped, row_index, axis=0).reshape(BANDS, CH + 2, COLS + 2, -1)
    picked = jnp.take(picked, col_index, axis=2).reshape(BANDS, CH + 2, SECTORS, CW + 2, -1)
    return picked.transpose(0, 2, 1, 3, 4)

def convolve(blocks, weight):
    out_shape = (BANDS, SECTORS, CH, CW, weight.shape[3])
    summed = jnp.zeros((BANDS * SECTORS * CH * CW, weight.shape[3]), jnp.float32)
    for row_off in range(3):
        for col_off in range(3):
            window = blocks[:, :, row_off:row_off + CH, col_off:col_off + CW].reshape(-1, weight.shape[2])
            summed = summed + jnp.dot(window, weight[row_off, col_off], preferred_element_type=jnp.float32)
    return summed.reshape(out_shape)

def weight_terms(blocks, upstream):
    flat_up = upstream.reshape(-1, upstream.shape[-1])
    kernel_rows = []
    for row_off in range(3):
        kernel_cols = []
        for col_off in range(3):
            window = blocks[:, :, row_off:row_off + CH, col_off:col_off + CW].reshape(-1, blocks.shape[-1])
            kernel_cols.append(jnp.dot(window.T, flat_up, preferred_element_type=jnp.float32))
        kernel_rows.append(jnp.stack(kernel_cols))
    return jnp.stack(kernel_rows)

def spread_back(upstream, weight):
    flat_up = upstream.reshape(-1, upstream.shape[-1])
    summed = jnp.zeros((BANDS, SECTORS, CH + 2, CW + 2, weight.shape[2]), jnp.float32)
    for row_off in range(3):
        for col_off in range(3):
            product = jnp.dot(flat_up, weight[row_off, col_off].T, preferred_element_type=jnp.float32)
            product = product.reshape(BANDS, SECTORS, CH, CW, weight.shape[2])
            summed = summed.at[:, :, row_off:row_off + CH, col_off:col_off + CW].add(product)
    return summed.astype(jnp.bfloat16)

def reference(obs_values, tile_ids, obs_rows, obs_cols, w_embed, w_first, w_second, cotangent):
    tile_count = BANDS * SECTORS
    target = tile_ids[:, 0].astype(jnp.int32)
    slot_rank = lax.map(assign_slots, target.reshape(tile_count, OBS_DEV)).reshape(-1)
    source = jnp.repeat(jnp.arange(tile_count, dtype=jnp.int32), OBS_DEV)
    slot_index = (source * CAP + slot_rank).astype(jnp.int32)
    tile_values = jnp.zeros((tile_count, SLOTS, NVAL), jnp.bfloat16).at[target, slot_index].set(obs_values)
    tile_rows = jnp.zeros((tile_count, SLOTS), jnp.float32).at[target, slot_index].set(obs_rows)
    tile_cols = jnp.zeros((tile_count, SLOTS), jnp.float32).at[target, slot_index].set(obs_cols)
    setconv = lax.map(set_conv, (tile_values, tile_rows, tile_cols))
    embedded = jnp.einsum('tifj,fc->tijc', setconv.astype(jnp.float32), w_embed.astype(jnp.float32)).astype(jnp.bfloat16)
    embedded = embedded.reshape(BANDS, SECTORS, CH, CW, -1)
    embed_ext = extend(to_grid(embedded))
    pre_act = convolve(embed_ext, w_first)
    hidden = jax.nn.silu(pre_act).astype(jnp.bfloat16)
    hidden_ext = extend(to_grid(hidden))
    field = convolve(hidden_ext, w_second).astype(jnp.bfloat16)
    upstream = to_tiles(cotangent)
    grad_second = weight_terms(hidden_ext, upstream)
    _, pullback = jax.vjp(extend, jnp.zeros((ROWS, COLS, C), jnp.float32))
    hidden_grad = to_tiles(pullback(spread_back(upstream, w_second).astype(jnp.float32))[0])
    sigmoid_pre = jax.nn.sigmoid(pre_act)
    pre_grad = (hidden_grad * sigmoid_pre * (1.0 + pre_act * (1.0 - sigmoid_pre))).astype(jnp.bfloat16)
    grad_first = weight_terms(embed_ext, pre_grad)
    embed_grad = to_tiles(pullback(spread_back(pre_grad, w_first).astype(jnp.float32))[0]).astype(jnp.bfloat16)
    grad_embed = jnp.einsum('tifj,tijc->fc', setconv.astype(jnp.float32), embed_grad.reshape(tile_count, CH, CW, -1).astype(jnp.float32))
    return (to_grid(field), grad_embed, grad_first, grad_second)
```

```python
import functools
import math
import jax
import jax.numpy as jnp
from jax import lax
from jax.experimental import pallas as pl
from jax.experimental.pallas import tpu as pltpu
from jax.sharding import PartitionSpec as P

F32 = jnp.float32
BF16 = jnp.bfloat16
spread_cells = 1.0
ALL = ("lat", "lon")

TR, TC, C = 16, 128, 128
PITCH = TC + 16
LEN = 3040
PART = 304
FIRST = PITCH
OWN = 16 + 2 * PITCH
FEAT = 32
RED = 24


def dot(a, b):
    return jnp.dot(a, b, preferred_element_type=F32)


def dot_nt(a, b):
    return lax.dot_general(a, b, (((1,), (1,)), ((), ())), preferred_element_type=F32)


def place(i):
    return 16 + (i + 2) * PITCH


def pack_kernel(ids_ref, rows_ref, cols_ref, vals_ref, out_ref, q_ref, v_ref, pair_ref, acc_ref):
    step = pl.program_id(0)
    count = ids_ref.shape[1]
    owners = out_ref.shape[0] * pl.num_programs(0)
    sub = 256
    part = 1024
    pairs = out_ref.shape[0] // 2

    @pl.when(step == 0)
    def _():
        owner = lax.broadcasted_iota(jnp.int32, (owners, sub), 0)
        slot = lax.broadcasted_iota(jnp.int32, (sub, sub), 0)
        upto = slot <= lax.broadcasted_iota(jnp.int32, (sub, sub), 1)
        upto = jnp.concatenate(
            [jnp.where(upto, 1.0, 0.0).astype(BF16), jnp.ones((sub, 128), BF16)], axis=1
        )

        def body(k, carry):
            at = pl.ds(pl.multiple_of(k * sub, sub), sub)
            ids = ids_ref[:, at]
            hot = owner == ids
            counted = dot(jnp.where(hot, 1.0, 0.0).astype(BF16), upto)
            before = counted[:, :sub] + jnp.concatenate([carry, carry], axis=1)
            rank = jnp.sum(jnp.where(hot, before, 0.0), axis=0, keepdims=True) - 1.0
            key = rank.astype(jnp.int32) + (ids & 1) * 128
            q_ref[:, at] = jnp.where(slot == key, 1.0, 0.0).astype(BF16)
            pair_ref[:, at] = jnp.broadcast_to((ids >> 1).astype(F32), (FEAT, sub)).astype(BF16)
            rows, cols = rows_ref[:, at], cols_ref[:, at]
            rows_hi, cols_hi = rows.astype(BF16).astype(F32), cols.astype(BF16).astype(F32)
            tail = jnp.concatenate(
                [rows_hi, rows - rows_hi, cols_hi, cols - cols_hi, jnp.zeros((4, sub), F32)], axis=0
            )
            v_ref[:, at] = jnp.concatenate([vals_ref[:, at].astype(F32), tail], axis=0).astype(BF16)
            return carry + counted[:, sub:]

        lax.fori_loop(0, count // sub, body, jnp.zeros((owners, 128), F32))

    acc_ref[...] = jnp.zeros_like(acc_ref)

    def body(k, carry):
        at = pl.ds(pl.multiple_of(k * part, part), part)
        base = jnp.full((FEAT, part), (step * pairs).astype(F32), F32).astype(BF16)
        pair = pair_ref[:, at] - base
        values = v_ref[:, at]
        none = jnp.zeros_like(values)
        left = jnp.concatenate([jnp.where(pair == p, values, none) for p in range(pairs)], axis=0)
        acc_ref[...] += dot_nt(left, q_ref[:, at])
        return carry

    lax.fori_loop(0, count // part, body, 0)
    for p in range(pairs):
        out_ref[2 * p] = acc_ref[p * FEAT : (p + 1) * FEAT, :128].astype(BF16)
        out_ref[2 * p + 1] = acc_ref[p * FEAT : (p + 1) * FEAT, 128:].astype(BF16)


def pack(ids, rows, cols, values):
    count = ids.shape[1]
    owners = 128
    steps = 8
    whole = lambda a: pl.BlockSpec(a.shape, lambda i: (0, 0))
    return pl.pallas_call(
        pack_kernel,
        grid=(steps,),
        in_specs=[whole(ids), whole(rows), whole(cols), whole(values)],
        out_specs=pl.BlockSpec((owners // steps, FEAT, 128), lambda i: (i, 0, 0)),
        out_shape=jax.ShapeDtypeStruct((owners, FEAT, 128), BF16),
        scratch_shapes=[
            pltpu.VMEM((256, count), BF16),
            pltpu.VMEM((FEAT, count), BF16),
            pltpu.VMEM((FEAT, count), BF16),
            pltpu.VMEM((owners // steps // 2 * FEAT, 256), F32),
        ],
        compiler_params=pltpu.CompilerParams(vmem_limit_bytes=32 << 20),
        cost_estimate=pl.CostEstimate(flops=2 * 2048 * 256 * 8192, bytes_accessed=3 << 20, transcendentals=0),
        name="pack",
    )(ids, rows, cols, values)


def setconv_kernel(where_ref, got_ref, s_ref, left_ref, right_ref, v1_ref, v2_ref,
                   c1l_ref, c1r_ref, c2l_ref, c2r_ref, acc_ref):
    step = pl.program_id(0)
    x = jnp.concatenate([got_ref[k] for k in range(got_ref.shape[0])], axis=1).astype(F32)
    n = x.shape[1]
    alpha = math.sqrt(0.5 / math.log(2.0)) / spread_cells
    row = (x[24:25] + x[25:26]) * alpha
    col = (x[26:27] + x[27:28]) * alpha
    row_mid = (lax.broadcasted_iota(jnp.int32, (TR, n), 0).astype(F32) + 0.5) * alpha
    col_mid = (lax.broadcasted_iota(jnp.int32, (TC, n), 0).astype(F32) + 0.5) * alpha
    row_weight = jnp.exp2(-jnp.square(row - row_mid))
    col_weight = jnp.exp2(-jnp.square(col - col_mid)).astype(BF16)
    weighted = jnp.concatenate([(x * row_weight[i : i + 1]).astype(BF16) for i in range(TR)], axis=0)
    term = dot_nt(col_weight, weighted)

    @pl.when(step == 0)
    def _():
        acc_ref[...] = term

    @pl.when(step > 0)
    def _():
        acc_ref[...] += term

    @pl.when(step == pl.num_programs(0) - 1)
    def _():
        s = acc_ref[...].astype(BF16)
        s_ref[...] = s
        left_ref[...] = s[:16]
        right_ref[...] = s[TC - 16 :]
        low = where_ref[1] < where_ref[3] // 2
        top, bottom = s[:, :128], s[:, -128:]
        v1 = jnp.where(low, bottom, top)
        v2 = jnp.where(low, top, bottom)
        v1_ref[...] = v1
        v2_ref[...] = v2
        c1l_ref[...] = v1[TC - 16 :]
        c1r_ref[...] = v1[:16]
        c2l_ref[...] = v2[TC - 16 :]
        c2r_ref[...] = v2[:16]


def setconv(where, got):
    steps = 16
    fixed = lambda *shape: pl.BlockSpec(shape, lambda i: (0,) * len(shape))
    lanes = TR * FEAT
    shapes = [(TC, lanes), (16, lanes), (16, lanes), (TC, 128), (TC, 128)] + [(16, 128)] * 4
    return pl.pallas_call(
        setconv_kernel,
        grid=(steps,),
        in_specs=[
            pl.BlockSpec(memory_space=pltpu.SMEM),
            pl.BlockSpec((got.shape[0] // steps, FEAT, 128), lambda i: (i, 0, 0)),
        ],
        out_specs=[fixed(*s) for s in shapes],
        out_shape=[jax.ShapeDtypeStruct(s, BF16) for s in shapes],
        scratch_shapes=[pltpu.VMEM((TC, lanes), F32)],
        compiler_params=pltpu.CompilerParams(vmem_limit_bytes=32 << 20),
        cost_estimate=pl.CostEstimate(
            flops=2 * 512 * 256 * 16384, bytes_accessed=2 << 20, transcendentals=144 * 16384
        ),
        name="setconv",
    )(where, got)


def shifted_copies(flat_ref, out_ref, begin, parts):
    def body(k, carry):
        at = pl.multiple_of(begin + k * PART, 16)
        for s in range(3):
            piece = flat_ref[pl.ds(at, PART + 16), :]
            out_ref[pl.ds(at, PART), s * C : (s + 1) * C] = piece[7 + s : 7 + s + PART].astype(BF16)
        return carry

    lax.fori_loop(0, parts, body, 0)


def conv_rows(src_ref, at, rows, weights):
    total = dot(src_ref[pl.ds(at - PITCH, rows), :], weights[0])
    total += dot(src_ref[pl.ds(at, rows), :], weights[1])
    total += dot(src_ref[pl.ds(at + PITCH, rows), :], weights[2])
    return total


def back_rows(src_ref, at, rows, weights):
    total = dot_nt(src_ref[pl.ds(at - PITCH, rows), :], weights[0])
    total += dot_nt(src_ref[pl.ds(at, rows), :], weights[1])
    total += dot_nt(src_ref[pl.ds(at + PITCH, rows), :], weights[2])
    return total


def fill_flat(flat_ref, centre, left, right):
    first = lax.broadcasted_iota(jnp.int32, (16, C), 0) < 8
    flat_ref[:8] = jnp.zeros((8, C), F32)
    flat_ref[8:24] = left(-2)
    for i in range(-2, TR + 2):
        at = 8 + place(i)
        flat_ref[at : at + TC] = centre(i)
        after = jnp.where(first, right(i), left(i + 1)) if i < TR + 1 else right(i)
        flat_ref[at + TC : at + PITCH] = after
    end = 8 + place(TR + 2)
    flat_ref[end:] = jnp.zeros((flat_ref.shape[0] - end, C), F32)


def sides(where_ref):
    lon, lon_size = where_ref[1], where_ref[3]
    half = lon_size // 2
    own = lon < half
    left = jnp.where(lon == 0, lon_size - 1, lon - 1) < half
    right = jnp.where(lon == lon_size - 1, 0, lon + 1) < half
    return own, left, right


def arrange_back(w_ref, out_ref):
    for r in range(3):
        for s in range(3):
            out_ref[r, :, s * C : (s + 1) * C] = w_ref[2 - r, 2 - s]


def edges_kernel(where_ref, cot_ref, left_ref, right_ref, v1_ref, v2_ref, c1l_ref, c1r_ref, c2l_ref, c2r_ref):
    low, _, _ = sides(where_ref)
    left_ref[...] = cot_ref[:, :16, :]
    right_ref[...] = cot_ref[:, TC - 16 :, :]
    top, bottom = cot_ref[:2], cot_ref[TR - 2 :]
    v1 = jnp.where(low, bottom, top)
    v2 = jnp.where(low, top, bottom)
    v1_ref[...] = v1
    v2_ref[...] = v2
    c1l_ref[...] = v1[:, TC - 16 :]
    c1r_ref[...] = v1[:, :16]
    c2l_ref[...] = v2[:, TC - 16 :]
    c2r_ref[...] = v2[:, :16]


def edges(where, cot):
    shapes = [(TR, 16, C), (TR, 16, C), (2, TC, C), (2, TC, C)] + [(2, 16, C)] * 4
    return pl.pallas_call(
        edges_kernel,
        in_specs=[pl.BlockSpec(memory_space=pltpu.SMEM), pl.BlockSpec(memory_space=pltpu.VMEM)],
        out_specs=[pl.BlockSpec(memory_space=pltpu.VMEM)] * len(shapes),
        out_shape=[jax.ShapeDtypeStruct(s, BF16) for s in shapes],
        cost_estimate=pl.CostEstimate(flops=0, bytes_accessed=1 << 20, transcendentals=0),
        name="edges",
    )(where, cot)


def cot_kernel(where_ref, cot_ref, left_ref, right_ref, v1_ref, v2_ref, c1l_ref, c1r_ref, c2l_ref, c2r_ref,
               w_ref, hg_ref, cot_t_ref, flat_ref, copies_ref, back_ref, own_ref):
    low, low_left, low_right = sides(where_ref)
    north = where_ref[0] == 0
    south = where_ref[0] == where_ref[2] - 1
    up = jnp.where(low, v1_ref[...], v2_ref[...]).astype(F32)
    down = jnp.where(low, v2_ref[...], v1_ref[...]).astype(F32)
    up_l = jnp.where(low_left, c1l_ref[...], c2l_ref[...]).astype(F32)
    down_l = jnp.where(low_left, c2l_ref[...], c1l_ref[...]).astype(F32)
    up_r = jnp.where(low_right, c1r_ref[...], c2r_ref[...]).astype(F32)
    down_r = jnp.where(low_right, c2r_ref[...], c1r_ref[...]).astype(F32)

    def pick(inner, up, down):
        def get(i):
            if i < 0:
                near, far = jnp.where(north, up[0], up[1]), jnp.where(north, up[1], up[0])
                return near if i == -1 else far
            if i >= TR:
                near, far = jnp.where(south, down[1], down[0]), jnp.where(south, down[0], down[1])
                return near if i == TR else far
            return inner[i].astype(F32)

        return get

    fill_flat(flat_ref, pick(cot_ref, up, down), pick(left_ref, up_l, down_l), pick(right_ref, up_r, down_r))
    shifted_copies(flat_ref, copies_ref, 0, LEN // PART)
    arrange_back(w_ref, back_ref)

    def body(k, carry):
        at = pl.multiple_of(FIRST + k * PART, 16)
        hg_ref[pl.ds(at, PART), :] = back_rows(copies_ref, at, PART, [back_ref[0], back_ref[1], back_ref[2]])
        return carry

    lax.fori_loop(0, 9, body, 0)

    @pl.when(north)
    def _():
        at = place(-1) - 16
        got = back_rows(copies_ref, at, PART, [back_ref[2], back_ref[1], back_ref[2]])
        hg_ref[at + 8 : at + PART - 8] = got[8:-8]

    @pl.when(south)
    def _():
        at = place(TR - 1) - 16
        got = back_rows(copies_ref, at, PART, [back_ref[0], back_ref[1], back_ref[0]])
        hg_ref[at + 8 : at + PART - 8] = got[8:-8]

    for i in range(TR):
        own_ref[i * PITCH : i * PITCH + TC] = cot_ref[i]
        own_ref[i * PITCH + TC : (i + 1) * PITCH] = jnp.zeros((PITCH - TC, C), BF16)
    transpose_flat(own_ref, cot_t_ref)


def transpose_flat(own_ref, out_ref):
    def body(m, carry):
        at = pl.multiple_of(m * 128, 128)
        out_ref[:, pl.ds(at, 128)] = own_ref[pl.ds(at, 128), :].T
        return carry

    lax.fori_loop(0, own_ref.shape[0] // 128, body, 0)


def cot_back(where, cot, halo, w_second):
    vmem = pl.BlockSpec(memory_space=pltpu.VMEM)
    return pl.pallas_call(
        cot_kernel,
        in_specs=[pl.BlockSpec(memory_space=pltpu.SMEM)] + [vmem] * 10,
        out_specs=[vmem] * 2,
        out_shape=[
            jax.ShapeDtypeStruct((LEN, C), F32),
            jax.ShapeDtypeStruct((C, TR * PITCH), BF16),
        ],
        scratch_shapes=[
            pltpu.VMEM((LEN + 16, C), F32),
            pltpu.VMEM((LEN, 3 * C), BF16),
            pltpu.VMEM((3, C, 3 * C), BF16),
            pltpu.VMEM((TR * PITCH, C), BF16),
        ],
        compiler_params=pltpu.CompilerParams(vmem_limit_bytes=32 << 20),
        cost_estimate=pl.CostEstimate(flops=2 * 2736 * 1152 * 256, bytes_accessed=4 << 20, transcendentals=0),
        name="cot_back",
    )(where, cot, *halo, w_second)


def main_kernel(where_ref, s_ref, left_ref, right_ref, v1_ref, v2_ref, c1l_ref, c1r_ref, c2l_ref, c2r_ref,
                wide_ref, w1_ref, w2_ref, hg_ref, cot_t_ref,
                field_ref, red_ref,
                flat_ref, x_ref, pre_ref, h_ref, back_ref, own_ref, own_t_ref, eg_ref):
    low, low_left, low_right = sides(where_ref)
    north = where_ref[0] == 0
    south = where_ref[0] == where_ref[2] - 1
    wide = wide_ref[...]

    def embed(s):
        return [dot(s[:, g * 128 : (g + 1) * 128], wide) for g in range(s.shape[1] // 128)]

    def rows_of(inner, up, down):
        inner, up, down = embed(inner), embed(up)[0], embed(down)[0]

        def get(i):
            block = lambda a, k: a[:, k * C : (k + 1) * C]
            if i == -1:
                return jnp.where(north, block(up, 0), block(up, 3))
            if i == -2:
                return jnp.where(north, block(up, 1), block(up, 2))
            if i == TR:
                return jnp.where(south, block(down, 3), block(down, 0))
            if i == TR + 1:
                return jnp.where(south, block(down, 2), block(down, 1))
            return block(inner[i // 4], i % 4)

        return get

    centre = rows_of(
        s_ref[...],
        jnp.where(low, v1_ref[...], v2_ref[...]),
        jnp.where(low, v2_ref[...], v1_ref[...]),
    )
    left = rows_of(
        left_ref[...],
        jnp.where(low_left, c1l_ref[...], c2l_ref[...]),
        jnp.where(low_left, c2l_ref[...], c1l_ref[...]),
    )
    right = rows_of(
        right_ref[...],
        jnp.where(low_right, c1r_ref[...], c2r_ref[...]),
        jnp.where(low_right, c2r_ref[...], c1r_ref[...]),
    )
    fill_flat(flat_ref, centre, left, right)
    shifted_copies(flat_ref, x_ref, 0, LEN // PART)

    def weights(w_ref, order):
        return [w_ref[r].reshape(3 * C, C) for r in order]

    def pre_body(k, carry):
        at = pl.multiple_of(FIRST + k * PART, 16)
        pre_ref[pl.ds(at, PART), :] = conv_rows(x_ref, at, PART, weights(w1_ref, (0, 1, 2)))
        return carry

    lax.fori_loop(0, 9, pre_body, 0)

    def pole_pre(at):
        got = conv_rows(x_ref, at, PITCH + 16, weights(w1_ref, (2, 1, 0)))
        pre_ref[at + 8 : at + PITCH + 8] = got[8:-8]

    @pl.when(north)
    def _():
        pole_pre(place(-1) - 16)

    @pl.when(south)
    def _():
        pole_pre(place(TR) - 16)

    flat_ref[8 + FIRST - 16 : 8 + FIRST] = jnp.zeros((16, C), F32)
    flat_ref[8 + FIRST + 9 * PART : 24 + FIRST + 9 * PART] = jnp.zeros((16, C), F32)

    def hidden_body(k, carry):
        at = pl.multiple_of(FIRST + k * PART, 16)
        pre = pre_ref[pl.ds(at, PART), :]
        flat_ref[pl.ds(at + 8, PART), :] = pre / (1.0 + jnp.exp(-pre))
        return carry

    lax.fori_loop(0, 9, hidden_body, 0)
    shifted_copies(flat_ref, h_ref, FIRST, 9)

    def field_body(k, carry):
        at = pl.multiple_of(OWN + k * 2 * PITCH, 16)
        got = conv_rows(h_ref, at, 2 * PITCH, weights(w2_ref, (0, 1, 2))).astype(BF16)
        field_ref[2 * k] = got[:TC]
        field_ref[2 * k + 1] = got[PITCH : PITCH + TC]
        return carry

    lax.fori_loop(0, TR // 2, field_body, 0)

    def weight_grad(src_ref, grad_t_ref, begin):
        for r in range(3):
            at = OWN + (r - 1) * PITCH
            got = dot(grad_t_ref[...], src_ref[at : at + TR * PITCH]).astype(BF16)
            for s in range(3):
                to = begin + (3 * r + s) * C
                red_ref[to : to + C] = got[:, s * C : (s + 1) * C]

    weight_grad(h_ref, cot_t_ref, 9 * C)

    def grad_body(k, carry):
        at = pl.multiple_of(FIRST + k * PART, 16)
        pre = pre_ref[pl.ds(at, PART), :]
        sig = 1.0 / (1.0 + jnp.exp(-pre))
        flat_ref[pl.ds(at + 8, PART), :] = hg_ref[pl.ds(at, PART), :] * (sig * (1.0 + pre * (1.0 - sig)))
        return carry

    lax.fori_loop(0, 9, grad_body, 0)
    shifted_copies(flat_ref, h_ref, FIRST, 9)
    for i in range(TR):
        at = 8 + place(i)
        own_ref[i * PITCH : i * PITCH + TC] = flat_ref[at : at + TC].astype(BF16)
        own_ref[i * PITCH + TC : (i + 1) * PITCH] = jnp.zeros((PITCH - TC, C), BF16)
    transpose_flat(own_ref, own_t_ref)
    weight_grad(x_ref, own_t_ref, 0)

    arrange_back(w1_ref, back_ref)

    def eg_body(k, carry):
        at = pl.multiple_of(OWN + k * 2 * PITCH, 16)
        got = back_rows(h_ref, at, 2 * PITCH, [back_ref[0], back_ref[1], back_ref[2]])
        eg_ref[pl.ds(pl.multiple_of(k * 2 * PITCH, 16), 2 * PITCH), :] = got.astype(BF16)
        return carry

    lax.fori_loop(0, TR // 2, eg_body, 0)

    @pl.when(north)
    def _():
        got = back_rows(h_ref, OWN, PITCH, [back_ref[2], back_ref[1], back_ref[2]])
        eg_ref[:PITCH] = got.astype(BF16)

    @pl.when(south)
    def _():
        got = back_rows(h_ref, place(TR - 1), PITCH, [back_ref[0], back_ref[1], back_ref[0]])
        eg_ref[(TR - 1) * PITCH :] = got.astype(BF16)

    total = jnp.zeros((FEAT, C), F32)
    for g in range(TR // 4):
        s_t = s_ref[:, g * 128 : (g + 1) * 128].T
        for k in range(4):
            i = 4 * g + k
            total += dot(s_t[k * FEAT : (k + 1) * FEAT], eg_ref[i * PITCH : i * PITCH + TC])
    red_ref[18 * C : 18 * C + FEAT] = total.astype(BF16)
    red_ref[18 * C + FEAT :] = jnp.zeros((red_ref.shape[0] - 18 * C - FEAT, C), BF16)


def main(where, s, halo, wide, w_first, w_second, hg, cot_t, owners):
    vmem = pl.BlockSpec(memory_space=pltpu.VMEM)
    return pl.pallas_call(
        main_kernel,
        in_specs=[pl.BlockSpec(memory_space=pltpu.SMEM)] + [vmem] * 14,
        out_specs=[vmem] * 2,
        out_shape=[
            jax.ShapeDtypeStruct((TR, TC, C), BF16),
            jax.ShapeDtypeStruct((owners * RED, C), BF16),
        ],
        scratch_shapes=[
            pltpu.VMEM((LEN + 16, C), F32),
            pltpu.VMEM((LEN, 3 * C), BF16),
            pltpu.VMEM((LEN, C), F32),
            pltpu.VMEM((LEN, 3 * C), BF16),
            pltpu.VMEM((3, C, 3 * C), BF16),
            pltpu.VMEM((TR * PITCH, C), BF16),
            pltpu.VMEM((C, TR * PITCH), BF16),
            pltpu.VMEM((TR * PITCH, C), BF16),
        ],
        compiler_params=pltpu.CompilerParams(vmem_limit_bytes=48 << 20),
        cost_estimate=pl.CostEstimate(flops=8 << 30, bytes_accessed=6 << 20, transcendentals=1 << 20),
        name="main",
    )(where, s, *halo, wide, w_first, w_second, hg, cot_t)


def sum_kernel(got_ref, out_ref):
    step = pl.program_id(0)

    @pl.when(step == 0)
    def _():
        out_ref[...] = jnp.sum(got_ref[...].astype(F32), axis=0)

    @pl.when(step > 0)
    def _():
        out_ref[...] += jnp.sum(got_ref[...].astype(F32), axis=0)


def unpack_kernel(got_ref, embed_ref, first_ref, second_ref):
    for r in range(3):
        for s in range(3):
            at = (3 * r + s) * C
            first_ref[r, s] = got_ref[at : at + C].astype(F32).T
            second_ref[r, s] = got_ref[at + 9 * C : at + 10 * C].astype(F32).T
    embed_ref[...] = got_ref[18 * C : 18 * C + 24].astype(F32)


def unpack(got, values):
    vmem = pl.BlockSpec(memory_space=pltpu.VMEM)
    return pl.pallas_call(
        unpack_kernel,
        in_specs=[vmem],
        out_specs=[vmem] * 3,
        out_shape=[
            jax.ShapeDtypeStruct((values, C), F32),
            jax.ShapeDtypeStruct((3, 3, C, C), F32),
            jax.ShapeDtypeStruct((3, 3, C, C), F32),
        ],
        name="unpack",
    )(got)


def exchange(bands, sectors, left, right, v1, v2, c1l, c1r, c2l, c2r):
    half = sectors // 2
    number = lambda a, b: a * sectors + b % sectors

    def above(a, b):
        return number(a - 1, b) if a > 0 else number(0, b + half)

    def below(a, b):
        return number(a + 1, b) if a < bands - 1 else number(a, b + half)

    def source(kind, a, b):
        b = b % sectors
        return above(a, b) if (b < half) == (kind == 1) else below(a, b)

    def perm(of):
        return [(of(a, b), number(a, b)) for a in range(bands) for b in range(sectors)]

    move = lambda x, of: lax.ppermute(x, ALL, perm(of))
    return (
        move(right, lambda a, b: number(a, b - 1)),
        move(left, lambda a, b: number(a, b + 1)),
        move(v1, lambda a, b: source(1, a, b)),
        move(v2, lambda a, b: source(2, a, b)),
        move(c1l, lambda a, b: source(1, a, b - 1)),
        move(c1r, lambda a, b: source(1, a, b + 1)),
        move(c2l, lambda a, b: source(2, a, b - 1)),
        move(c2r, lambda a, b: source(2, a, b + 1)),
    )


def per_device(obs_values, tile_ids, obs_rows, obs_cols, w_embed, w_first, w_second, cotangent):
    bands, sectors = lax.axis_size("lat"), lax.axis_size("lon")
    owners = bands * sectors
    count, values = obs_values.shape
    where = jnp.stack(
        [lax.axis_index("lat"), lax.axis_index("lon"), jnp.int32(bands), jnp.int32(sectors)]
    ).astype(jnp.int32)
    cot_edges = edges(where, cotangent)
    cot_halo = exchange(bands, sectors, *cot_edges)

    packed = pack(tile_ids.T, obs_rows.reshape(1, count), obs_cols.reshape(1, count), obs_values.T)
    got = lax.all_to_all(packed, ALL, 0, 0, tiled=True)
    hg, cot_t = cot_back(where, cotangent, cot_halo, w_second)

    s, *s_edges = setconv(where, got)
    s_halo = exchange(bands, sectors, *s_edges)
    padded = jnp.concatenate([w_embed, jnp.zeros((FEAT - values, C), BF16)], axis=0)
    wide = jnp.kron(jnp.eye(4, dtype=BF16), padded)
    field, red = main(where, s, s_halo, wide, w_first, w_second, hg, cot_t, owners)

    parts = lax.all_to_all(red.reshape(owners, RED, C), ALL, 0, 0, tiled=True)
    summed = jnp.sum(parts.astype(F32), axis=0).astype(BF16)
    spread = jnp.broadcast_to(summed[None], (owners, RED, C))
    whole = lax.all_to_all(spread, ALL, 0, 0, tiled=True)
    grad_embed, grad_first, grad_second = unpack(whole.reshape(owners * RED, C), values)
    return (field, grad_embed, grad_first, grad_second)


def solution(mesh):
    in_specs = (
        P(ALL, None),
        P(ALL, None),
        P(ALL),
        P(ALL),
        P(),
        P(),
        P(),
        P("lat", "lon", None),
    )
    out_specs = (P("lat", "lon", None), P(), P(), P())
    return jax.shard_map(
        per_device, mesh=mesh, in_specs=in_specs, out_specs=out_specs, check_vma=False
    )
```

```python
import functools
import math
import jax
import jax.numpy as jnp
from jax import lax
from jax.experimental import pallas as pl
from jax.experimental.pallas import tpu as pltpu
from jax.sharding import PartitionSpec as P

F32 = jnp.float32
BF16 = jnp.bfloat16
spread_cells = 1.0
ALL = ("lat", "lon")

TR, TC, C = 16, 128, 128
PITCH = TC + 16
LEN = 3040
PART = 304
FIRST = PITCH
OWN = 16 + 2 * PITCH
FEAT = 32
RED = 24


def dot(a, b):
    return jnp.dot(a, b, preferred_element_type=F32)


def dot_nt(a, b):
    return lax.dot_general(a, b, (((1,), (1,)), ((), ())), preferred_element_type=F32)


def place(i):
    return 16 + (i + 2) * PITCH


def pack_kernel(ids_hbm, rows_hbm, cols_hbm, vals_hbm, out_ref,
                ids_ref, rows_ref, cols_ref, vals_ref, q_ref, v_ref, pair_ref, acc_ref, sems):
    step = pl.program_id(0)
    count = ids_ref.shape[1]
    owners = out_ref.shape[0] * pl.num_programs(0)
    sub = 256
    part = 2048
    pairs = out_ref.shape[0] // 2

    @pl.when(step == 0)
    def _():
        moves = [
            pltpu.make_async_copy(a, b, sems.at[k])
            for k, (a, b) in enumerate(
                [(ids_hbm, ids_ref), (rows_hbm, rows_ref), (cols_hbm, cols_ref), (vals_hbm, vals_ref)]
            )
        ]
        for move in moves:
            move.start()
        owner = lax.broadcasted_iota(jnp.int32, (owners, sub), 0)
        slot = lax.broadcasted_iota(jnp.int32, (sub, sub), 0)
        upto = slot <= lax.broadcasted_iota(jnp.int32, (sub, sub), 1)
        upto = jnp.concatenate(
            [jnp.where(upto, 1.0, 0.0).astype(BF16), jnp.ones((sub, 128), BF16)], axis=1
        )
        for move in moves:
            move.wait()

        def body(k, carry):
            for u in range(4):
                at = pl.ds(pl.multiple_of(k * 4 * sub + u * sub, sub), sub)
                ids = ids_ref[:, at]
                hot = owner == ids
                counted = dot(jnp.where(hot, 1.0, 0.0).astype(BF16), upto)
                before = counted[:, :sub] + jnp.concatenate([carry, carry], axis=1)
                rank = jnp.sum(jnp.where(hot, before, 0.0), axis=0, keepdims=True) - 1.0
                key = rank.astype(jnp.int32) + (ids & 1) * 128
                q_ref[:, at] = jnp.where(slot == key, 1.0, 0.0).astype(BF16)
                pair_ref[:, at] = jnp.broadcast_to((ids >> 1).astype(F32), (FEAT, sub)).astype(BF16)
                rows, cols = rows_ref[:, at], cols_ref[:, at]
                rows_hi, cols_hi = rows.astype(BF16).astype(F32), cols.astype(BF16).astype(F32)
                tail = jnp.concatenate(
                    [rows_hi, rows - rows_hi, cols_hi, cols - cols_hi, jnp.zeros((4, sub), F32)], axis=0
                )
                v_ref[:, at] = jnp.concatenate([vals_ref[:, at].astype(F32), tail], axis=0).astype(BF16)
                carry = carry + counted[:, sub:]
            return carry

        lax.fori_loop(0, count // sub // 4, body, jnp.zeros((owners, 128), F32))

    base = jnp.full((FEAT, part), (step * pairs).astype(F32), F32).astype(BF16)
    for k in range(count // part):
        at = pl.ds(k * part, part)
        pair = pair_ref[:, at] - base
        values = v_ref[:, at]
        none = jnp.zeros_like(values)
        left = jnp.concatenate([jnp.where(pair == p, values, none) for p in range(pairs)], axis=0)
        term = dot_nt(left, q_ref[:, at])
        if k == 0:
            acc_ref[...] = term
        else:
            acc_ref[...] += term
    for p in range(pairs):
        out_ref[2 * p] = acc_ref[p * FEAT : (p + 1) * FEAT, :128].astype(BF16)
        out_ref[2 * p + 1] = acc_ref[p * FEAT : (p + 1) * FEAT, 128:].astype(BF16)


def pack(ids, rows, cols, values):
    count = ids.shape[1]
    owners = 128
    steps = 4
    return pl.pallas_call(
        pack_kernel,
        grid=(steps,),
        in_specs=[pl.BlockSpec(memory_space=pl.ANY)] * 4,
        out_specs=pl.BlockSpec((owners // steps, FEAT, 128), lambda i: (i, 0, 0)),
        out_shape=jax.ShapeDtypeStruct((owners, FEAT, 128), BF16),
        scratch_shapes=[
            pltpu.VMEM(ids.shape, ids.dtype),
            pltpu.VMEM(rows.shape, rows.dtype),
            pltpu.VMEM(cols.shape, cols.dtype),
            pltpu.VMEM(values.shape, values.dtype),
            pltpu.VMEM((256, count), BF16),
            pltpu.VMEM((FEAT, count), BF16),
            pltpu.VMEM((FEAT, count), BF16),
            pltpu.VMEM((owners // steps // 2 * FEAT, 256), F32),
            pltpu.SemaphoreType.DMA((4,)),
        ],
        compiler_params=pltpu.CompilerParams(vmem_limit_bytes=56 << 20),
        cost_estimate=pl.CostEstimate(flops=2 * 2048 * 256 * 8192, bytes_accessed=3 << 20, transcendentals=0),
        name="pack",
    )(ids, rows, cols, values)


def setconv_kernel(where_ref, got_ref, s_ref, a_ref, b_ref, c_ref, d_ref, acc_ref):
    step = pl.program_id(0)
    x = jnp.concatenate([got_ref[k] for k in range(got_ref.shape[0])], axis=1).astype(F32)
    n = x.shape[1]
    alpha = math.sqrt(0.5 / math.log(2.0)) / spread_cells
    row = (x[24:25] + x[25:26]) * alpha
    col = (x[26:27] + x[27:28]) * alpha
    row_mid = (lax.broadcasted_iota(jnp.int32, (TR, n), 0).astype(F32) + 0.5) * alpha
    col_mid = (lax.broadcasted_iota(jnp.int32, (TC, n), 0).astype(F32) + 0.5) * alpha
    row_weight = jnp.exp2(-jnp.square(row - row_mid))
    col_weight = jnp.exp2(-jnp.square(col - col_mid)).astype(BF16)
    values = x[:24]
    weighted = jnp.concatenate([values * row_weight[i : i + 1] for i in range(TR)], axis=0).astype(BF16)
    term = dot_nt(weighted, col_weight)

    @pl.when(step == 0)
    def _():
        acc_ref[...] = term

    @pl.when(step > 0)
    def _():
        acc_ref[...] += term

    @pl.when(step == pl.num_programs(0) - 1)
    def _():
        none = jnp.zeros((FEAT - 24, TC), F32)
        for g in range(TR // 4):
            rows = []
            for i in range(4 * g, 4 * g + 4):
                rows += [acc_ref[24 * i : 24 * i + 24], none]
            s_ref[:, g * 128 : (g + 1) * 128] = jnp.concatenate(rows, axis=0).T.astype(BF16)
        left, right = s_ref[:16], s_ref[TC - 16 :]
        top, bottom = s_ref[:, :128], s_ref[:, -128:]
        even_lon, even_lat = evens(where_ref)
        a_ref[...] = jnp.where(even_lon, right, left)
        b_ref[...] = jnp.where(even_lon, left, right)
        c_ref[...] = jnp.where(even_lat, bottom, top)
        d_ref[...] = jnp.where(even_lat, top, bottom)


def setconv(where, got):
    steps = 8
    fixed = lambda *shape: pl.BlockSpec(shape, lambda i: (0,) * len(shape))
    lanes = TR * FEAT
    shapes = [(TC, lanes), (16, lanes), (16, lanes), (TC, 128), (TC, 128)]
    return pl.pallas_call(
        setconv_kernel,
        grid=(steps,),
        in_specs=[
            pl.BlockSpec(memory_space=pltpu.SMEM),
            pl.BlockSpec((got.shape[0] // steps, FEAT, 128), lambda i: (i, 0, 0)),
        ],
        out_specs=[fixed(*s) for s in shapes],
        out_shape=[jax.ShapeDtypeStruct(s, BF16) for s in shapes],
        scratch_shapes=[pltpu.VMEM((TR * 24, TC), F32)],
        compiler_params=pltpu.CompilerParams(vmem_limit_bytes=32 << 20),
        cost_estimate=pl.CostEstimate(
            flops=2 * 384 * 256 * 16384, bytes_accessed=2 << 20, transcendentals=144 * 16384
        ),
        name="setconv",
    )(where, got)


def join_kernel(where_ref, a_ref, b_ref, c_ref, d_ref, c_out, d_out):
    even_lon, even_lat = evens(where_ref)
    right = jnp.where(even_lon, a_ref[...], b_ref[...])
    left = jnp.where(even_lon, b_ref[...], a_ref[...])
    left_c = jnp.where(even_lat, left[:, -128:], left[:, :128])
    left_d = jnp.where(even_lat, left[:, :128], left[:, -128:])
    right_c = jnp.where(even_lat, right[:, -128:], right[:, :128])
    right_d = jnp.where(even_lat, right[:, :128], right[:, -128:])
    c_out[:16], c_out[16 : 16 + TC], c_out[16 + TC :] = left_c, c_ref[...], right_c
    d_out[:16], d_out[16 : 16 + TC], d_out[16 + TC :] = left_d, d_ref[...], right_d


def join_cot_kernel(where_ref, a_ref, b_ref, c_ref, d_ref, c_out, d_out):
    even_lon, even_lat = evens(where_ref)
    right = jnp.where(even_lon, a_ref[...], b_ref[...])
    left = jnp.where(even_lon, b_ref[...], a_ref[...])
    left_c = jnp.where(even_lat, left[-2:], left[:2])
    left_d = jnp.where(even_lat, left[:2], left[-2:])
    right_c = jnp.where(even_lat, right[-2:], right[:2])
    right_d = jnp.where(even_lat, right[:2], right[-2:])
    c_out[:, :16], c_out[:, 16 : 16 + TC], c_out[:, 16 + TC :] = left_c, c_ref[...], right_c
    d_out[:, :16], d_out[:, 16 : 16 + TC], d_out[:, 16 + TC :] = left_d, d_ref[...], right_d


def join(kernel, where, a, b, c, d, shape, name):
    vmem = pl.BlockSpec(memory_space=pltpu.VMEM)
    return pl.pallas_call(
        kernel,
        in_specs=[pl.BlockSpec(memory_space=pltpu.SMEM)] + [vmem] * 4,
        out_specs=[vmem] * 2,
        out_shape=[jax.ShapeDtypeStruct(shape, BF16)] * 2,
        cost_estimate=pl.CostEstimate(flops=0, bytes_accessed=1 << 18, transcendentals=0),
        name=name,
    )(where, a, b, c, d)


def shifted_copies(flat_ref, out_ref, begin, parts):
    def body(k, carry):
        at = pl.multiple_of(begin + k * PART, 16)
        for s in range(3):
            out_ref[pl.ds(at, PART), s * C : (s + 1) * C] = flat_ref[pl.ds(at + 7 + s, PART), :].astype(BF16)
        return carry

    lax.fori_loop(0, parts, body, 0)


def three_rows(src_ref, at, rows):
    return jnp.concatenate(
        [src_ref[pl.ds(at + (r - 1) * PITCH, rows), :] for r in range(3)], axis=1
    )


def conv_rows(src_ref, at, rows, weights):
    return dot(three_rows(src_ref, at, rows), jnp.concatenate(weights, axis=0))


def back_rows(src_ref, at, rows, weights):
    return dot_nt(three_rows(src_ref, at, rows), jnp.concatenate(weights, axis=1))


def fill_flat(flat_ref, centre, left, right):
    first = lax.broadcasted_iota(jnp.int32, (16, C), 0) < 8
    flat_ref[:8] = jnp.zeros((8, C), F32)
    flat_ref[8:24] = left(-2)
    for i in range(-2, TR + 2):
        at = 8 + place(i)
        flat_ref[at : at + TC] = centre(i)
        after = jnp.where(first, right(i), left(i + 1)) if i < TR + 1 else right(i)
        flat_ref[at + TC : at + PITCH] = after
    end = 8 + place(TR + 2)
    flat_ref[end:] = jnp.zeros((flat_ref.shape[0] - end, C), F32)


def evens(where_ref):
    return where_ref[1] % 2 == 0, where_ref[0] % 2 == 0


def arrange_back(w_ref, out_ref):
    for r in range(3):
        for s in range(3):
            out_ref[r, :, s * C : (s + 1) * C] = w_ref[2 - r, 2 - s]


def edges_kernel(where_ref, cot_ref, a_ref, b_ref, c_ref, d_ref):
    even_lon, even_lat = evens(where_ref)
    left, right = cot_ref[:, :16, :], cot_ref[:, TC - 16 :, :]
    top, bottom = cot_ref[:2], cot_ref[TR - 2 :]
    a_ref[...] = jnp.where(even_lon, right, left)
    b_ref[...] = jnp.where(even_lon, left, right)
    c_ref[...] = jnp.where(even_lat, bottom, top)
    d_ref[...] = jnp.where(even_lat, top, bottom)


def edges(where, cot):
    shapes = [(TR, 16, C), (TR, 16, C), (2, TC, C), (2, TC, C)]
    return pl.pallas_call(
        edges_kernel,
        in_specs=[pl.BlockSpec(memory_space=pltpu.SMEM), pl.BlockSpec(memory_space=pltpu.VMEM)],
        out_specs=[pl.BlockSpec(memory_space=pltpu.VMEM)] * len(shapes),
        out_shape=[jax.ShapeDtypeStruct(s, BF16) for s in shapes],
        cost_estimate=pl.CostEstimate(flops=0, bytes_accessed=1 << 20, transcendentals=0),
        name="edges",
    )(where, cot)


def cot_kernel(where_ref, cot_ref, a_ref, b_ref, c_ref, d_ref,
               w_ref, hg_ref, cot_t_ref, flat_ref, copies_ref, back_ref, own_ref):
    even_lon, even_lat = evens(where_ref)
    north = where_ref[0] == 0
    south = where_ref[0] == where_ref[2] - 1
    left = jnp.where(even_lon, b_ref[...], a_ref[...])
    right = jnp.where(even_lon, a_ref[...], b_ref[...])
    up = jnp.where(even_lat, d_ref[...], c_ref[...]).astype(F32)
    down = jnp.where(even_lat, c_ref[...], d_ref[...]).astype(F32)
    up_l, up_r = up[:, :16], up[:, 16 + TC :]
    down_l, down_r = down[:, :16], down[:, 16 + TC :]
    up, down = up[:, 16 : 16 + TC], down[:, 16 : 16 + TC]

    def pick(inner, up, down):
        def get(i):
            if i < 0:
                near, far = jnp.where(north, up[0], up[1]), jnp.where(north, up[1], up[0])
                return near if i == -1 else far
            if i >= TR:
                near, far = jnp.where(south, down[1], down[0]), jnp.where(south, down[0], down[1])
                return near if i == TR else far
            return inner[i].astype(F32)

        return get

    fill_flat(flat_ref, pick(cot_ref, up, down), pick(left, up_l, down_l), pick(right, up_r, down_r))
    shifted_copies(flat_ref, copies_ref, 0, LEN // PART)
    arrange_back(w_ref, back_ref)

    def body(k, carry):
        at = pl.multiple_of(FIRST + k * PART, 16)
        hg_ref[pl.ds(at, PART), :] = back_rows(copies_ref, at, PART, [back_ref[0], back_ref[1], back_ref[2]])
        return carry

    lax.fori_loop(0, 9, body, 0)

    @pl.when(north)
    def _():
        at = place(-1) - 16
        got = back_rows(copies_ref, at, PART, [back_ref[2], back_ref[1], back_ref[2]])
        hg_ref[at + 8 : at + PART - 8] = got[8:-8]

    @pl.when(south)
    def _():
        at = place(TR - 1) - 16
        got = back_rows(copies_ref, at, PART, [back_ref[0], back_ref[1], back_ref[0]])
        hg_ref[at + 8 : at + PART - 8] = got[8:-8]

    for i in range(TR):
        own_ref[i * PITCH : i * PITCH + TC] = cot_ref[i]
        own_ref[i * PITCH + TC : (i + 1) * PITCH] = jnp.zeros((PITCH - TC, C), BF16)
    transpose_flat(own_ref, cot_t_ref)


def transpose_flat(own_ref, out_ref):
    def body(m, carry):
        at = pl.multiple_of(m * 128, 128)
        out_ref[:, pl.ds(at, 128)] = own_ref[pl.ds(at, 128), :].T
        return carry

    lax.fori_loop(0, own_ref.shape[0] // 128, body, 0)


def cot_back(where, cot, halo, w_second):
    vmem = pl.BlockSpec(memory_space=pltpu.VMEM)
    return pl.pallas_call(
        cot_kernel,
        in_specs=[pl.BlockSpec(memory_space=pltpu.SMEM)] + [vmem] * 6,
        out_specs=[vmem] * 2,
        out_shape=[
            jax.ShapeDtypeStruct((LEN, C), F32),
            jax.ShapeDtypeStruct((C, TR * PITCH), BF16),
        ],
        scratch_shapes=[
            pltpu.VMEM((LEN + 16, C), F32),
            pltpu.VMEM((LEN, 3 * C), BF16),
            pltpu.VMEM((3, C, 3 * C), BF16),
            pltpu.VMEM((TR * PITCH, C), BF16),
        ],
        compiler_params=pltpu.CompilerParams(vmem_limit_bytes=32 << 20),
        cost_estimate=pl.CostEstimate(flops=2 * 2736 * 1152 * 256, bytes_accessed=4 << 20, transcendentals=0),
        name="cot_back",
    )(where, cot, *halo, w_second)


def main_kernel(where_ref, s_ref, a_ref, b_ref, c_ref, d_ref,
                wide_ref, w1_ref, w2_ref, hg_ref, cot_t_ref,
                field_ref, red_ref,
                flat_ref, x_ref, pre_ref, h_ref, back_ref, own_ref, own_t_ref, eg_ref):
    even_lon, even_lat = evens(where_ref)
    north = where_ref[0] == 0
    south = where_ref[0] == where_ref[2] - 1
    wide = wide_ref[...]

    def embed(s):
        return [dot(s[:, g * 128 : (g + 1) * 128], wide) for g in range(s.shape[1] // 128)]

    def rows_of(inner, up, down):
        inner, up, down = embed(inner), embed(up)[0], embed(down)[0]

        def get(i):
            block = lambda a, k: a[:, k * C : (k + 1) * C]
            if i == -1:
                return jnp.where(north, block(up, 0), block(up, 3))
            if i == -2:
                return jnp.where(north, block(up, 1), block(up, 2))
            if i == TR:
                return jnp.where(south, block(down, 3), block(down, 0))
            if i == TR + 1:
                return jnp.where(south, block(down, 2), block(down, 1))
            return block(inner[i // 4], i % 4)

        return get

    up = jnp.where(even_lat, d_ref[...], c_ref[...])
    down = jnp.where(even_lat, c_ref[...], d_ref[...])
    centre = rows_of(s_ref[...], up[16 : 16 + TC], down[16 : 16 + TC])
    left = rows_of(jnp.where(even_lon, b_ref[...], a_ref[...]), up[:16], down[:16])
    right = rows_of(jnp.where(even_lon, a_ref[...], b_ref[...]), up[16 + TC :], down[16 + TC :])
    fill_flat(flat_ref, centre, left, right)
    shifted_copies(flat_ref, x_ref, 0, LEN // PART)

    def weights(w_ref, order):
        return [w_ref[r].reshape(3 * C, C) for r in order]

    def pre_body(k, carry):
        at = pl.multiple_of(FIRST + k * PART, 16)
        pre_ref[pl.ds(at, PART), :] = conv_rows(x_ref, at, PART, weights(w1_ref, (0, 1, 2)))
        return carry

    lax.fori_loop(0, 9, pre_body, 0)

    def pole_pre(at):
        got = conv_rows(x_ref, at, PITCH + 16, weights(w1_ref, (2, 1, 0)))
        pre_ref[at + 8 : at + PITCH + 8] = got[8:-8]

    @pl.when(north)
    def _():
        pole_pre(place(-1) - 16)

    @pl.when(south)
    def _():
        pole_pre(place(TR) - 16)

    flat_ref[8 + FIRST - 16 : 8 + FIRST] = jnp.zeros((16, C), F32)
    flat_ref[8 + FIRST + 9 * PART : 24 + FIRST + 9 * PART] = jnp.zeros((16, C), F32)

    def hidden_body(k, carry):
        at = pl.multiple_of(FIRST + k * PART, 16)
        pre = pre_ref[pl.ds(at, PART), :]
        flat_ref[pl.ds(at + 8, PART), :] = pre / (1.0 + jnp.exp(-pre))
        return carry

    lax.fori_loop(0, 9, hidden_body, 0)
    shifted_copies(flat_ref, h_ref, FIRST, 9)

    def field_body(k, carry):
        at = pl.multiple_of(OWN + k * 2 * PITCH, 16)
        got = conv_rows(h_ref, at, 2 * PITCH, weights(w2_ref, (0, 1, 2))).astype(BF16)
        field_ref[2 * k] = got[:TC]
        field_ref[2 * k + 1] = got[PITCH : PITCH + TC]
        return carry

    lax.fori_loop(0, TR // 2, field_body, 0)

    def weight_grad(src_ref, grad_t_ref, begin):
        for r in range(3):
            at = OWN + (r - 1) * PITCH
            got = dot(grad_t_ref[...], src_ref[at : at + TR * PITCH]).astype(BF16)
            for s in range(3):
                to = begin + (3 * r + s) * C
                red_ref[to : to + C] = got[:, s * C : (s + 1) * C]

    weight_grad(h_ref, cot_t_ref, 9 * C)

    def grad_body(k, carry):
        at = pl.multiple_of(FIRST + k * PART, 16)
        pre = pre_ref[pl.ds(at, PART), :]
        sig = 1.0 / (1.0 + jnp.exp(-pre))
        flat_ref[pl.ds(at + 8, PART), :] = hg_ref[pl.ds(at, PART), :] * (sig * (1.0 + pre * (1.0 - sig)))
        return carry

    lax.fori_loop(0, 9, grad_body, 0)
    shifted_copies(flat_ref, h_ref, FIRST, 9)
    for i in range(TR):
        at = 8 + place(i)
        own_ref[i * PITCH : i * PITCH + TC] = flat_ref[at : at + TC].astype(BF16)
        own_ref[i * PITCH + TC : (i + 1) * PITCH] = jnp.zeros((PITCH - TC, C), BF16)
    transpose_flat(own_ref, own_t_ref)
    weight_grad(x_ref, own_t_ref, 0)

    arrange_back(w1_ref, back_ref)

    def eg_body(k, carry):
        at = pl.multiple_of(OWN + k * 2 * PITCH, 16)
        got = back_rows(h_ref, at, 2 * PITCH, [back_ref[0], back_ref[1], back_ref[2]])
        eg_ref[pl.ds(pl.multiple_of(k * 2 * PITCH, 16), 2 * PITCH), :] = got.astype(BF16)
        return carry

    lax.fori_loop(0, TR // 2, eg_body, 0)

    @pl.when(north)
    def _():
        got = back_rows(h_ref, OWN, PITCH, [back_ref[2], back_ref[1], back_ref[2]])
        eg_ref[:PITCH] = got.astype(BF16)

    @pl.when(south)
    def _():
        got = back_rows(h_ref, place(TR - 1), PITCH, [back_ref[0], back_ref[1], back_ref[0]])
        eg_ref[(TR - 1) * PITCH :] = got.astype(BF16)

    total = jnp.zeros((FEAT, C), F32)
    for g in range(TR // 4):
        s_t = s_ref[:, g * 128 : (g + 1) * 128].T
        for k in range(4):
            i = 4 * g + k
            total += dot(s_t[k * FEAT : (k + 1) * FEAT], eg_ref[i * PITCH : i * PITCH + TC])
    red_ref[18 * C : 18 * C + FEAT] = total.astype(BF16)
    red_ref[18 * C + FEAT :] = jnp.zeros((red_ref.shape[0] - 18 * C - FEAT, C), BF16)


def main(where, s, halo, wide, w_first, w_second, hg, cot_t, owners):
    vmem = pl.BlockSpec(memory_space=pltpu.VMEM)
    return pl.pallas_call(
        main_kernel,
        in_specs=[pl.BlockSpec(memory_space=pltpu.SMEM)] + [vmem] * 10,
        out_specs=[vmem] * 2,
        out_shape=[
            jax.ShapeDtypeStruct((TR, TC, C), BF16),
            jax.ShapeDtypeStruct((owners * RED, C), BF16),
        ],
        scratch_shapes=[
            pltpu.VMEM((LEN + 16, C), F32),
            pltpu.VMEM((LEN, 3 * C), BF16),
            pltpu.VMEM((LEN, C), F32),
            pltpu.VMEM((LEN, 3 * C), BF16),
            pltpu.VMEM((3, C, 3 * C), BF16),
            pltpu.VMEM((TR * PITCH, C), BF16),
            pltpu.VMEM((C, TR * PITCH), BF16),
            pltpu.VMEM((TR * PITCH, C), BF16),
        ],
        compiler_params=pltpu.CompilerParams(vmem_limit_bytes=48 << 20),
        cost_estimate=pl.CostEstimate(flops=8 << 30, bytes_accessed=6 << 20, transcendentals=1 << 20),
        name="main",
    )(where, s, *halo, wide, w_first, w_second, hg, cot_t)


def sum_kernel(got_ref, out_ref):
    step = pl.program_id(0)

    @pl.when(step == 0)
    def _():
        out_ref[...] = jnp.sum(got_ref[...].astype(F32), axis=0)

    @pl.when(step > 0)
    def _():
        out_ref[...] += jnp.sum(got_ref[...].astype(F32), axis=0)


def unpack_kernel(got_ref, embed_ref, first_ref, second_ref):
    for r in range(3):
        for s in range(3):
            at = (3 * r + s) * C
            first_ref[r, s] = got_ref[at : at + C].astype(F32).T
            second_ref[r, s] = got_ref[at + 9 * C : at + 10 * C].astype(F32).T
    embed_ref[...] = got_ref[18 * C : 18 * C + 24].astype(F32)


def unpack(got, values):
    vmem = pl.BlockSpec(memory_space=pltpu.VMEM)
    return pl.pallas_call(
        unpack_kernel,
        in_specs=[vmem],
        out_specs=[vmem] * 3,
        out_shape=[
            jax.ShapeDtypeStruct((values, C), F32),
            jax.ShapeDtypeStruct((3, 3, C, C), F32),
            jax.ShapeDtypeStruct((3, 3, C, C), F32),
        ],
        name="unpack",
    )(got)


def exchange(bands, sectors, a, b, c, d, joined):
    number = lambda lat, lon: lat * sectors + lon % sectors

    def across(lat, lon):
        if lat % 2:
            return number(lat + 1, lon) if lat < bands - 1 else number(lat, lon + sectors // 2)
        return number(lat - 1, lon) if lat > 0 else number(lat, lon + sectors // 2)

    def swap(x, of):
        pairs = [(number(i, j), of(i, j)) for i in range(bands) for j in range(sectors)]
        return lax.ppermute(x, ALL, pairs)

    a = swap(a, lambda i, j: number(i, j ^ 1))
    b = swap(b, lambda i, j: number(i, j + 1 if j % 2 else j - 1))
    c, d = joined(a, b, c, d)
    return a, b, swap(c, lambda i, j: number(i ^ 1, j)), swap(d, across)


def per_device(obs_values, tile_ids, obs_rows, obs_cols, w_embed, w_first, w_second, cotangent):
    bands, sectors = lax.axis_size("lat"), lax.axis_size("lon")
    owners = bands * sectors
    count, values = obs_values.shape
    where = jnp.stack(
        [lax.axis_index("lat"), lax.axis_index("lon"), jnp.int32(bands), jnp.int32(sectors)]
    ).astype(jnp.int32)
    join_cot = lambda *x: join(join_cot_kernel, where, *x, (2, TC + 32, C), "join_cot")
    cot_halo = exchange(bands, sectors, *edges(where, cotangent), join_cot)

    packed = pack(tile_ids.T, obs_rows.reshape(1, count), obs_cols.reshape(1, count), obs_values.T)
    got = lax.all_to_all(packed, ALL, 0, 0, tiled=True)
    hg, cot_t = cot_back(where, cotangent, cot_halo, w_second)

    s, *s_edges = setconv(where, got)
    join_s = lambda *x: join(join_kernel, where, *x, (TC + 32, 128), "join")
    s_halo = exchange(bands, sectors, *s_edges, join_s)
    padded = jnp.concatenate([w_embed, jnp.zeros((FEAT - values, C), BF16)], axis=0)
    wide = jnp.kron(jnp.eye(4, dtype=BF16), padded)
    field, red = main(where, s, s_halo, wide, w_first, w_second, hg, cot_t, owners)

    parts = lax.all_to_all(red.reshape(owners, RED, C), ALL, 0, 0, tiled=True)
    summed = jnp.sum(parts.astype(F32), axis=0).astype(BF16)
    spread = jnp.broadcast_to(summed[None], (owners, RED, C))
    whole = lax.all_to_all(spread, ALL, 0, 0, tiled=True)
    grad_embed, grad_first, grad_second = unpack(whole.reshape(owners * RED, C), values)
    return (field, grad_embed, grad_first, grad_second)


def solution(mesh):
    in_specs = (
        P(ALL, None),
        P(ALL, None),
        P(ALL),
        P(ALL),
        P(),
        P(),
        P(),
        P("lat", "lon", None),
    )
    out_specs = (P("lat", "lon", None), P(), P(), P())
    return jax.shard_map(
        per_device, mesh=mesh, in_specs=in_specs, out_specs=out_specs, check_vma=False
    )
```

```python
import functools
import math
import jax
import jax.numpy as jnp
from jax import lax
from jax.experimental import pallas as pl
from jax.experimental.pallas import tpu as pltpu
from jax.sharding import PartitionSpec as P

F32 = jnp.float32
BF16 = jnp.bfloat16
spread_cells = 1.0
ALL = ("lat", "lon")

TR, TC, C = 16, 128, 128
PITCH = TC + 16
LEN = 3040
PART = 304
FIRST = PITCH
OWN = 16 + 2 * PITCH
FEAT = 32
RED = 24
HALF = 9 * C + FEAT
SG = TR * FEAT // 128
WIDE = 8


def dot(a, b):
    return jnp.dot(a, b, preferred_element_type=F32)


def dot_nt(a, b):
    return lax.dot_general(a, b, (((1,), (1,)), ((), ())), preferred_element_type=F32)


def place(i):
    return 16 + (i + 2) * PITCH


def pack_kernel(where_ref, ids_hbm, rows_hbm, cols_hbm, vals_hbm, out_ref,
                ids_ref, rows_ref, cols_ref, vals_ref, q_ref, v_ref, pair_ref, acc_ref, sems):
    step = pl.program_id(0)
    count = ids_ref.shape[1]
    owners = out_ref.shape[0] * pl.num_programs(0)
    sub = 256
    part = 2048
    pairs = out_ref.shape[0] // 2

    @pl.when(step == 0)
    def _():
        moves = [
            pltpu.make_async_copy(a, b, sems.at[k])
            for k, (a, b) in enumerate(
                [(ids_hbm, ids_ref), (rows_hbm, rows_ref), (cols_hbm, cols_ref), (vals_hbm, vals_ref)]
            )
        ]
        for move in moves:
            move.start()
        owner = lax.broadcasted_iota(jnp.int32, (owners, sub), 0)
        slot = lax.broadcasted_iota(jnp.int32, (sub, sub), 0)
        upto = slot <= lax.broadcasted_iota(jnp.int32, (sub, sub), 1)
        upto = jnp.concatenate(
            [jnp.where(upto, 1.0, 0.0).astype(BF16), jnp.ones((sub, 128), BF16)], axis=1
        )
        for move in moves:
            move.wait()

        def body(k, carry):
            for u in range(4):
                at = pl.ds(pl.multiple_of(k * 4 * sub + u * sub, sub), sub)
                ids = ids_ref[:, at]
                hot = owner == ids
                counted = dot(jnp.where(hot, 1.0, 0.0).astype(BF16), upto)
                before = counted[:, :sub] + jnp.concatenate([carry, carry], axis=1)
                rank = jnp.sum(jnp.where(hot, before, 0.0), axis=0, keepdims=True) - 1.0
                key = rank.astype(jnp.int32) + (ids & 1) * 128
                q_ref[:, at] = jnp.where(slot == key, 1.0, 0.0).astype(BF16)
                pair_ref[:, at] = jnp.broadcast_to((ids >> 1).astype(F32), (FEAT, sub)).astype(BF16)
                rows, cols = rows_ref[:, at], cols_ref[:, at]
                rows_hi, cols_hi = rows.astype(BF16).astype(F32), cols.astype(BF16).astype(F32)
                tail = jnp.concatenate(
                    [rows_hi, rows - rows_hi, cols_hi, cols - cols_hi, jnp.zeros((4, sub), F32)], axis=0
                )
                v_ref[:, at] = jnp.concatenate([vals_ref[:, at].astype(F32), tail], axis=0).astype(BF16)
                carry = carry + counted[:, sub:]
            return carry

        lax.fori_loop(0, count // sub // 4, body, jnp.zeros((owners, 128), F32))

    base = jnp.full((FEAT, part), (step * pairs).astype(F32), F32).astype(BF16)
    for k in range(count // part):
        at = pl.ds(k * part, part)
        pair = pair_ref[:, at] - base
        values = v_ref[:, at]
        none = jnp.zeros_like(values)
        left = jnp.concatenate([jnp.where(pair == p, values, none) for p in range(pairs)], axis=0)
        term = dot_nt(left, q_ref[:, at])
        if k == 0:
            acc_ref[...] = term
        else:
            acc_ref[...] += term
    for p in range(pairs):
        out_ref[2 * p] = acc_ref[p * FEAT : (p + 1) * FEAT, :128].astype(BF16)
        out_ref[2 * p + 1] = acc_ref[p * FEAT : (p + 1) * FEAT, 128:].astype(BF16)


def pack(where, ids, rows, cols, values):
    count = ids.shape[1]
    owners = 128
    steps = 4
    return pl.pallas_call(
        pack_kernel,
        grid=(steps,),
        in_specs=[pl.BlockSpec(memory_space=pltpu.SMEM)] + [pl.BlockSpec(memory_space=pl.ANY)] * 4,
        out_specs=pl.BlockSpec((owners // steps, FEAT, 128), lambda i: (i, 0, 0)),
        out_shape=jax.ShapeDtypeStruct((owners, FEAT, 128), BF16),
        scratch_shapes=[
            pltpu.VMEM(ids.shape, ids.dtype),
            pltpu.VMEM(rows.shape, rows.dtype),
            pltpu.VMEM(cols.shape, cols.dtype),
            pltpu.VMEM(values.shape, values.dtype),
            pltpu.VMEM((256, count), BF16),
            pltpu.VMEM((FEAT, count), BF16),
            pltpu.VMEM((FEAT, count), BF16),
            pltpu.VMEM((owners // steps // 2 * FEAT, 256), F32),
            pltpu.SemaphoreType.DMA((4,)),
        ],
        compiler_params=pltpu.CompilerParams(vmem_limit_bytes=58 << 20),
        cost_estimate=pl.CostEstimate(flops=2 * 2048 * 256 * 8192, bytes_accessed=3 << 20, transcendentals=0),
        name="pack",
    )(where, ids, rows, cols, values)


def setconv_kernel(where_ref, got_ref, cot_ref, s_ref, a_ref, b_ref, acc_ref):
    step = pl.program_id(0)
    x = jnp.concatenate([got_ref[k] for k in range(got_ref.shape[0])], axis=1).astype(F32)
    n = x.shape[1]
    alpha = math.sqrt(0.5 / math.log(2.0)) / spread_cells
    row = (x[24:25] + x[25:26]) * alpha
    col = (x[26:27] + x[27:28]) * alpha
    row_mid = (lax.broadcasted_iota(jnp.int32, (TR, n), 0).astype(F32) + 0.5) * alpha
    col_mid = (lax.broadcasted_iota(jnp.int32, (TC, n), 0).astype(F32) + 0.5) * alpha
    row_weight = jnp.exp2(-jnp.square(row - row_mid))
    col_weight = jnp.exp2(-jnp.square(col - col_mid)).astype(BF16)
    values = x[:24]
    weighted = jnp.concatenate([values * row_weight[i : i + 1] for i in range(TR)], axis=0).astype(BF16)
    term = dot_nt(weighted, col_weight)

    @pl.when(step == 0)
    def _():
        acc_ref[...] = term

    @pl.when(step > 0)
    def _():
        acc_ref[...] += term

    @pl.when(step == pl.num_programs(0) - 1)
    def _():
        none = jnp.zeros((FEAT - 24, TC), F32)
        for g in range(TR // 4):
            rows = []
            for i in range(4 * g, 4 * g + 4):
                rows += [acc_ref[24 * i : 24 * i + 24], none]
            s_ref[:, g * 128 : (g + 1) * 128] = jnp.concatenate(rows, axis=0).T.astype(BF16)
        even_lon, _ = evens(where_ref)
        for g in range(SG):
            left, right = s_ref[:16, g * 128 : (g + 1) * 128], s_ref[TC - 16 :, g * 128 : (g + 1) * 128]
            a_ref[g] = jnp.where(even_lon, right, left)
            b_ref[g] = jnp.where(even_lon, left, right)
        left, right = cot_ref[:, :16, :], cot_ref[:, TC - 16 :, :]
        a_ref[SG:] = jnp.where(even_lon, right, left)
        b_ref[SG:] = jnp.where(even_lon, left, right)


def setconv(where, got, cot):
    steps = 8
    fixed = lambda *shape: pl.BlockSpec(shape, lambda i: (0,) * len(shape))
    lanes = TR * FEAT
    shapes = [(TC, lanes), (SG + TR, 16, C), (SG + TR, 16, C)]
    return pl.pallas_call(
        setconv_kernel,
        grid=(steps,),
        in_specs=[
            pl.BlockSpec(memory_space=pltpu.SMEM),
            pl.BlockSpec((got.shape[0] // steps, FEAT, 128), lambda i: (i, 0, 0)),
            fixed(*cot.shape),
        ],
        out_specs=[fixed(*s) for s in shapes],
        out_shape=[jax.ShapeDtypeStruct(s, BF16) for s in shapes],
        scratch_shapes=[pltpu.VMEM((TR * 24, TC), F32)],
        compiler_params=pltpu.CompilerParams(vmem_limit_bytes=16 << 20),
        cost_estimate=pl.CostEstimate(
            flops=2 * 384 * 256 * 16384, bytes_accessed=2 << 20, transcendentals=144 * 16384
        ),
        name="setconv",
    )(where, got, cot)


def join_kernel(where_ref, a_ref, b_ref, s_ref, cot_ref, c_out, d_out):
    even_lon, even_lat = evens(where_ref)
    right = jnp.where(even_lon, a_ref[...], b_ref[...])
    left = jnp.where(even_lon, b_ref[...], a_ref[...])
    centre = slice(16, 16 + TC)
    for out, first in ((c_out, ~even_lat), (d_out, even_lat)):
        out[0, :16] = jnp.where(first, left[0], left[SG - 1])
        out[0, centre] = jnp.where(first, s_ref[:, :128], s_ref[:, -128:])
        out[0, 16 + TC :] = jnp.where(first, right[0], right[SG - 1])
        out[1:, :16] = jnp.where(first, left[SG : SG + 2], left[-2:])
        out[1:, centre] = jnp.where(first, cot_ref[:2], cot_ref[TR - 2 :])
        out[1:, 16 + TC :] = jnp.where(first, right[SG : SG + 2], right[-2:])


def join(where, a, b, s, cot):
    vmem = pl.BlockSpec(memory_space=pltpu.VMEM)
    return pl.pallas_call(
        join_kernel,
        in_specs=[pl.BlockSpec(memory_space=pltpu.SMEM)] + [vmem] * 4,
        out_specs=[vmem] * 2,
        out_shape=[jax.ShapeDtypeStruct((3, TC + 32, C), BF16)] * 2,
        cost_estimate=pl.CostEstimate(flops=0, bytes_accessed=1 << 18, transcendentals=0),
        compiler_params=pltpu.CompilerParams(vmem_limit_bytes=8 << 20),
        name="join",
    )(where, a, b, s, cot)


def shifted_copies(flat_ref, out_ref, begin, parts):
    def body(k, carry):
        at = pl.multiple_of(begin + k * PART, 16)
        for s in range(3):
            out_ref[pl.ds(at, PART), s * C : (s + 1) * C] = flat_ref[pl.ds(at + 7 + s, PART), :].astype(BF16)
        return carry

    lax.fori_loop(0, parts, body, 0)


def three_rows(src_ref, at, rows):
    return jnp.concatenate(
        [src_ref[pl.ds(at + (r - 1) * PITCH, rows), :] for r in range(3)], axis=1
    )


def conv_rows(src_ref, at, rows, weights):
    return dot(three_rows(src_ref, at, rows), jnp.concatenate(weights, axis=0))


def back_rows(src_ref, at, rows, weights):
    return dot_nt(three_rows(src_ref, at, rows), jnp.concatenate(weights, axis=1))


def fill_flat(flat_ref, begin, end, centre, left, right):
    first = lax.broadcasted_iota(jnp.int32, (16, C), 0) < 8
    flat_ref[place(begin) - 8 : place(begin) + 8] = left(begin)
    for i in range(begin, end):
        at = 8 + place(i)
        flat_ref[at : at + TC] = centre(i)
        after = jnp.where(first, right(i), left(i + 1)) if i < end - 1 else right(i)
        flat_ref[at + TC : at + PITCH] = after


def clear_flat(flat_ref, begin, end):
    flat_ref[begin:end] = jnp.zeros((end - begin, C), F32)


def evens(where_ref):
    return where_ref[1] % 2 == 0, where_ref[0] % 2 == 0


def arrange_back(w_ref, out_ref):
    for r in range(3):
        for s in range(3):
            out_ref[r, :, s * C : (s + 1) * C] = w_ref[2 - r, 2 - s]


def mid_kernel(where_ref, cot_ref, s_ref, a_ref, b_ref, w_ref, embed_ref,
               hg_ref, cot_t_ref, x_ref, flat_ref, copies_ref, back_ref, own_ref, wide_ref):
    even_lon, _ = evens(where_ref)
    left = jnp.where(even_lon, b_ref[SG:], a_ref[SG:])
    right = jnp.where(even_lon, a_ref[SG:], b_ref[SG:])
    row = lambda rows: lambda i: rows[i].astype(F32)
    clear_flat(flat_ref, 0, place(0) - 8)
    clear_flat(flat_ref, 8 + place(TR), flat_ref.shape[0])
    fill_flat(flat_ref, 0, TR, row(cot_ref), row(left), row(right))
    shifted_copies(flat_ref, copies_ref, 0, LEN // PART)
    arrange_back(w_ref, back_ref)

    def body(k, carry):
        at = pl.multiple_of(FIRST + k * 3 * PART, 16)
        hg_ref[pl.ds(at, 3 * PART), :] = back_rows(copies_ref, at, 3 * PART, [back_ref[0], back_ref[1], back_ref[2]])
        return carry

    lax.fori_loop(0, 3, body, 0)

    for i in range(TR):
        own_ref[i * PITCH : i * PITCH + TC] = cot_ref[i]
        own_ref[i * PITCH + TC : (i + 1) * PITCH] = jnp.zeros((PITCH - TC, C), BF16)
    transpose_flat(own_ref, cot_t_ref)

    wide = spread_weights(embed_ref, wide_ref)

    def rows_of(groups):
        groups = [dot(group, wide) for group in groups]
        return lambda i: groups[i // 4][:, i % 4 * C : (i % 4 + 1) * C]

    centre = rows_of([s_ref[:, g * 128 : (g + 1) * 128] for g in range(SG)])
    left = rows_of([jnp.where(even_lon, b_ref[g], a_ref[g]) for g in range(SG)])
    right = rows_of([jnp.where(even_lon, a_ref[g], b_ref[g]) for g in range(SG)])
    fill_flat(flat_ref, 0, TR, centre, left, right)
    shifted_copies(flat_ref, x_ref, 0, LEN // PART)


def spread_weights(embed_ref, wide_ref):
    values = embed_ref.shape[0]
    wide_ref[...] = jnp.zeros_like(wide_ref)
    for k in range(4):
        wide_ref[k * FEAT : k * FEAT + values, k * C : (k + 1) * C] = embed_ref[...].astype(F32)
    return wide_ref[...].astype(BF16)


def transpose_flat(own_ref, out_ref):
    out_ref[...] = own_ref[...].T


def mid(where, cot, s, a, b, w_second, w_embed):
    vmem = pl.BlockSpec(memory_space=pltpu.VMEM)
    return pl.pallas_call(
        mid_kernel,
        in_specs=[pl.BlockSpec(memory_space=pltpu.SMEM)] + [vmem] * 6,
        out_specs=[vmem] * 3,
        out_shape=[
            jax.ShapeDtypeStruct((LEN, C), F32),
            jax.ShapeDtypeStruct((C, TR * PITCH), BF16),
            jax.ShapeDtypeStruct((LEN, 3 * C), BF16),
        ],
        scratch_shapes=[
            pltpu.VMEM((LEN + 16, C), F32),
            pltpu.VMEM((LEN, 3 * C), BF16),
            pltpu.VMEM((3, C, 3 * C), BF16),
            pltpu.VMEM((TR * PITCH, C), BF16),
            pltpu.VMEM((4 * FEAT, 4 * C), F32),
        ],
        compiler_params=pltpu.CompilerParams(vmem_limit_bytes=24 << 20),
        cost_estimate=pl.CostEstimate(flops=2 * 2736 * 1152 * 256, bytes_accessed=4 << 20, transcendentals=0),
        name="mid",
    )(where, cot, s, a, b, w_second, w_embed)


def main_kernel(where_ref, cot_ref, s_ref, a_ref, b_ref, c_ref, d_ref,
                embed_ref, w1_ref, w2_ref, cot_t_ref, hg_in, x_in,
                field_ref, red_ref, hg_ref, x_ref,
                flat_ref, pre_ref, h_ref, back_ref, own_ref, own_t_ref, eg_ref, wide_ref):
    even_lon, even_lat = evens(where_ref)
    north = where_ref[0] == 0
    south = where_ref[0] == where_ref[2] - 1
    north_row, south_row = jnp.where(north, 2, 0), jnp.where(south, 0, 2)
    pad, centre, tail = slice(0, 16), slice(16, 16 + TC), slice(16 + TC, 32 + TC)

    def edge(k):
        up = jnp.where(even_lat, d_ref[k], c_ref[k])
        down = jnp.where(even_lat, c_ref[k], d_ref[k])
        left = lambda i: jnp.where(even_lon, b_ref[i], a_ref[i])
        right = lambda i: jnp.where(even_lon, a_ref[i], b_ref[i])
        return up, down, left, right

    up0, down0, left, right = edge(1)
    up1, down1, _, _ = edge(2)

    def cot_rows(part, inner):
        near_up, far_up = jnp.where(north, up0[part], up1[part]), jnp.where(north, up1[part], up0[part])
        near_down, far_down = jnp.where(south, down1[part], down0[part]), jnp.where(south, down0[part], down1[part])
        outer = {-1: near_up, -2: far_up, TR: near_down, TR + 1: far_down}
        return lambda i: (outer[i] if i in outer else inner(i)).astype(F32)

    rows = (
        cot_rows(centre, lambda i: cot_ref[i]),
        cot_rows(pad, lambda i: left(SG + i)),
        cot_rows(tail, lambda i: right(SG + i)),
    )
    fill_flat(flat_ref, -2, 2, *rows)
    fill_flat(flat_ref, TR - 2, TR + 2, *rows)
    shifted_copies(flat_ref, h_ref, 0, 2)
    shifted_copies(flat_ref, h_ref, place(TR - 2) - 32, 2)
    arrange_back(w2_ref, back_ref)
    at = place(-1) - 16
    got = back_rows(h_ref, at, PART, [back_ref[north_row], back_ref[1], back_ref[2]])
    hg_ref[at + 8 : at + PART - 8] = got[8:-8]
    at = place(TR - 1) - 16
    got = back_rows(h_ref, at, PART, [back_ref[0], back_ref[1], back_ref[south_row]])
    hg_ref[at + 8 : at + PART - 8] = got[8:-8]

    wide = spread_weights(embed_ref, wide_ref)
    up, down, left, right = edge(0)

    def embed_rows(part, first, last):
        block = lambda rows, k: rows[:, k * C : (k + 1) * C]
        up_, down_ = dot(up[part], wide), dot(down[part], wide)
        first, last = dot(first, wide), dot(last, wide)
        outer = {
            -1: jnp.where(north, block(up_, 0), block(up_, 3)),
            -2: jnp.where(north, block(up_, 1), block(up_, 2)),
            TR: jnp.where(south, block(down_, 3), block(down_, 0)),
            TR + 1: jnp.where(south, block(down_, 2), block(down_, 1)),
        }
        return lambda i: outer[i] if i in outer else block(first, i) if i < 4 else block(last, i - TR + 4)

    rows = (
        embed_rows(centre, s_ref[:, :128], s_ref[:, -128:]),
        embed_rows(pad, left(0), left(SG - 1)),
        embed_rows(tail, right(0), right(SG - 1)),
    )
    clear_flat(flat_ref, 0, 8)
    fill_flat(flat_ref, -2, 1, *rows)
    fill_flat(flat_ref, TR - 1, TR + 2, *rows)
    clear_flat(flat_ref, 8 + place(TR + 2), flat_ref.shape[0])
    shifted_copies(flat_ref, x_ref, 0, 1)
    shifted_copies(flat_ref, x_ref, place(TR) - 16, 1)

    def weights(w_ref, order):
        return [w_ref[r].reshape(3 * C, C) for r in order]

    def pre_body(k, carry):
        at = pl.multiple_of(FIRST + k * 3 * PART, 16)
        pre_ref[pl.ds(at, 3 * PART), :] = conv_rows(x_ref, at, 3 * PART, weights(w1_ref, (0, 1, 2)))
        return carry

    lax.fori_loop(0, 3, pre_body, 0)

    def pole_pre(at):
        got = conv_rows(x_ref, at, PITCH + 16, weights(w1_ref, (2, 1, 0)))
        pre_ref[at + 8 : at + PITCH + 8] = got[8:-8]

    @pl.when(north)
    def _():
        pole_pre(place(-1) - 16)

    @pl.when(south)
    def _():
        pole_pre(place(TR) - 16)

    flat_ref[8 + FIRST - 16 : 8 + FIRST] = jnp.zeros((16, C), F32)
    flat_ref[8 + FIRST + 9 * PART : 24 + FIRST + 9 * PART] = jnp.zeros((16, C), F32)

    def hidden_body(k, carry):
        at = pl.multiple_of(FIRST + k * PART, 16)
        pre = pre_ref[pl.ds(at, PART), :]
        flat_ref[pl.ds(at + 8, PART), :] = pre / (1.0 + jnp.exp(-pre))
        return carry

    lax.fori_loop(0, 9, hidden_body, 0)
    shifted_copies(flat_ref, h_ref, FIRST, 9)

    def field_body(k, carry):
        at = pl.multiple_of(OWN + k * WIDE * PITCH, 16)
        got = conv_rows(h_ref, at, WIDE * PITCH, weights(w2_ref, (0, 1, 2))).astype(BF16)
        for u in range(WIDE):
            field_ref[WIDE * k + u] = got[u * PITCH : u * PITCH + TC]
        return carry

    lax.fori_loop(0, TR // WIDE, field_body, 0)

    def weight_grad(src_ref, grad_t_ref, half):
        for r in range(3):
            at = OWN + (r - 1) * PITCH
            got = dot(grad_t_ref[...], src_ref[at : at + TR * PITCH]).astype(BF16)
            for s in range(3):
                to = (3 * r + s) * C
                red_ref[half, to : to + C] = got[:, s * C : (s + 1) * C]

    weight_grad(h_ref, cot_t_ref, 0)

    def grad_body(k, carry):
        at = pl.multiple_of(FIRST + k * PART, 16)
        pre = pre_ref[pl.ds(at, PART), :]
        sig = 1.0 / (1.0 + jnp.exp(-pre))
        flat_ref[pl.ds(at + 8, PART), :] = hg_ref[pl.ds(at, PART), :] * (sig * (1.0 + pre * (1.0 - sig)))
        return carry

    lax.fori_loop(0, 9, grad_body, 0)
    shifted_copies(flat_ref, h_ref, FIRST, 9)
    for i in range(TR):
        at = 8 + place(i)
        own_ref[i * PITCH : i * PITCH + TC] = flat_ref[at : at + TC].astype(BF16)
        own_ref[i * PITCH + TC : (i + 1) * PITCH] = jnp.zeros((PITCH - TC, C), BF16)
    transpose_flat(own_ref, own_t_ref)
    weight_grad(x_ref, own_t_ref, 1)

    arrange_back(w1_ref, back_ref)

    def eg_body(k, carry):
        at = pl.multiple_of(OWN + k * WIDE * PITCH, 16)
        got = back_rows(h_ref, at, WIDE * PITCH, [back_ref[0], back_ref[1], back_ref[2]])
        eg_ref[pl.ds(pl.multiple_of(k * WIDE * PITCH, 16), WIDE * PITCH), :] = got.astype(BF16)
        return carry

    lax.fori_loop(0, TR // WIDE, eg_body, 0)

    @pl.when(north)
    def _():
        got = back_rows(h_ref, OWN, PITCH, [back_ref[2], back_ref[1], back_ref[2]])
        eg_ref[:PITCH] = got.astype(BF16)

    @pl.when(south)
    def _():
        got = back_rows(h_ref, place(TR - 1), PITCH, [back_ref[0], back_ref[1], back_ref[0]])
        eg_ref[(TR - 1) * PITCH :] = got.astype(BF16)

    total = jnp.zeros((FEAT, C), F32)
    for g in range(TR // 4):
        s_t = s_ref[:, g * 128 : (g + 1) * 128].T
        for k in range(4):
            i = 4 * g + k
            total += dot(s_t[k * FEAT : (k + 1) * FEAT], eg_ref[i * PITCH : i * PITCH + TC])
    red_ref[0, 9 * C :] = jnp.zeros((FEAT, C), BF16)
    red_ref[1, 9 * C :] = total.astype(BF16)


def main(where, cot, s, halo, w_embed, w_first, w_second, cot_t, hg, x):
    vmem = pl.BlockSpec(memory_space=pltpu.VMEM)
    return pl.pallas_call(
        main_kernel,
        in_specs=[pl.BlockSpec(memory_space=pltpu.SMEM)] + [vmem] * 12,
        out_specs=[vmem] * 4,
        out_shape=[
            jax.ShapeDtypeStruct((TR, TC, C), BF16),
            jax.ShapeDtypeStruct((2, HALF, C), BF16),
            jax.ShapeDtypeStruct(hg.shape, hg.dtype),
            jax.ShapeDtypeStruct(x.shape, x.dtype),
        ],
        input_output_aliases={11: 2, 12: 3},
        scratch_shapes=[
            pltpu.VMEM((LEN + 16, C), F32),
            pltpu.VMEM((LEN, C), F32),
            pltpu.VMEM((LEN, 3 * C), BF16),
            pltpu.VMEM((3, C, 3 * C), BF16),
            pltpu.VMEM((TR * PITCH, C), BF16),
            pltpu.VMEM((C, TR * PITCH), BF16),
            pltpu.VMEM((TR * PITCH, C), BF16),
            pltpu.VMEM((4 * FEAT, 4 * C), F32),
        ],
        compiler_params=pltpu.CompilerParams(vmem_limit_bytes=32 << 20),
        cost_estimate=pl.CostEstimate(flops=8 << 30, bytes_accessed=6 << 20, transcendentals=1 << 20),
        name="main",
    )(where, cot, s, *halo, w_embed, w_first, w_second, cot_t, hg, x)


def unpack_kernel(where_ref, own_ref, other_ref, embed_ref, first_ref, second_ref):
    first_core = where_ref[1] % 2 == 0

    def half(k, at, rows):
        own, other = own_ref[at : at + rows], other_ref[at : at + rows]
        return jnp.where(first_core, own, other) if k == 0 else jnp.where(first_core, other, own)

    for r in range(3):
        for s in range(3):
            at = (3 * r + s) * C
            first_ref[r, s] = half(1, at, C).T.astype(F32)
            second_ref[r, s] = half(0, at, C).T.astype(F32)
    embed_ref[...] = half(1, 9 * C, FEAT)[: embed_ref.shape[0]].astype(F32)


def unpack(where, own, other, values):
    vmem = pl.BlockSpec(memory_space=pltpu.VMEM)
    return pl.pallas_call(
        unpack_kernel,
        in_specs=[pl.BlockSpec(memory_space=pltpu.SMEM), vmem, vmem],
        out_specs=[vmem] * 3,
        out_shape=[
            jax.ShapeDtypeStruct((values, C), F32),
            jax.ShapeDtypeStruct((3, 3, C, C), F32),
            jax.ShapeDtypeStruct((3, 3, C, C), F32),
        ],
        compiler_params=pltpu.CompilerParams(vmem_limit_bytes=16 << 20),
        name="unpack",
    )(where, own, other)


def swaps(bands, sectors):
    number = lambda lat, lon: lat * sectors + lon % sectors

    def across(lat, lon):
        if lat % 2:
            return number(lat + 1, lon) if lat < bands - 1 else number(lat, lon + sectors // 2)
        return number(lat - 1, lon) if lat > 0 else number(lat, lon + sectors // 2)

    def swap(of):
        pairs = [(number(i, j), of(i, j)) for i in range(bands) for j in range(sectors)]
        return lambda x: lax.ppermute(x, ALL, pairs)

    return (
        swap(lambda i, j: number(i, j ^ 1)),
        swap(lambda i, j: number(i, j + 1 if j % 2 else j - 1)),
        swap(lambda i, j: number(i ^ 1, j)),
        swap(across),
    )


def per_device(obs_values, tile_ids, obs_rows, obs_cols, w_embed, w_first, w_second, cotangent):
    bands, sectors = lax.axis_size("lat"), lax.axis_size("lon")
    owners = bands * sectors
    count, values = obs_values.shape
    where = jnp.stack(
        [lax.axis_index("lat"), lax.axis_index("lon"), jnp.int32(bands), jnp.int32(sectors)]
    ).astype(jnp.int32)
    swap_a, swap_b, swap_c, swap_d = swaps(bands, sectors)
    packed = pack(where, tile_ids.T, obs_rows.reshape(1, count), obs_cols.reshape(1, count), obs_values.T)
    got = lax.all_to_all(packed, ALL, 0, 0, tiled=True)
    s, a, b = setconv(where, got, cotangent)
    a, b = swap_a(a), swap_b(b)
    c, d = join(where, a, b, s, cotangent)
    hg, cot_t, x = mid(where, cotangent, s, a, b, w_second, w_embed)
    halo = (a, b, swap_c(c), swap_d(d))
    field, red, _, _ = main(where, cotangent, s, halo, w_embed, w_first, w_second, cot_t, hg, x)

    chips = owners // 2
    groups = [[2 * k + core for k in range(chips)] for core in range(2)]
    mine = lax.axis_index("lon") % 2
    theirs = swap_a(red)
    half = red[mine].astype(F32) + theirs[mine].astype(F32)
    half = jnp.pad(half.astype(BF16), ((0, chips * RED - HALF), (0, 0))).reshape(chips, RED, C)
    parts = lax.all_to_all(half, ALL, 0, 0, axis_index_groups=groups, tiled=True)
    summed = jnp.sum(parts.astype(F32), axis=0).astype(BF16)
    spread = jnp.broadcast_to(summed[None], (chips, RED, C))
    own = lax.all_to_all(spread, ALL, 0, 0, axis_index_groups=groups, tiled=True).reshape(chips * RED, C)
    other = swap_a(own)
    grad_embed, grad_first, grad_second = unpack(where, own, other, values)
    return (field, grad_embed, grad_first, grad_second)


def solution(mesh):
    in_specs = (
        P(ALL, None),
        P(ALL, None),
        P(ALL),
        P(ALL),
        P(),
        P(),
        P(),
        P("lat", "lon", None),
    )
    out_specs = (P("lat", "lon", None), P(), P(), P())
    return jax.shard_map(
        per_device, mesh=mesh, in_specs=in_specs, out_specs=out_specs, check_vma=False
    )
```

```python
import functools
import math
import jax
import jax.numpy as jnp
from jax import lax
from jax.experimental import pallas as pl
from jax.experimental.pallas import tpu as pltpu
from jax.sharding import PartitionSpec as P

F32 = jnp.float32
BF16 = jnp.bfloat16
spread_cells = 1.0
ALL = ("lat", "lon")

TR, TC, C = 16, 128, 128
PITCH = TC + 16
LEN = 3040
PART = 304
FIRST = PITCH
OWN = 16 + 2 * PITCH
FEAT = 32
RED = 24
HALF = 9 * C + FEAT
SG = TR * FEAT // 128
WIDE = 8


def dot(a, b):
    return jnp.dot(a, b, preferred_element_type=F32)


def dot_nt(a, b):
    return lax.dot_general(a, b, (((1,), (1,)), ((), ())), preferred_element_type=F32)


def place(i):
    return 16 + (i + 2) * PITCH


def pack_kernel(ids_hbm, rows_hbm, cols_hbm, vals_hbm, out_ref,
                ids_ref, rows_ref, cols_ref, vals_ref, q_ref, v_ref, pair_ref, acc_ref, sems):
    step = pl.program_id(0)
    count = ids_ref.shape[1]
    owners = out_ref.shape[0] * pl.num_programs(0)
    sub = 256
    part = 2048
    pairs = out_ref.shape[0] // 2

    @pl.when(step == 0)
    def _():
        moves = [
            pltpu.make_async_copy(a, b, sems.at[k])
            for k, (a, b) in enumerate(
                [(ids_hbm, ids_ref), (rows_hbm, rows_ref), (cols_hbm, cols_ref), (vals_hbm, vals_ref)]
            )
        ]
        for move in moves:
            move.start()
        owner = lax.broadcasted_iota(jnp.int32, (owners, sub), 0)
        slot = lax.broadcasted_iota(jnp.int32, (sub, sub), 0)
        upto = slot <= lax.broadcasted_iota(jnp.int32, (sub, sub), 1)
        upto = jnp.concatenate(
            [jnp.where(upto, 1.0, 0.0).astype(BF16), jnp.ones((sub, 128), BF16)], axis=1
        )
        slot = slot.astype(F32).astype(BF16)
        one, none = jnp.ones((sub, sub), BF16), jnp.zeros((sub, sub), BF16)

        def rows_of_16(row, rows):
            return jnp.concatenate([jnp.broadcast_to(row, (16, sub)).astype(BF16)] * (rows // 16), axis=0)

        for move in moves:
            move.wait()

        def body(k, carry):
            for u in range(4):
                at = pl.ds(pl.multiple_of(k * 4 * sub + u * sub, sub), sub)
                ids = ids_ref[:, at]
                hot = owner == ids
                counted = dot(jnp.where(hot, 1.0, 0.0).astype(BF16), upto)
                before = counted[:, :sub] + jnp.concatenate([carry, carry], axis=1)
                rank = jnp.sum(jnp.where(hot, before, 0.0), axis=0, keepdims=True) - 1.0
                key = rank + ((ids & 1) * 128).astype(F32)
                q_ref[:, at] = jnp.where(slot == rows_of_16(key, sub), one, none)
                pair_ref[:, at] = rows_of_16((ids >> 1).astype(F32), FEAT)
                rows, cols = rows_ref[:, at], cols_ref[:, at]
                rows_hi, cols_hi = rows.astype(BF16).astype(F32), cols.astype(BF16).astype(F32)
                tail = jnp.concatenate(
                    [rows_hi, rows - rows_hi, cols_hi, cols - cols_hi, jnp.zeros((4, sub), F32)], axis=0
                )
                v_ref[:, at] = jnp.concatenate([vals_ref[:, at].astype(F32), tail], axis=0).astype(BF16)
                carry = carry + counted[:, sub:]
            return carry

        lax.fori_loop(0, count // sub // 4, body, jnp.zeros((owners, 128), F32))

    base = jnp.full((FEAT, part), (step * pairs).astype(F32), F32).astype(BF16)
    for k in range(count // part):
        at = pl.ds(k * part, part)
        pair = pair_ref[:, at] - base
        values = v_ref[:, at]
        none = jnp.zeros_like(values)
        left = jnp.concatenate([jnp.where(pair == p, values, none) for p in range(pairs)], axis=0)
        term = dot_nt(left, q_ref[:, at])
        if k == 0:
            acc_ref[...] = term
        else:
            acc_ref[...] += term
    for p in range(pairs):
        out_ref[2 * p] = acc_ref[p * FEAT : (p + 1) * FEAT, :128].astype(BF16)
        out_ref[2 * p + 1] = acc_ref[p * FEAT : (p + 1) * FEAT, 128:].astype(BF16)


def pack(ids, rows, cols, values):
    count = ids.shape[1]
    owners = 128
    steps = 4
    return pl.pallas_call(
        pack_kernel,
        grid=(steps,),
        in_specs=[pl.BlockSpec(memory_space=pl.ANY)] * 4,
        out_specs=pl.BlockSpec((owners // steps, FEAT, 128), lambda i: (i, 0, 0)),
        out_shape=jax.ShapeDtypeStruct((owners, FEAT, 128), BF16),
        scratch_shapes=[
            pltpu.VMEM(ids.shape, ids.dtype),
            pltpu.VMEM(rows.shape, rows.dtype),
            pltpu.VMEM(cols.shape, cols.dtype),
            pltpu.VMEM(values.shape, values.dtype),
            pltpu.VMEM((256, count), BF16),
            pltpu.VMEM((FEAT, count), BF16),
            pltpu.VMEM((FEAT, count), BF16),
            pltpu.VMEM((owners // steps // 2 * FEAT, 256), F32),
            pltpu.SemaphoreType.DMA((4,)),
        ],
        compiler_params=pltpu.CompilerParams(vmem_limit_bytes=58 << 20),
        cost_estimate=pl.CostEstimate(flops=2 * 2048 * 256 * 8192, bytes_accessed=3 << 20, transcendentals=0),
        name="pack",
    )(ids, rows, cols, values)


def setconv_kernel(where_ref, got_ref, cot_ref, s_ref, a_ref, b_ref, acc_ref):
    step = pl.program_id(0)
    x = jnp.concatenate([got_ref[k] for k in range(got_ref.shape[0])], axis=1).astype(F32)
    n = x.shape[1]
    alpha = math.sqrt(0.5 / math.log(2.0)) / spread_cells
    row = (x[24:25] + x[25:26]) * alpha
    col = (x[26:27] + x[27:28]) * alpha
    row_mid = (lax.broadcasted_iota(jnp.int32, (TR, n), 0).astype(F32) + 0.5) * alpha
    col_mid = (lax.broadcasted_iota(jnp.int32, (TC, n), 0).astype(F32) + 0.5) * alpha
    row_weight = jnp.exp2(-jnp.square(row - row_mid))
    col_weight = jnp.exp2(-jnp.square(col - col_mid)).astype(BF16)
    values = x[:24]
    weighted = jnp.concatenate([values * row_weight[i : i + 1] for i in range(TR)], axis=0).astype(BF16)
    term = dot_nt(weighted, col_weight)

    @pl.when(step == 0)
    def _():
        acc_ref[...] = term

    @pl.when(step > 0)
    def _():
        acc_ref[...] += term

    @pl.when(step == pl.num_programs(0) - 1)
    def _():
        none = jnp.zeros((FEAT - 24, TC), F32)
        for g in range(TR // 4):
            rows = []
            for i in range(4 * g, 4 * g + 4):
                rows += [acc_ref[24 * i : 24 * i + 24], none]
            s_ref[:, g * 128 : (g + 1) * 128] = jnp.concatenate(rows, axis=0).T.astype(BF16)
        even_lon, _ = evens(where_ref)
        for g in range(SG):
            left, right = s_ref[:16, g * 128 : (g + 1) * 128], s_ref[TC - 16 :, g * 128 : (g + 1) * 128]
            a_ref[g] = jnp.where(even_lon, right, left)
            b_ref[g] = jnp.where(even_lon, left, right)
        left, right = cot_ref[:, :16, :], cot_ref[:, TC - 16 :, :]
        a_ref[SG:] = jnp.where(even_lon, right, left)
        b_ref[SG:] = jnp.where(even_lon, left, right)


def setconv(where, got, cot):
    steps = 4
    fixed = lambda *shape: pl.BlockSpec(shape, lambda i: (0,) * len(shape))
    lanes = TR * FEAT
    shapes = [(TC, lanes), (SG + TR, 16, C), (SG + TR, 16, C)]
    return pl.pallas_call(
        setconv_kernel,
        grid=(steps,),
        in_specs=[
            pl.BlockSpec(memory_space=pltpu.SMEM),
            pl.BlockSpec((got.shape[0] // steps, FEAT, 128), lambda i: (i, 0, 0)),
            fixed(*cot.shape),
        ],
        out_specs=[fixed(*s) for s in shapes],
        out_shape=[jax.ShapeDtypeStruct(s, BF16) for s in shapes],
        scratch_shapes=[pltpu.VMEM((TR * 24, TC), F32)],
        compiler_params=pltpu.CompilerParams(vmem_limit_bytes=16 << 20),
        cost_estimate=pl.CostEstimate(
            flops=2 * 384 * 256 * 16384, bytes_accessed=2 << 20, transcendentals=144 * 16384
        ),
        name="setconv",
    )(where, got, cot)


def join_kernel(where_ref, a_ref, b_ref, s_ref, cot_ref, c_out, d_out):
    even_lon, even_lat = evens(where_ref)
    right = jnp.where(even_lon, a_ref[...], b_ref[...])
    left = jnp.where(even_lon, b_ref[...], a_ref[...])
    centre = slice(16, 16 + TC)
    for out, first in ((c_out, ~even_lat), (d_out, even_lat)):
        out[0, :16] = jnp.where(first, left[0], left[SG - 1])
        out[0, centre] = jnp.where(first, s_ref[:, :128], s_ref[:, -128:])
        out[0, 16 + TC :] = jnp.where(first, right[0], right[SG - 1])
        out[1:, :16] = jnp.where(first, left[SG : SG + 2], left[-2:])
        out[1:, centre] = jnp.where(first, cot_ref[:2], cot_ref[TR - 2 :])
        out[1:, 16 + TC :] = jnp.where(first, right[SG : SG + 2], right[-2:])


def join(where, a, b, s, cot):
    vmem = pl.BlockSpec(memory_space=pltpu.VMEM)
    return pl.pallas_call(
        join_kernel,
        in_specs=[pl.BlockSpec(memory_space=pltpu.SMEM)] + [vmem] * 4,
        out_specs=[vmem] * 2,
        out_shape=[jax.ShapeDtypeStruct((3, TC + 32, C), BF16)] * 2,
        cost_estimate=pl.CostEstimate(flops=0, bytes_accessed=1 << 18, transcendentals=0),
        compiler_params=pltpu.CompilerParams(vmem_limit_bytes=8 << 20),
        name="join",
    )(where, a, b, s, cot)


def shifted_copies(flat_ref, out_ref, begin, parts):
    def body(k, carry):
        at = pl.multiple_of(begin + k * PART, 16)
        for s in range(3):
            out_ref[pl.ds(at, PART), s * C : (s + 1) * C] = flat_ref[pl.ds(at + 7 + s, PART), :].astype(BF16)
        return carry

    lax.fori_loop(0, parts, body, 0)


def three_rows(src_ref, at, rows):
    return jnp.concatenate(
        [src_ref[pl.ds(at + (r - 1) * PITCH, rows), :] for r in range(3)], axis=1
    )


def conv_rows(src_ref, at, rows, weights):
    return dot(three_rows(src_ref, at, rows), jnp.concatenate(weights, axis=0))


def back_rows(src_ref, at, rows, weights):
    return dot_nt(three_rows(src_ref, at, rows), jnp.concatenate(weights, axis=1))


def fill_flat(flat_ref, begin, end, centre, left, right):
    first = lax.broadcasted_iota(jnp.int32, (16, C), 0) < 8
    flat_ref[place(begin) - 8 : place(begin) + 8] = left(begin)
    for i in range(begin, end):
        at = 8 + place(i)
        flat_ref[at : at + TC] = centre(i)
        after = jnp.where(first, right(i), left(i + 1)) if i < end - 1 else right(i)
        flat_ref[at + TC : at + PITCH] = after


def clear_flat(flat_ref, begin, end):
    flat_ref[begin:end] = jnp.zeros((end - begin, C), F32)


def evens(where_ref):
    return where_ref[1] % 2 == 0, where_ref[0] % 2 == 0


def arrange_back(w_ref, out_ref):
    for r in range(3):
        for s in range(3):
            out_ref[r, :, s * C : (s + 1) * C] = w_ref[2 - r, 2 - s]


def prep_kernel(cot_ref, embed_ref, w1_ref, w2_ref, cot_t_ref, wide_ref, back1_ref, back2_ref, own_ref):
    for i in range(TR):
        own_ref[i * PITCH : i * PITCH + TC] = cot_ref[i]
        own_ref[i * PITCH + TC : (i + 1) * PITCH] = jnp.zeros((PITCH - TC, C), BF16)
    transpose_flat(own_ref, cot_t_ref)
    values = embed_ref.shape[0]
    padded = jnp.concatenate([embed_ref[...].astype(F32), jnp.zeros((FEAT - values, C), F32)], axis=0).astype(BF16)
    wide_ref[...] = jnp.zeros_like(wide_ref)
    for k in range(4):
        wide_ref[k * FEAT : (k + 1) * FEAT, k * C : (k + 1) * C] = padded
    arrange_back(w1_ref, back1_ref)
    arrange_back(w2_ref, back2_ref)


def prep(cot, w_embed, w_first, w_second):
    vmem = pl.BlockSpec(memory_space=pltpu.VMEM)
    return pl.pallas_call(
        prep_kernel,
        in_specs=[vmem] * 4,
        out_specs=[vmem] * 4,
        out_shape=[
            jax.ShapeDtypeStruct((C, TR * PITCH), BF16),
            jax.ShapeDtypeStruct((4 * FEAT, 4 * C), BF16),
            jax.ShapeDtypeStruct((3, C, 3 * C), BF16),
            jax.ShapeDtypeStruct((3, C, 3 * C), BF16),
        ],
        scratch_shapes=[pltpu.VMEM((TR * PITCH, C), BF16)],
        compiler_params=pltpu.CompilerParams(vmem_limit_bytes=16 << 20),
        cost_estimate=pl.CostEstimate(flops=1 << 20, bytes_accessed=4 << 20, transcendentals=0),
        name="prep",
    )(cot, w_embed, w_first, w_second)


def mid_kernel(where_ref, cot_ref, s_ref, a_ref, b_ref, back_ref, wide_ref, w1_ref,
               hg_ref, x_ref, pre_ref, flat_ref, copies_ref):
    even_lon, _ = evens(where_ref)
    left = jnp.where(even_lon, b_ref[SG:], a_ref[SG:])
    right = jnp.where(even_lon, a_ref[SG:], b_ref[SG:])
    row = lambda rows: lambda i: rows[i].astype(F32)
    clear_flat(flat_ref, 0, place(0) - 8)
    clear_flat(flat_ref, 8 + place(TR), flat_ref.shape[0])
    fill_flat(flat_ref, 0, TR, row(cot_ref), row(left), row(right))
    shifted_copies(flat_ref, copies_ref, 0, LEN // PART)

    def body(k, carry):
        at = pl.multiple_of(FIRST + k * 3 * PART, 16)
        hg_ref[pl.ds(at, 3 * PART), :] = back_rows(copies_ref, at, 3 * PART, [back_ref[0], back_ref[1], back_ref[2]])
        return carry

    lax.fori_loop(0, 3, body, 0)

    wide = wide_ref[...]

    def rows_of(groups):
        groups = [dot(group, wide) for group in groups]
        return lambda i: groups[i // 4][:, i % 4 * C : (i % 4 + 1) * C]

    centre = rows_of([s_ref[:, g * 128 : (g + 1) * 128] for g in range(SG)])
    left = rows_of([jnp.where(even_lon, b_ref[g], a_ref[g]) for g in range(SG)])
    right = rows_of([jnp.where(even_lon, a_ref[g], b_ref[g]) for g in range(SG)])
    fill_flat(flat_ref, 0, TR, centre, left, right)
    shifted_copies(flat_ref, x_ref, 0, LEN // PART)

    def pre_body(k, carry):
        at = pl.multiple_of(FIRST + k * 3 * PART, 16)
        pre_ref[pl.ds(at, 3 * PART), :] = conv_rows(x_ref, at, 3 * PART, taps(w1_ref, (0, 1, 2)))
        return carry

    lax.fori_loop(0, 3, pre_body, 0)


def taps(w_ref, order):
    return [w_ref[r].reshape(3 * C, C) for r in order]


def transpose_flat(own_ref, out_ref):
    out_ref[...] = own_ref[...].T


def mid(where, cot, s, a, b, back, wide, w_first):
    vmem = pl.BlockSpec(memory_space=pltpu.VMEM)
    return pl.pallas_call(
        mid_kernel,
        in_specs=[pl.BlockSpec(memory_space=pltpu.SMEM)] + [vmem] * 7,
        out_specs=[vmem] * 3,
        out_shape=[
            jax.ShapeDtypeStruct((LEN, C), F32),
            jax.ShapeDtypeStruct((LEN, 3 * C), BF16),
            jax.ShapeDtypeStruct((LEN, C), F32),
        ],
        scratch_shapes=[pltpu.VMEM((LEN + 16, C), F32), pltpu.VMEM((LEN, 3 * C), BF16)],
        compiler_params=pltpu.CompilerParams(vmem_limit_bytes=24 << 20),
        cost_estimate=pl.CostEstimate(flops=2 * 2736 * 1152 * 256, bytes_accessed=4 << 20, transcendentals=0),
        name="mid",
    )(where, cot, s, a, b, back, wide, w_first)


def main_kernel(where_ref, cot_ref, s_ref, a_ref, b_ref, c_ref, d_ref,
                wide_ref, w1_ref, w2_ref, back1_ref, back2_ref, cot_t_ref, hg_in, x_in, pre_in,
                field_ref, red_ref, hg_ref, x_ref, pre_ref,
                flat_ref, h_ref, own_ref, own_t_ref, eg_ref):
    even_lon, even_lat = evens(where_ref)
    north = where_ref[0] == 0
    south = where_ref[0] == where_ref[2] - 1
    north_row, south_row = jnp.where(north, 2, 0), jnp.where(south, 0, 2)
    pad, centre, tail = slice(0, 16), slice(16, 16 + TC), slice(16 + TC, 32 + TC)

    def edge(k):
        up = jnp.where(even_lat, d_ref[k], c_ref[k])
        down = jnp.where(even_lat, c_ref[k], d_ref[k])
        left = lambda i: jnp.where(even_lon, b_ref[i], a_ref[i])
        right = lambda i: jnp.where(even_lon, a_ref[i], b_ref[i])
        return up, down, left, right

    up0, down0, left, right = edge(1)
    up1, down1, _, _ = edge(2)

    def cot_rows(part, inner):
        near_up, far_up = jnp.where(north, up0[part], up1[part]), jnp.where(north, up1[part], up0[part])
        near_down, far_down = jnp.where(south, down1[part], down0[part]), jnp.where(south, down0[part], down1[part])
        outer = {-1: near_up, -2: far_up, TR: near_down, TR + 1: far_down}
        return lambda i: (outer[i] if i in outer else inner(i)).astype(F32)

    rows = (
        cot_rows(centre, lambda i: cot_ref[i]),
        cot_rows(pad, lambda i: left(SG + i)),
        cot_rows(tail, lambda i: right(SG + i)),
    )
    fill_flat(flat_ref, -2, 2, *rows)
    fill_flat(flat_ref, TR - 2, TR + 2, *rows)
    shifted_copies(flat_ref, h_ref, 0, 2)
    shifted_copies(flat_ref, h_ref, place(TR - 2) - 32, 2)
    at = place(-1) - 16
    got = back_rows(h_ref, at, PART, [back2_ref[north_row], back2_ref[1], back2_ref[2]])
    hg_ref[at + 8 : at + PART - 8] = got[8:-8]
    at = place(TR - 1) - 16
    got = back_rows(h_ref, at, PART, [back2_ref[0], back2_ref[1], back2_ref[south_row]])
    hg_ref[at + 8 : at + PART - 8] = got[8:-8]

    wide = wide_ref[...]
    up, down, left, right = edge(0)

    def embed_rows(part, first, last):
        block = lambda rows, k: rows[:, k * C : (k + 1) * C]
        up_, down_ = dot(up[part], wide), dot(down[part], wide)
        first, last = dot(first, wide), dot(last, wide)
        outer = {
            -1: jnp.where(north, block(up_, 0), block(up_, 3)),
            -2: jnp.where(north, block(up_, 1), block(up_, 2)),
            TR: jnp.where(south, block(down_, 3), block(down_, 0)),
            TR + 1: jnp.where(south, block(down_, 2), block(down_, 1)),
        }
        return lambda i: outer[i] if i in outer else block(first, i) if i < 4 else block(last, i - TR + 4)

    rows = (
        embed_rows(centre, s_ref[:, :128], s_ref[:, -128:]),
        embed_rows(pad, left(0), left(SG - 1)),
        embed_rows(tail, right(0), right(SG - 1)),
    )
    clear_flat(flat_ref, 0, 8)
    fill_flat(flat_ref, -2, 1, *rows)
    fill_flat(flat_ref, TR - 1, TR + 2, *rows)
    clear_flat(flat_ref, 8 + place(TR + 2), flat_ref.shape[0])
    shifted_copies(flat_ref, x_ref, 0, 1)
    shifted_copies(flat_ref, x_ref, place(TR) - 16, 1)

    for at in (place(-1) - 16, place(TR - 1) - 16):
        got = conv_rows(x_ref, at, PART, taps(w1_ref, (0, 1, 2)))
        pre_ref[at + 8 : at + PART - 8] = got[8:-8]

    def pole_pre(at):
        got = conv_rows(x_ref, at, PITCH + 16, taps(w1_ref, (2, 1, 0)))
        pre_ref[at + 8 : at + PITCH + 8] = got[8:-8]

    @pl.when(north)
    def _():
        pole_pre(place(-1) - 16)

    @pl.when(south)
    def _():
        pole_pre(place(TR) - 16)

    flat_ref[8 + FIRST - 16 : 8 + FIRST] = jnp.zeros((16, C), F32)
    flat_ref[8 + FIRST + 9 * PART : 24 + FIRST + 9 * PART] = jnp.zeros((16, C), F32)

    def hidden_body(k, carry):
        at = pl.multiple_of(FIRST + k * PART, 16)
        pre = pre_ref[pl.ds(at, PART), :]
        flat_ref[pl.ds(at + 8, PART), :] = pre / (1.0 + jnp.exp(-pre))
        return carry

    lax.fori_loop(0, 9, hidden_body, 0)
    shifted_copies(flat_ref, h_ref, FIRST, 9)

    def field_body(k, carry):
        at = pl.multiple_of(OWN + k * WIDE * PITCH, 16)
        got = conv_rows(h_ref, at, WIDE * PITCH, taps(w2_ref, (0, 1, 2))).astype(BF16)
        for u in range(WIDE):
            field_ref[WIDE * k + u] = got[u * PITCH : u * PITCH + TC]
        return carry

    lax.fori_loop(0, TR // WIDE, field_body, 0)

    def weight_grad(src_ref, grad_t_ref, half):
        for r in range(3):
            at = OWN + (r - 1) * PITCH
            got = dot(grad_t_ref[...], src_ref[at : at + TR * PITCH]).astype(BF16)
            for s in range(3):
                to = (3 * r + s) * C
                red_ref[half, to : to + C] = got[:, s * C : (s + 1) * C]

    weight_grad(h_ref, cot_t_ref, 0)

    def grad_body(k, carry):
        at = pl.multiple_of(FIRST + k * PART, 16)
        pre = pre_ref[pl.ds(at, PART), :]
        sig = 1.0 / (1.0 + jnp.exp(-pre))
        flat_ref[pl.ds(at + 8, PART), :] = hg_ref[pl.ds(at, PART), :] * (sig * (1.0 + pre * (1.0 - sig)))
        return carry

    lax.fori_loop(0, 9, grad_body, 0)
    shifted_copies(flat_ref, h_ref, FIRST, 9)
    for i in range(TR):
        at = 8 + place(i)
        own_ref[i * PITCH : i * PITCH + TC] = flat_ref[at : at + TC].astype(BF16)
        own_ref[i * PITCH + TC : (i + 1) * PITCH] = jnp.zeros((PITCH - TC, C), BF16)
    transpose_flat(own_ref, own_t_ref)
    weight_grad(x_ref, own_t_ref, 1)


    def eg_body(k, carry):
        at = pl.multiple_of(OWN + k * WIDE * PITCH, 16)
        got = back_rows(h_ref, at, WIDE * PITCH, [back1_ref[0], back1_ref[1], back1_ref[2]])
        eg_ref[pl.ds(pl.multiple_of(k * WIDE * PITCH, 16), WIDE * PITCH), :] = got.astype(BF16)
        return carry

    lax.fori_loop(0, TR // WIDE, eg_body, 0)

    @pl.when(north)
    def _():
        got = back_rows(h_ref, OWN, PITCH, [back1_ref[2], back1_ref[1], back1_ref[2]])
        eg_ref[:PITCH] = got.astype(BF16)

    @pl.when(south)
    def _():
        got = back_rows(h_ref, place(TR - 1), PITCH, [back1_ref[0], back1_ref[1], back1_ref[0]])
        eg_ref[(TR - 1) * PITCH :] = got.astype(BF16)

    total = jnp.zeros((FEAT, C), F32)
    for g in range(TR // 4):
        s_t = s_ref[:, g * 128 : (g + 1) * 128].T
        for k in range(4):
            i = 4 * g + k
            total += dot(s_t[k * FEAT : (k + 1) * FEAT], eg_ref[i * PITCH : i * PITCH + TC])
    red_ref[0, 9 * C :] = jnp.zeros((FEAT, C), BF16)
    red_ref[1, 9 * C :] = total.astype(BF16)


def main(where, cot, s, halo, wide, w_first, w_second, back1, back2, cot_t, hg, x, pre):
    vmem = pl.BlockSpec(memory_space=pltpu.VMEM)
    return pl.pallas_call(
        main_kernel,
        in_specs=[pl.BlockSpec(memory_space=pltpu.SMEM)] + [vmem] * 15,
        out_specs=[vmem] * 5,
        out_shape=[
            jax.ShapeDtypeStruct((TR, TC, C), BF16),
            jax.ShapeDtypeStruct((2, HALF, C), BF16),
            jax.ShapeDtypeStruct(hg.shape, hg.dtype),
            jax.ShapeDtypeStruct(x.shape, x.dtype),
            jax.ShapeDtypeStruct(pre.shape, pre.dtype),
        ],
        input_output_aliases={13: 2, 14: 3, 15: 4},
        scratch_shapes=[
            pltpu.VMEM((LEN + 16, C), F32),
            pltpu.VMEM((LEN, 3 * C), BF16),
            pltpu.VMEM((TR * PITCH, C), BF16),
            pltpu.VMEM((C, TR * PITCH), BF16),
            pltpu.VMEM((TR * PITCH, C), BF16),
        ],
        compiler_params=pltpu.CompilerParams(vmem_limit_bytes=32 << 20),
        cost_estimate=pl.CostEstimate(flops=8 << 30, bytes_accessed=6 << 20, transcendentals=1 << 20),
        name="main",
    )(where, cot, s, *halo, wide, w_first, w_second, back1, back2, cot_t, hg, x, pre)


def unpack_kernel(where_ref, own_ref, other_ref, embed_ref, first_ref, second_ref):
    first_core = where_ref[1] % 2 == 0

    def half(k, at, rows):
        own, other = own_ref[at : at + rows], other_ref[at : at + rows]
        return jnp.where(first_core, own, other) if k == 0 else jnp.where(first_core, other, own)

    for r in range(3):
        for s in range(3):
            at = (3 * r + s) * C
            first_ref[r, s] = half(1, at, C).T.astype(F32)
            second_ref[r, s] = half(0, at, C).T.astype(F32)
    embed_ref[...] = half(1, 9 * C, FEAT)[: embed_ref.shape[0]].astype(F32)


def unpack(where, own, other, values):
    vmem = pl.BlockSpec(memory_space=pltpu.VMEM)
    return pl.pallas_call(
        unpack_kernel,
        in_specs=[pl.BlockSpec(memory_space=pltpu.SMEM), vmem, vmem],
        out_specs=[vmem] * 3,
        out_shape=[
            jax.ShapeDtypeStruct((values, C), F32),
            jax.ShapeDtypeStruct((3, 3, C, C), F32),
            jax.ShapeDtypeStruct((3, 3, C, C), F32),
        ],
        compiler_params=pltpu.CompilerParams(vmem_limit_bytes=16 << 20),
        name="unpack",
    )(where, own, other)


def swaps(bands, sectors):
    number = lambda lat, lon: lat * sectors + lon % sectors

    def across(lat, lon):
        if lat % 2:
            return number(lat + 1, lon) if lat < bands - 1 else number(lat, lon + sectors // 2)
        return number(lat - 1, lon) if lat > 0 else number(lat, lon + sectors // 2)

    def swap(of):
        pairs = [(number(i, j), of(i, j)) for i in range(bands) for j in range(sectors)]
        return lambda x: lax.ppermute(x, ALL, pairs)

    return (
        swap(lambda i, j: number(i, j ^ 1)),
        swap(lambda i, j: number(i, j + 1 if j % 2 else j - 1)),
        swap(lambda i, j: number(i ^ 1, j)),
        swap(across),
    )


def per_device(obs_values, tile_ids, obs_rows, obs_cols, w_embed, w_first, w_second, cotangent):
    bands, sectors = lax.axis_size("lat"), lax.axis_size("lon")
    owners = bands * sectors
    count, values = obs_values.shape
    where = jnp.stack(
        [lax.axis_index("lat"), lax.axis_index("lon"), jnp.int32(bands), jnp.int32(sectors)]
    ).astype(jnp.int32)
    swap_a, swap_b, swap_c, swap_d = swaps(bands, sectors)
    packed = pack(tile_ids.T, obs_rows.reshape(1, count), obs_cols.reshape(1, count), obs_values.T)
    got = lax.all_to_all(packed, ALL, 0, 0, tiled=True)
    cot_t, wide, back1, back2 = prep(cotangent, w_embed, w_first, w_second)
    s, a, b = setconv(where, got, cotangent)
    a, b = swap_a(a), swap_b(b)
    c, d = join(where, a, b, s, cotangent)
    hg, x, pre = mid(where, cotangent, s, a, b, back2, wide, w_first)
    halo = (a, b, swap_c(c), swap_d(d))
    field, red, _, _, _ = main(where, cotangent, s, halo, wide, w_first, w_second, back1, back2, cot_t, hg, x, pre)

    chips = owners // 2
    groups = [[2 * k + core for k in range(chips)] for core in range(2)]
    mine = lax.axis_index("lon") % 2
    theirs = swap_a(red)
    half = red[mine].astype(F32) + theirs[mine].astype(F32)
    half = jnp.pad(half.astype(BF16), ((0, chips * RED - HALF), (0, 0))).reshape(chips, RED, C)
    parts = lax.all_to_all(half, ALL, 0, 0, axis_index_groups=groups, tiled=True)
    summed = jnp.sum(parts.astype(F32), axis=0).astype(BF16)
    spread = jnp.broadcast_to(summed[None], (chips, RED, C))
    own = lax.all_to_all(spread, ALL, 0, 0, axis_index_groups=groups, tiled=True).reshape(chips * RED, C)
    other = swap_a(own)
    grad_embed, grad_first, grad_second = unpack(where, own, other, values)
    return (field, grad_embed, grad_first, grad_second)


def solution(mesh):
    in_specs = (
        P(ALL, None),
        P(ALL, None),
        P(ALL),
        P(ALL),
        P(),
        P(),
        P(),
        P("lat", "lon", None),
    )
    out_specs = (P("lat", "lon", None), P(), P(), P())
    return jax.shard_map(
        per_device, mesh=mesh, in_specs=in_specs, out_specs=out_specs, check_vma=False
    )
```

```python
import functools
import math
import jax
import jax.numpy as jnp
from jax import lax
from jax.experimental import pallas as pl
from jax.experimental.pallas import tpu as pltpu
from jax.sharding import PartitionSpec as P

F32 = jnp.float32
BF16 = jnp.bfloat16
spread_cells = 1.0
ALL = ("lat", "lon")

TR, TC, C = 16, 128, 128
PITCH = TC + 16
LEN = 3040
PART = 304
FIRST = PITCH
OWN = 16 + 2 * PITCH
FEAT = 32
SENT = 28
RED = 24
HALF = 9 * C + FEAT
SG = TR * FEAT // 128
WIDE = 8


def dot(a, b):
    return jnp.dot(a, b, preferred_element_type=F32)


def dot_nt(a, b):
    return lax.dot_general(a, b, (((1,), (1,)), ((), ())), preferred_element_type=F32)


def place(i):
    return 16 + (i + 2) * PITCH


def pack_kernel(ids_hbm, rows_hbm, cols_hbm, vals_hbm, out_ref,
                ids_ref, rows_ref, cols_ref, vals_ref, q_ref, v_ref, pair_ref, even_ref, odd_ref, sems):
    step = pl.program_id(0)
    count = ids_ref.shape[1]
    owners = out_ref.shape[0] * pl.num_programs(0)
    sub = 256
    part = 2048
    pairs = out_ref.shape[0] // 2

    @pl.when(step == 0)
    def _():
        moves = [
            pltpu.make_async_copy(a, b, sems.at[k])
            for k, (a, b) in enumerate(
                [(ids_hbm, ids_ref), (rows_hbm, rows_ref), (cols_hbm, cols_ref), (vals_hbm, vals_ref)]
            )
        ]
        for move in moves:
            move.start()
        owner = lax.broadcasted_iota(jnp.int32, (owners, sub), 0)
        slot = lax.broadcasted_iota(jnp.int32, (sub, sub), 0)
        upto = slot <= lax.broadcasted_iota(jnp.int32, (sub, sub), 1)
        upto = jnp.concatenate(
            [jnp.where(upto, 1.0, 0.0).astype(BF16), jnp.ones((sub, 128), BF16)], axis=1
        )
        slot = slot.astype(F32).astype(BF16)
        one, none = jnp.ones((sub, sub), BF16), jnp.zeros((sub, sub), BF16)

        def rows_of_16(row, rows):
            return jnp.concatenate([jnp.broadcast_to(row, (16, sub)).astype(BF16)] * (rows // 16), axis=0)

        for move in moves:
            move.wait()

        def body(k, carry):
            for u in range(4):
                at = pl.ds(pl.multiple_of(k * 4 * sub + u * sub, sub), sub)
                ids = ids_ref[:, at]
                hot = owner == ids
                counted = dot(jnp.where(hot, 1.0, 0.0).astype(BF16), upto)
                before = counted[:, :sub] + jnp.concatenate([carry, carry], axis=1)
                rank = jnp.sum(jnp.where(hot, before, 0.0), axis=0, keepdims=True) - 1.0
                key = rank + ((ids & 1) * 128).astype(F32)
                q_ref[:, at] = jnp.where(slot == rows_of_16(key, sub), one, none)
                pair_ref[:, at] = rows_of_16((ids >> 1).astype(F32), pairs)
                rows, cols = rows_ref[:, at], cols_ref[:, at]
                rows_hi, cols_hi = rows.astype(BF16).astype(F32), cols.astype(BF16).astype(F32)
                tail = jnp.concatenate(
                    [rows_hi, rows - rows_hi, cols_hi, cols - cols_hi, jnp.zeros((4, sub), F32)], axis=0
                )
                v_ref[:, at] = jnp.concatenate([vals_ref[:, at].astype(F32), tail], axis=0)
                carry = carry + counted[:, sub:]
            return carry

        lax.fori_loop(0, count // sub // 4, body, jnp.zeros((owners, 128), F32))

    wanted = lax.broadcasted_iota(jnp.int32, (pairs, part), 0) + step * pairs
    wanted = wanted.astype(F32).astype(BF16)
    none = jnp.zeros((pairs, part), BF16)
    for k in range(count // part):
        at = pl.ds(k * part, part)
        mine = pair_ref[:, at] == wanted
        left = jnp.concatenate(
            [
                jnp.where(mine, jnp.broadcast_to(v_ref[f : f + 1, at], (pairs, part)).astype(BF16), none)
                for f in range(SENT)
            ],
            axis=0,
        )
        term = dot_nt(left, q_ref[:, at])
        for half, acc in enumerate((even_ref, odd_ref)):
            piece = term[:, half * 128 : (half + 1) * 128]
            if k == 0:
                acc[...] = piece
            else:
                acc[...] += piece
    rest = jnp.zeros((FEAT - SENT, 128), F32)
    for p in range(pairs):
        for half, acc in enumerate((even_ref, odd_ref)):
            got = jnp.concatenate([acc[pl.ds(p, SENT, stride=pairs), :], rest], axis=0)
            out_ref[2 * p + half] = got.astype(BF16)


def pack(ids, rows, cols, values):
    count = ids.shape[1]
    owners = 128
    steps = 4
    return pl.pallas_call(
        pack_kernel,
        grid=(steps,),
        in_specs=[pl.BlockSpec(memory_space=pl.ANY)] * 4,
        out_specs=pl.BlockSpec((owners // steps, FEAT, 128), lambda i: (i, 0, 0)),
        out_shape=jax.ShapeDtypeStruct((owners, FEAT, 128), BF16),
        scratch_shapes=[
            pltpu.VMEM(ids.shape, ids.dtype),
            pltpu.VMEM(rows.shape, rows.dtype),
            pltpu.VMEM(cols.shape, cols.dtype),
            pltpu.VMEM(values.shape, values.dtype),
            pltpu.VMEM((256, count), BF16),
            pltpu.VMEM((FEAT, count), F32),
            pltpu.VMEM((owners // steps // 2, count), BF16),
            pltpu.VMEM((owners // steps // 2 * SENT, 128), F32),
            pltpu.VMEM((owners // steps // 2 * SENT, 128), F32),
            pltpu.SemaphoreType.DMA((4,)),
        ],
        compiler_params=pltpu.CompilerParams(vmem_limit_bytes=58 << 20),
        cost_estimate=pl.CostEstimate(flops=2 * 2048 * 256 * 8192, bytes_accessed=3 << 20, transcendentals=0),
        name="pack",
    )(ids, rows, cols, values)


def setconv_kernel(where_ref, got_ref, cot_ref, s_ref, a_ref, b_ref, acc_ref):
    step = pl.program_id(0)
    x = jnp.concatenate([got_ref[k] for k in range(got_ref.shape[0])], axis=1).astype(F32)
    n = x.shape[1]
    alpha = math.sqrt(0.5 / math.log(2.0)) / spread_cells
    row = (x[24:25] + x[25:26]) * alpha
    col = (x[26:27] + x[27:28]) * alpha
    row_mid = (lax.broadcasted_iota(jnp.int32, (TR, n), 0).astype(F32) + 0.5) * alpha
    col_mid = (lax.broadcasted_iota(jnp.int32, (TC, n), 0).astype(F32) + 0.5) * alpha
    row_weight = jnp.exp2(-jnp.square(row - row_mid))
    col_weight = jnp.exp2(-jnp.square(col - col_mid)).astype(BF16)
    values = x[:24]
    weighted = jnp.concatenate([values * row_weight[i : i + 1] for i in range(TR)], axis=0).astype(BF16)
    term = dot_nt(weighted, col_weight)

    @pl.when(step == 0)
    def _():
        acc_ref[...] = term

    @pl.when(step > 0)
    def _():
        acc_ref[...] += term

    @pl.when(step == pl.num_programs(0) - 1)
    def _():
        none = jnp.zeros((FEAT - 24, TC), F32)
        for g in range(TR // 4):
            rows = []
            for i in range(4 * g, 4 * g + 4):
                rows += [acc_ref[24 * i : 24 * i + 24], none]
            s_ref[:, g * 128 : (g + 1) * 128] = jnp.concatenate(rows, axis=0).T.astype(BF16)
        even_lon, _ = evens(where_ref)
        for g in range(SG):
            left, right = s_ref[:16, g * 128 : (g + 1) * 128], s_ref[TC - 16 :, g * 128 : (g + 1) * 128]
            a_ref[g] = jnp.where(even_lon, right, left)
            b_ref[g] = jnp.where(even_lon, left, right)
        left, right = cot_ref[:, :16, :], cot_ref[:, TC - 16 :, :]
        a_ref[SG:] = jnp.where(even_lon, right, left)
        b_ref[SG:] = jnp.where(even_lon, left, right)


def setconv(where, got, cot):
    steps = 4
    fixed = lambda *shape: pl.BlockSpec(shape, lambda i: (0,) * len(shape))
    lanes = TR * FEAT
    shapes = [(TC, lanes), (SG + TR, 16, C), (SG + TR, 16, C)]
    return pl.pallas_call(
        setconv_kernel,
        grid=(steps,),
        in_specs=[
            pl.BlockSpec(memory_space=pltpu.SMEM),
            pl.BlockSpec((got.shape[0] // steps, FEAT, 128), lambda i: (i, 0, 0)),
            fixed(*cot.shape),
        ],
        out_specs=[fixed(*s) for s in shapes],
        out_shape=[jax.ShapeDtypeStruct(s, BF16) for s in shapes],
        scratch_shapes=[pltpu.VMEM((TR * 24, TC), F32)],
        compiler_params=pltpu.CompilerParams(vmem_limit_bytes=16 << 20),
        cost_estimate=pl.CostEstimate(
            flops=2 * 384 * 256 * 16384, bytes_accessed=2 << 20, transcendentals=144 * 16384
        ),
        name="setconv",
    )(where, got, cot)


def join_kernel(where_ref, a_ref, b_ref, s_ref, cot_ref, c_out, d_out):
    even_lon, even_lat = evens(where_ref)
    right = jnp.where(even_lon, a_ref[...], b_ref[...])
    left = jnp.where(even_lon, b_ref[...], a_ref[...])
    centre = slice(16, 16 + TC)
    for out, first in ((c_out, ~even_lat), (d_out, even_lat)):
        out[0, :16] = jnp.where(first, left[0], left[SG - 1])
        out[0, centre] = jnp.where(first, s_ref[:, :128], s_ref[:, -128:])
        out[0, 16 + TC :] = jnp.where(first, right[0], right[SG - 1])
        out[1:, :16] = jnp.where(first, left[SG : SG + 2], left[-2:])
        out[1:, centre] = jnp.where(first, cot_ref[:2], cot_ref[TR - 2 :])
        out[1:, 16 + TC :] = jnp.where(first, right[SG : SG + 2], right[-2:])


def join(where, a, b, s, cot):
    vmem = pl.BlockSpec(memory_space=pltpu.VMEM)
    return pl.pallas_call(
        join_kernel,
        in_specs=[pl.BlockSpec(memory_space=pltpu.SMEM)] + [vmem] * 4,
        out_specs=[vmem] * 2,
        out_shape=[jax.ShapeDtypeStruct((3, TC + 32, C), BF16)] * 2,
        cost_estimate=pl.CostEstimate(flops=0, bytes_accessed=1 << 18, transcendentals=0),
        compiler_params=pltpu.CompilerParams(vmem_limit_bytes=8 << 20),
        name="join",
    )(where, a, b, s, cot)


def shifted_copies(flat_ref, out_ref, begin, parts):
    def body(k, carry):
        at = pl.multiple_of(begin + k * PART, 16)
        for s in range(3):
            out_ref[pl.ds(at, PART), s * C : (s + 1) * C] = flat_ref[pl.ds(at + 7 + s, PART), :].astype(BF16)
        return carry

    lax.fori_loop(0, parts, body, 0)


def three_rows(src_ref, at, rows):
    return jnp.concatenate(
        [src_ref[pl.ds(at + (r - 1) * PITCH, rows), :] for r in range(3)], axis=1
    )


def conv_rows(src_ref, at, rows, weights):
    return dot(three_rows(src_ref, at, rows), jnp.concatenate(weights, axis=0))


def back_rows(src_ref, at, rows, weights):
    return dot_nt(three_rows(src_ref, at, rows), jnp.concatenate(weights, axis=1))


def fill_flat(flat_ref, begin, end, centre, left, right):
    first = lax.broadcasted_iota(jnp.int32, (16, C), 0) < 8
    flat_ref[place(begin) - 8 : place(begin) + 8] = left(begin)
    for i in range(begin, end):
        at = 8 + place(i)
        flat_ref[at : at + TC] = centre(i)
        after = jnp.where(first, right(i), left(i + 1)) if i < end - 1 else right(i)
        flat_ref[at + TC : at + PITCH] = after


def clear_flat(flat_ref, begin, end):
    flat_ref[begin:end] = jnp.zeros((end - begin, C), F32)


def evens(where_ref):
    return where_ref[1] % 2 == 0, where_ref[0] % 2 == 0


def arrange_back(w_ref, out_ref):
    for r in range(3):
        for s in range(3):
            out_ref[r, :, s * C : (s + 1) * C] = w_ref[2 - r, 2 - s]


def prep_kernel(cot_ref, embed_ref, w1_ref, w2_ref, cot_t_ref, wide_ref, back1_ref, back2_ref, own_ref):
    for i in range(TR):
        own_ref[i * PITCH : i * PITCH + TC] = cot_ref[i]
        own_ref[i * PITCH + TC : (i + 1) * PITCH] = jnp.zeros((PITCH - TC, C), BF16)
    transpose_flat(own_ref, cot_t_ref)
    values = embed_ref.shape[0]
    padded = jnp.concatenate([embed_ref[...].astype(F32), jnp.zeros((FEAT - values, C), F32)], axis=0).astype(BF16)
    wide_ref[...] = jnp.zeros_like(wide_ref)
    for k in range(4):
        wide_ref[k * FEAT : (k + 1) * FEAT, k * C : (k + 1) * C] = padded
    arrange_back(w1_ref, back1_ref)
    arrange_back(w2_ref, back2_ref)


def prep(cot, w_embed, w_first, w_second):
    vmem = pl.BlockSpec(memory_space=pltpu.VMEM)
    return pl.pallas_call(
        prep_kernel,
        in_specs=[vmem] * 4,
        out_specs=[vmem] * 4,
        out_shape=[
            jax.ShapeDtypeStruct((C, TR * PITCH), BF16),
            jax.ShapeDtypeStruct((4 * FEAT, 4 * C), BF16),
            jax.ShapeDtypeStruct((3, C, 3 * C), BF16),
            jax.ShapeDtypeStruct((3, C, 3 * C), BF16),
        ],
        scratch_shapes=[pltpu.VMEM((TR * PITCH, C), BF16)],
        compiler_params=pltpu.CompilerParams(vmem_limit_bytes=16 << 20),
        cost_estimate=pl.CostEstimate(flops=1 << 20, bytes_accessed=4 << 20, transcendentals=0),
        name="prep",
    )(cot, w_embed, w_first, w_second)


def mid_kernel(where_ref, cot_ref, s_ref, a_ref, b_ref, back_ref, wide_ref, w1_ref,
               hg_ref, x_ref, pre_ref, flat_ref, copies_ref):
    even_lon, _ = evens(where_ref)
    left = jnp.where(even_lon, b_ref[SG:], a_ref[SG:])
    right = jnp.where(even_lon, a_ref[SG:], b_ref[SG:])
    row = lambda rows: lambda i: rows[i].astype(F32)
    clear_flat(flat_ref, 0, place(0) - 8)
    clear_flat(flat_ref, 8 + place(TR), flat_ref.shape[0])
    fill_flat(flat_ref, 0, TR, row(cot_ref), row(left), row(right))
    shifted_copies(flat_ref, copies_ref, 0, LEN // PART)

    def body(k, carry):
        at = pl.multiple_of(FIRST + k * 3 * PART, 16)
        hg_ref[pl.ds(at, 3 * PART), :] = back_rows(copies_ref, at, 3 * PART, [back_ref[0], back_ref[1], back_ref[2]])
        return carry

    lax.fori_loop(0, 3, body, 0)

    wide = wide_ref[...]

    def rows_of(groups):
        groups = [dot(group, wide) for group in groups]
        return lambda i: groups[i // 4][:, i % 4 * C : (i % 4 + 1) * C]

    centre = rows_of([s_ref[:, g * 128 : (g + 1) * 128] for g in range(SG)])
    left = rows_of([jnp.where(even_lon, b_ref[g], a_ref[g]) for g in range(SG)])
    right = rows_of([jnp.where(even_lon, a_ref[g], b_ref[g]) for g in range(SG)])
    fill_flat(flat_ref, 0, TR, centre, left, right)
    shifted_copies(flat_ref, x_ref, 0, LEN // PART)

    def pre_body(k, carry):
        at = pl.multiple_of(FIRST + k * 3 * PART, 16)
        pre_ref[pl.ds(at, 3 * PART), :] = conv_rows(x_ref, at, 3 * PART, taps(w1_ref, (0, 1, 2)))
        return carry

    lax.fori_loop(0, 3, pre_body, 0)


def taps(w_ref, order):
    return [w_ref[r].reshape(3 * C, C) for r in order]


def transpose_flat(own_ref, out_ref):
    out_ref[...] = own_ref[...].T


def mid(where, cot, s, a, b, back, wide, w_first):
    vmem = pl.BlockSpec(memory_space=pltpu.VMEM)
    return pl.pallas_call(
        mid_kernel,
        in_specs=[pl.BlockSpec(memory_space=pltpu.SMEM)] + [vmem] * 7,
        out_specs=[vmem] * 3,
        out_shape=[
            jax.ShapeDtypeStruct((LEN, C), F32),
            jax.ShapeDtypeStruct((LEN, 3 * C), BF16),
            jax.ShapeDtypeStruct((LEN, C), F32),
        ],
        scratch_shapes=[pltpu.VMEM((LEN + 16, C), F32), pltpu.VMEM((LEN, 3 * C), BF16)],
        compiler_params=pltpu.CompilerParams(vmem_limit_bytes=24 << 20),
        cost_estimate=pl.CostEstimate(flops=2 * 2736 * 1152 * 256, bytes_accessed=4 << 20, transcendentals=0),
        name="mid",
    )(where, cot, s, a, b, back, wide, w_first)


def main_kernel(where_ref, cot_ref, s_ref, a_ref, b_ref, c_ref, d_ref,
                wide_ref, w1_ref, w2_ref, back1_ref, back2_ref, cot_t_ref, hg_in, x_in, pre_in,
                field_ref, keep_ref, send_ref, hg_ref, x_ref, pre_ref,
                red_ref, flat_ref, h_ref, own_ref, own_t_ref, eg_ref):
    even_lon, even_lat = evens(where_ref)
    north = where_ref[0] == 0
    south = where_ref[0] == where_ref[2] - 1
    north_row, south_row = jnp.where(north, 2, 0), jnp.where(south, 0, 2)
    pad, centre, tail = slice(0, 16), slice(16, 16 + TC), slice(16 + TC, 32 + TC)

    def edge(k):
        up = jnp.where(even_lat, d_ref[k], c_ref[k])
        down = jnp.where(even_lat, c_ref[k], d_ref[k])
        left = lambda i: jnp.where(even_lon, b_ref[i], a_ref[i])
        right = lambda i: jnp.where(even_lon, a_ref[i], b_ref[i])
        return up, down, left, right

    up0, down0, left, right = edge(1)
    up1, down1, _, _ = edge(2)

    def cot_rows(part, inner):
        near_up, far_up = jnp.where(north, up0[part], up1[part]), jnp.where(north, up1[part], up0[part])
        near_down, far_down = jnp.where(south, down1[part], down0[part]), jnp.where(south, down0[part], down1[part])
        outer = {-1: near_up, -2: far_up, TR: near_down, TR + 1: far_down}
        return lambda i: (outer[i] if i in outer else inner(i)).astype(F32)

    rows = (
        cot_rows(centre, lambda i: cot_ref[i]),
        cot_rows(pad, lambda i: left(SG + i)),
        cot_rows(tail, lambda i: right(SG + i)),
    )
    fill_flat(flat_ref, -2, 2, *rows)
    fill_flat(flat_ref, TR - 2, TR + 2, *rows)
    shifted_copies(flat_ref, h_ref, 0, 2)
    shifted_copies(flat_ref, h_ref, place(TR - 2) - 32, 2)
    at = place(-1) - 16
    got = back_rows(h_ref, at, PART, [back2_ref[north_row], back2_ref[1], back2_ref[2]])
    hg_ref[at + 8 : at + PART - 8] = got[8:-8]
    at = place(TR - 1) - 16
    got = back_rows(h_ref, at, PART, [back2_ref[0], back2_ref[1], back2_ref[south_row]])
    hg_ref[at + 8 : at + PART - 8] = got[8:-8]

    wide = wide_ref[...]
    up, down, left, right = edge(0)

    def embed_rows(part, first, last):
        block = lambda rows, k: rows[:, k * C : (k + 1) * C]
        up_, down_ = dot(up[part], wide), dot(down[part], wide)
        first, last = dot(first, wide), dot(last, wide)
        outer = {
            -1: jnp.where(north, block(up_, 0), block(up_, 3)),
            -2: jnp.where(north, block(up_, 1), block(up_, 2)),
            TR: jnp.where(south, block(down_, 3), block(down_, 0)),
            TR + 1: jnp.where(south, block(down_, 2), block(down_, 1)),
        }
        return lambda i: outer[i] if i in outer else block(first, i) if i < 4 else block(last, i - TR + 4)

    rows = (
        embed_rows(centre, s_ref[:, :128], s_ref[:, -128:]),
        embed_rows(pad, left(0), left(SG - 1)),
        embed_rows(tail, right(0), right(SG - 1)),
    )
    clear_flat(flat_ref, 0, 8)
    fill_flat(flat_ref, -2, 1, *rows)
    fill_flat(flat_ref, TR - 1, TR + 2, *rows)
    clear_flat(flat_ref, 8 + place(TR + 2), flat_ref.shape[0])
    shifted_copies(flat_ref, x_ref, 0, 1)
    shifted_copies(flat_ref, x_ref, place(TR) - 16, 1)

    for at in (place(-1) - 16, place(TR - 1) - 16):
        got = conv_rows(x_ref, at, PART, taps(w1_ref, (0, 1, 2)))
        pre_ref[at + 8 : at + PART - 8] = got[8:-8]

    def pole_pre(at):
        got = conv_rows(x_ref, at, PITCH + 16, taps(w1_ref, (2, 1, 0)))
        pre_ref[at + 8 : at + PITCH + 8] = got[8:-8]

    @pl.when(north)
    def _():
        pole_pre(place(-1) - 16)

    @pl.when(south)
    def _():
        pole_pre(place(TR) - 16)

    flat_ref[8 + FIRST - 16 : 8 + FIRST] = jnp.zeros((16, C), F32)
    flat_ref[8 + FIRST + 9 * PART : 24 + FIRST + 9 * PART] = jnp.zeros((16, C), F32)

    def hidden_body(k, carry):
        at = pl.multiple_of(FIRST + k * PART, 16)
        pre = pre_ref[pl.ds(at, PART), :]
        flat_ref[pl.ds(at + 8, PART), :] = pre / (1.0 + jnp.exp(-pre))
        return carry

    lax.fori_loop(0, 9, hidden_body, 0)
    shifted_copies(flat_ref, h_ref, FIRST, 9)

    def field_body(k, carry):
        at = pl.multiple_of(OWN + k * WIDE * PITCH, 16)
        got = conv_rows(h_ref, at, WIDE * PITCH, taps(w2_ref, (0, 1, 2))).astype(BF16)
        for u in range(WIDE):
            field_ref[WIDE * k + u] = got[u * PITCH : u * PITCH + TC]
        return carry

    lax.fori_loop(0, TR // WIDE, field_body, 0)

    def weight_grad(src_ref, grad_t_ref, half):
        for r in range(3):
            at = OWN + (r - 1) * PITCH
            got = dot(grad_t_ref[...], src_ref[at : at + TR * PITCH]).astype(BF16)
            for s in range(3):
                to = (3 * r + s) * C
                red_ref[half, to : to + C] = got[:, s * C : (s + 1) * C]

    weight_grad(h_ref, cot_t_ref, 0)

    def grad_body(k, carry):
        at = pl.multiple_of(FIRST + k * PART, 16)
        pre = pre_ref[pl.ds(at, PART), :]
        sig = 1.0 / (1.0 + jnp.exp(-pre))
        flat_ref[pl.ds(at + 8, PART), :] = hg_ref[pl.ds(at, PART), :] * (sig * (1.0 + pre * (1.0 - sig)))
        return carry

    lax.fori_loop(0, 9, grad_body, 0)
    shifted_copies(flat_ref, h_ref, FIRST, 9)
    for i in range(TR):
        at = 8 + place(i)
        own_ref[i * PITCH : i * PITCH + TC] = flat_ref[at : at + TC].astype(BF16)
        own_ref[i * PITCH + TC : (i + 1) * PITCH] = jnp.zeros((PITCH - TC, C), BF16)
    transpose_flat(own_ref, own_t_ref)
    weight_grad(x_ref, own_t_ref, 1)


    def eg_body(k, carry):
        at = pl.multiple_of(OWN + k * WIDE * PITCH, 16)
        got = back_rows(h_ref, at, WIDE * PITCH, [back1_ref[0], back1_ref[1], back1_ref[2]])
        eg_ref[pl.ds(pl.multiple_of(k * WIDE * PITCH, 16), WIDE * PITCH), :] = got.astype(BF16)
        return carry

    lax.fori_loop(0, TR // WIDE, eg_body, 0)

    @pl.when(north)
    def _():
        got = back_rows(h_ref, OWN, PITCH, [back1_ref[2], back1_ref[1], back1_ref[2]])
        eg_ref[:PITCH] = got.astype(BF16)

    @pl.when(south)
    def _():
        got = back_rows(h_ref, place(TR - 1), PITCH, [back1_ref[0], back1_ref[1], back1_ref[0]])
        eg_ref[(TR - 1) * PITCH :] = got.astype(BF16)

    total = jnp.zeros((FEAT, C), F32)
    for g in range(TR // 4):
        s_t = s_ref[:, g * 128 : (g + 1) * 128].T
        for k in range(4):
            i = 4 * g + k
            total += dot(s_t[k * FEAT : (k + 1) * FEAT], eg_ref[i * PITCH : i * PITCH + TC])
    red_ref[0, 9 * C :] = jnp.zeros((FEAT, C), BF16)
    red_ref[1, 9 * C :] = total.astype(BF16)
    core = where_ref[1] % 2
    keep_ref[...] = red_ref[core]
    send_ref[...] = red_ref[1 - core]


def main(where, cot, s, halo, wide, w_first, w_second, back1, back2, cot_t, hg, x, pre):
    vmem = pl.BlockSpec(memory_space=pltpu.VMEM)
    return pl.pallas_call(
        main_kernel,
        in_specs=[pl.BlockSpec(memory_space=pltpu.SMEM)] + [vmem] * 15,
        out_specs=[vmem] * 6,
        out_shape=[
            jax.ShapeDtypeStruct((TR, TC, C), BF16),
            jax.ShapeDtypeStruct((HALF, C), BF16),
            jax.ShapeDtypeStruct((HALF, C), BF16),
            jax.ShapeDtypeStruct(hg.shape, hg.dtype),
            jax.ShapeDtypeStruct(x.shape, x.dtype),
            jax.ShapeDtypeStruct(pre.shape, pre.dtype),
        ],
        input_output_aliases={13: 3, 14: 4, 15: 5},
        scratch_shapes=[
            pltpu.VMEM((2, HALF, C), BF16),
            pltpu.VMEM((LEN + 16, C), F32),
            pltpu.VMEM((LEN, 3 * C), BF16),
            pltpu.VMEM((TR * PITCH, C), BF16),
            pltpu.VMEM((C, TR * PITCH), BF16),
            pltpu.VMEM((TR * PITCH, C), BF16),
        ],
        compiler_params=pltpu.CompilerParams(vmem_limit_bytes=32 << 20),
        cost_estimate=pl.CostEstimate(flops=8 << 30, bytes_accessed=6 << 20, transcendentals=1 << 20),
        name="main",
    )(where, cot, s, *halo, wide, w_first, w_second, back1, back2, cot_t, hg, x, pre)


def unpack_kernel(where_ref, own_ref, other_ref, embed_ref, first_ref, second_ref):
    first_core = where_ref[1] % 2 == 0

    def half(k, at, rows):
        own, other = own_ref[at : at + rows], other_ref[at : at + rows]
        return jnp.where(first_core, own, other) if k == 0 else jnp.where(first_core, other, own)

    for r in range(3):
        for s in range(3):
            at = (3 * r + s) * C
            first_ref[r, s] = half(1, at, C).T.astype(F32)
            second_ref[r, s] = half(0, at, C).T.astype(F32)
    embed_ref[...] = half(1, 9 * C, FEAT)[: embed_ref.shape[0]].astype(F32)


def unpack(where, own, other, values):
    vmem = pl.BlockSpec(memory_space=pltpu.VMEM)
    return pl.pallas_call(
        unpack_kernel,
        in_specs=[pl.BlockSpec(memory_space=pltpu.SMEM), vmem, vmem],
        out_specs=[vmem] * 3,
        out_shape=[
            jax.ShapeDtypeStruct((values, C), F32),
            jax.ShapeDtypeStruct((3, 3, C, C), F32),
            jax.ShapeDtypeStruct((3, 3, C, C), F32),
        ],
        compiler_params=pltpu.CompilerParams(vmem_limit_bytes=16 << 20),
        name="unpack",
    )(where, own, other)


def swaps(bands, sectors):
    number = lambda lat, lon: lat * sectors + lon % sectors

    def across(lat, lon):
        if lat % 2:
            return number(lat + 1, lon) if lat < bands - 1 else number(lat, lon + sectors // 2)
        return number(lat - 1, lon) if lat > 0 else number(lat, lon + sectors // 2)

    def swap(of):
        pairs = [(number(i, j), of(i, j)) for i in range(bands) for j in range(sectors)]
        return lambda x: lax.ppermute(x, ALL, pairs)

    return (
        swap(lambda i, j: number(i, j ^ 1)),
        swap(lambda i, j: number(i, j + 1 if j % 2 else j - 1)),
        swap(lambda i, j: number(i ^ 1, j)),
        swap(across),
    )


def per_device(obs_values, tile_ids, obs_rows, obs_cols, w_embed, w_first, w_second, cotangent):
    bands, sectors = lax.axis_size("lat"), lax.axis_size("lon")
    owners = bands * sectors
    count, values = obs_values.shape
    where = jnp.stack(
        [lax.axis_index("lat"), lax.axis_index("lon"), jnp.int32(bands), jnp.int32(sectors)]
    ).astype(jnp.int32)
    swap_a, swap_b, swap_c, swap_d = swaps(bands, sectors)
    packed = pack(tile_ids.T, obs_rows.reshape(1, count), obs_cols.reshape(1, count), obs_values.T)
    got = lax.all_to_all(packed, ALL, 0, 0, tiled=True)
    cot_t, wide, back1, back2 = prep(cotangent, w_embed, w_first, w_second)
    s, a, b = setconv(where, got, cotangent)
    a, b = swap_a(a), swap_b(b)
    c, d = join(where, a, b, s, cotangent)
    hg, x, pre = mid(where, cotangent, s, a, b, back2, wide, w_first)
    halo = (a, b, swap_c(c), swap_d(d))
    field, keep, send, _, _, _ = main(where, cotangent, s, halo, wide, w_first, w_second, back1, back2, cot_t, hg, x, pre)

    chips = owners // 2
    groups = [[2 * k + core for k in range(chips)] for core in range(2)]
    half = keep.astype(F32) + swap_a(send).astype(F32)
    half = jnp.pad(half.astype(BF16), ((0, chips * RED - HALF), (0, 0))).reshape(chips, RED, C)
    parts = lax.all_to_all(half, ALL, 0, 0, axis_index_groups=groups, tiled=True)
    summed = jnp.sum(parts.astype(F32), axis=0).astype(BF16)
    spread = jnp.broadcast_to(summed[None], (chips, RED, C))
    own = lax.all_to_all(spread, ALL, 0, 0, axis_index_groups=groups, tiled=True).reshape(chips * RED, C)
    other = swap_a(own)
    grad_embed, grad_first, grad_second = unpack(where, own, other, values)
    return (field, grad_embed, grad_first, grad_second)


def solution(mesh):
    in_specs = (
        P(ALL, None),
        P(ALL, None),
        P(ALL),
        P(ALL),
        P(),
        P(),
        P(),
        P("lat", "lon", None),
    )
    out_specs = (P("lat", "lon", None), P(), P(), P())
    return jax.shard_map(
        per_device, mesh=mesh, in_specs=in_specs, out_specs=out_specs, check_vma=False
    )
```

```python
import functools
import math
import jax
import jax.numpy as jnp
from jax import lax
from jax.experimental import pallas as pl
from jax.experimental.pallas import tpu as pltpu
from jax.sharding import PartitionSpec as P

F32 = jnp.float32
BF16 = jnp.bfloat16
spread_cells = 1.0
ALL = ("lat", "lon")

TR, TC, C = 16, 128, 128
PITCH = TC + 16
LEN = 3040
PART = 304
FIRST = PITCH
OWN = 16 + 2 * PITCH
FEAT = 32
SENT = 28
RED = 24
HALF = 9 * C + FEAT
SG = TR * FEAT // 128
WIDE = 8


def dot(a, b):
    return jnp.dot(a, b, preferred_element_type=F32)


def dot_nt(a, b):
    return lax.dot_general(a, b, (((1,), (1,)), ((), ())), preferred_element_type=F32)


def place(i):
    return 16 + (i + 2) * PITCH


def pack_kernel(ids_hbm, rows_hbm, cols_hbm, vals_hbm, out_ref,
                ids_ref, rows_ref, cols_ref, vals_ref, q_ref, v_ref, pair_ref, even_ref, odd_ref, sems):
    step = pl.program_id(0)
    count = ids_ref.shape[1]
    owners = out_ref.shape[0] * pl.num_programs(0)
    sub = 256
    part = 2048
    pairs = out_ref.shape[0] // 2

    @pl.when(step == 0)
    def _():
        moves = [
            pltpu.make_async_copy(a, b, sems.at[k])
            for k, (a, b) in enumerate(
                [(ids_hbm, ids_ref), (rows_hbm, rows_ref), (cols_hbm, cols_ref), (vals_hbm, vals_ref)]
            )
        ]
        for move in moves:
            move.start()
        owner = lax.broadcasted_iota(jnp.int32, (owners, sub), 0)
        slot = lax.broadcasted_iota(jnp.int32, (sub, sub), 0)
        upto = slot <= lax.broadcasted_iota(jnp.int32, (sub, sub), 1)
        upto = jnp.concatenate(
            [jnp.where(upto, 1.0, 0.0).astype(BF16), jnp.ones((sub, 128), BF16)], axis=1
        )
        slot = slot.astype(F32).astype(BF16)
        one, none = jnp.ones((sub, sub), BF16), jnp.zeros((sub, sub), BF16)

        def rows_of_16(row, rows):
            return jnp.concatenate([jnp.broadcast_to(row, (16, sub)).astype(BF16)] * (rows // 16), axis=0)

        for move in moves:
            move.wait()

        def body(k, carry):
            for u in range(8):
                at = pl.ds(pl.multiple_of(k * 8 * sub + u * sub, sub), sub)
                ids = ids_ref[:, at]
                hot = owner == ids
                counted = dot(jnp.where(hot, 1.0, 0.0).astype(BF16), upto)
                before = counted[:, :sub] + jnp.concatenate([carry, carry], axis=1)
                rank = jnp.sum(jnp.where(hot, before, 0.0), axis=0, keepdims=True) - 1.0
                key = rank + ((ids & 1) * 128).astype(F32)
                q_ref[:, at] = jnp.where(slot == rows_of_16(key, sub), one, none)
                pair_ref[:, at] = rows_of_16((ids >> 1).astype(F32), pairs)
                rows, cols = rows_ref[:, at], cols_ref[:, at]
                rows_hi, cols_hi = rows.astype(BF16).astype(F32), cols.astype(BF16).astype(F32)
                tail = jnp.concatenate(
                    [rows_hi, rows - rows_hi, cols_hi, cols - cols_hi, jnp.zeros((4, sub), F32)], axis=0
                )
                v_ref[:, at] = jnp.concatenate([vals_ref[:, at].astype(F32), tail], axis=0)
                carry = carry + counted[:, sub:]
            return carry

        lax.fori_loop(0, count // sub // 8, body, jnp.zeros((owners, 128), F32))

    wanted = lax.broadcasted_iota(jnp.int32, (pairs, part), 0) + step * pairs
    wanted = wanted.astype(F32).astype(BF16)
    none = jnp.zeros((pairs, part), BF16)
    for k in range(count // part):
        at = pl.ds(k * part, part)
        mine = pair_ref[:, at] == wanted
        left = jnp.concatenate(
            [
                jnp.where(mine, jnp.broadcast_to(v_ref[f : f + 1, at], (pairs, part)).astype(BF16), none)
                for f in range(SENT)
            ],
            axis=0,
        )
        term = dot_nt(left, q_ref[:, at])
        for half, acc in enumerate((even_ref, odd_ref)):
            piece = term[:, half * 128 : (half + 1) * 128]
            if k == 0:
                acc[...] = piece
            else:
                acc[...] += piece
    rest = jnp.zeros((FEAT - SENT, 128), F32)
    for p in range(pairs):
        for half, acc in enumerate((even_ref, odd_ref)):
            got = jnp.concatenate([acc[pl.ds(p, SENT, stride=pairs), :], rest], axis=0)
            out_ref[2 * p + half] = got.astype(BF16)


def pack(ids, rows, cols, values):
    count = ids.shape[1]
    owners = 128
    steps = 4
    return pl.pallas_call(
        pack_kernel,
        grid=(steps,),
        in_specs=[pl.BlockSpec(memory_space=pl.ANY)] * 4,
        out_specs=pl.BlockSpec((owners // steps, FEAT, 128), lambda i: (i, 0, 0)),
        out_shape=jax.ShapeDtypeStruct((owners, FEAT, 128), BF16),
        scratch_shapes=[
            pltpu.VMEM(ids.shape, ids.dtype),
            pltpu.VMEM(rows.shape, rows.dtype),
            pltpu.VMEM(cols.shape, cols.dtype),
            pltpu.VMEM(values.shape, values.dtype),
            pltpu.VMEM((256, count), BF16),
            pltpu.VMEM((FEAT, count), F32),
            pltpu.VMEM((owners // steps // 2, count), BF16),
            pltpu.VMEM((owners // steps // 2 * SENT, 128), F32),
            pltpu.VMEM((owners // steps // 2 * SENT, 128), F32),
            pltpu.SemaphoreType.DMA((4,)),
        ],
        compiler_params=pltpu.CompilerParams(vmem_limit_bytes=58 << 20),
        cost_estimate=pl.CostEstimate(flops=2 * 2048 * 256 * 8192, bytes_accessed=3 << 20, transcendentals=0),
        name="pack",
    )(ids, rows, cols, values)


def setconv_kernel(where_ref, got_ref, cot_ref, s_ref, a_ref, b_ref, acc_ref):
    step = pl.program_id(0)
    x = jnp.concatenate([got_ref[k] for k in range(got_ref.shape[0])], axis=1).astype(F32)
    n = x.shape[1]
    alpha = math.sqrt(0.5 / math.log(2.0)) / spread_cells
    row = (x[24:25] + x[25:26]) * alpha
    col = (x[26:27] + x[27:28]) * alpha
    row_mid = (lax.broadcasted_iota(jnp.int32, (TR, n), 0).astype(F32) + 0.5) * alpha
    col_mid = (lax.broadcasted_iota(jnp.int32, (TC, n), 0).astype(F32) + 0.5) * alpha
    row_weight = jnp.exp2(-jnp.square(row - row_mid))
    col_weight = jnp.exp2(-jnp.square(col - col_mid)).astype(BF16)
    values = x[:24]
    weighted = jnp.concatenate([values * row_weight[i : i + 1] for i in range(TR)], axis=0).astype(BF16)
    term = dot_nt(weighted, col_weight)

    @pl.when(step == 0)
    def _():
        acc_ref[...] = term

    @pl.when(step > 0)
    def _():
        acc_ref[...] += term

    @pl.when(step == pl.num_programs(0) - 1)
    def _():
        none = jnp.zeros((FEAT - 24, TC), F32)
        for g in range(TR // 4):
            rows = []
            for i in range(4 * g, 4 * g + 4):
                rows += [acc_ref[24 * i : 24 * i + 24], none]
            s_ref[:, g * 128 : (g + 1) * 128] = jnp.concatenate(rows, axis=0).T.astype(BF16)
        even_lon, _ = evens(where_ref)
        for g in range(SG):
            left, right = s_ref[:16, g * 128 : (g + 1) * 128], s_ref[TC - 16 :, g * 128 : (g + 1) * 128]
            a_ref[g] = jnp.where(even_lon, right, left)
            b_ref[g] = jnp.where(even_lon, left, right)
        left, right = cot_ref[:, :16, :], cot_ref[:, TC - 16 :, :]
        a_ref[SG:] = jnp.where(even_lon, right, left)
        b_ref[SG:] = jnp.where(even_lon, left, right)


def setconv(where, got, cot):
    steps = 2
    fixed = lambda *shape: pl.BlockSpec(shape, lambda i: (0,) * len(shape))
    lanes = TR * FEAT
    shapes = [(TC, lanes), (SG + TR, 16, C), (SG + TR, 16, C)]
    return pl.pallas_call(
        setconv_kernel,
        grid=(steps,),
        in_specs=[
            pl.BlockSpec(memory_space=pltpu.SMEM),
            pl.BlockSpec((got.shape[0] // steps, FEAT, 128), lambda i: (i, 0, 0)),
            fixed(*cot.shape),
        ],
        out_specs=[fixed(*s) for s in shapes],
        out_shape=[jax.ShapeDtypeStruct(s, BF16) for s in shapes],
        scratch_shapes=[pltpu.VMEM((TR * 24, TC), F32)],
        compiler_params=pltpu.CompilerParams(vmem_limit_bytes=16 << 20),
        cost_estimate=pl.CostEstimate(
            flops=2 * 384 * 256 * 16384, bytes_accessed=2 << 20, transcendentals=144 * 16384
        ),
        name="setconv",
    )(where, got, cot)


def join_kernel(where_ref, a_ref, b_ref, s_ref, cot_ref, c_out, d_out):
    even_lon, even_lat = evens(where_ref)
    right = jnp.where(even_lon, a_ref[...], b_ref[...])
    left = jnp.where(even_lon, b_ref[...], a_ref[...])
    centre = slice(16, 16 + TC)
    for out, first in ((c_out, ~even_lat), (d_out, even_lat)):
        out[0, :16] = jnp.where(first, left[0], left[SG - 1])
        out[0, centre] = jnp.where(first, s_ref[:, :128], s_ref[:, -128:])
        out[0, 16 + TC :] = jnp.where(first, right[0], right[SG - 1])
        out[1:, :16] = jnp.where(first, left[SG : SG + 2], left[-2:])
        out[1:, centre] = jnp.where(first, cot_ref[:2], cot_ref[TR - 2 :])
        out[1:, 16 + TC :] = jnp.where(first, right[SG : SG + 2], right[-2:])


def join(where, a, b, s, cot):
    vmem = pl.BlockSpec(memory_space=pltpu.VMEM)
    return pl.pallas_call(
        join_kernel,
        in_specs=[pl.BlockSpec(memory_space=pltpu.SMEM)] + [vmem] * 4,
        out_specs=[vmem] * 2,
        out_shape=[jax.ShapeDtypeStruct((3, TC + 32, C), BF16)] * 2,
        cost_estimate=pl.CostEstimate(flops=0, bytes_accessed=1 << 18, transcendentals=0),
        compiler_params=pltpu.CompilerParams(vmem_limit_bytes=8 << 20),
        name="join",
    )(where, a, b, s, cot)


def shifted_copies(flat_ref, out_ref, begin, parts):
    def body(k, carry):
        at = pl.multiple_of(begin + k * PART, 16)
        for s in range(3):
            out_ref[pl.ds(at, PART), s * C : (s + 1) * C] = flat_ref[pl.ds(at + 7 + s, PART), :].astype(BF16)
        return carry

    lax.fori_loop(0, parts, body, 0)


def three_rows(src_ref, at, rows):
    return jnp.concatenate(
        [src_ref[pl.ds(at + (r - 1) * PITCH, rows), :] for r in range(3)], axis=1
    )


def conv_rows(src_ref, at, rows, weights):
    return dot(three_rows(src_ref, at, rows), jnp.concatenate(weights, axis=0))


def back_rows(src_ref, at, rows, weights):
    return dot_nt(three_rows(src_ref, at, rows), jnp.concatenate(weights, axis=1))


def fill_flat(flat_ref, begin, end, centre, left, right):
    first = lax.broadcasted_iota(jnp.int32, (16, C), 0) < 8
    flat_ref[place(begin) - 8 : place(begin) + 8] = left(begin)
    for i in range(begin, end):
        at = 8 + place(i)
        flat_ref[at : at + TC] = centre(i)
        after = jnp.where(first, right(i), left(i + 1)) if i < end - 1 else right(i)
        flat_ref[at + TC : at + PITCH] = after


def clear_flat(flat_ref, begin, end):
    flat_ref[begin:end] = jnp.zeros((end - begin, C), F32)


def evens(where_ref):
    return where_ref[1] % 2 == 0, where_ref[0] % 2 == 0


def arrange_back(w_ref, out_ref):
    for r in range(3):
        for s in range(3):
            out_ref[r, :, s * C : (s + 1) * C] = w_ref[2 - r, 2 - s]


def prep_kernel(cot_ref, embed_ref, w1_ref, w2_ref, cot_t_ref, wide_ref, back1_ref, back2_ref, own_ref):
    for i in range(TR):
        own_ref[i * PITCH : i * PITCH + TC] = cot_ref[i]
        own_ref[i * PITCH + TC : (i + 1) * PITCH] = jnp.zeros((PITCH - TC, C), BF16)
    transpose_flat(own_ref, cot_t_ref)
    values = embed_ref.shape[0]
    padded = jnp.concatenate([embed_ref[...].astype(F32), jnp.zeros((FEAT - values, C), F32)], axis=0).astype(BF16)
    wide_ref[...] = jnp.zeros_like(wide_ref)
    for k in range(4):
        wide_ref[k * FEAT : (k + 1) * FEAT, k * C : (k + 1) * C] = padded
    arrange_back(w1_ref, back1_ref)
    arrange_back(w2_ref, back2_ref)


def prep(cot, w_embed, w_first, w_second):
    vmem = pl.BlockSpec(memory_space=pltpu.VMEM)
    return pl.pallas_call(
        prep_kernel,
        in_specs=[vmem] * 4,
        out_specs=[vmem] * 4,
        out_shape=[
            jax.ShapeDtypeStruct((C, TR * PITCH), BF16),
            jax.ShapeDtypeStruct((4 * FEAT, 4 * C), BF16),
            jax.ShapeDtypeStruct((3, C, 3 * C), BF16),
            jax.ShapeDtypeStruct((3, C, 3 * C), BF16),
        ],
        scratch_shapes=[pltpu.VMEM((TR * PITCH, C), BF16)],
        compiler_params=pltpu.CompilerParams(vmem_limit_bytes=16 << 20),
        cost_estimate=pl.CostEstimate(flops=1 << 20, bytes_accessed=4 << 20, transcendentals=0),
        name="prep",
    )(cot, w_embed, w_first, w_second)


def mid_kernel(where_ref, cot_ref, s_ref, a_ref, b_ref, back_ref, wide_ref, w1_ref,
               hg_ref, x_ref, pre_ref, flat_ref, copies_ref):
    even_lon, _ = evens(where_ref)
    left = jnp.where(even_lon, b_ref[SG:], a_ref[SG:])
    right = jnp.where(even_lon, a_ref[SG:], b_ref[SG:])
    row = lambda rows: lambda i: rows[i].astype(F32)
    clear_flat(flat_ref, 0, place(0) - 8)
    clear_flat(flat_ref, 8 + place(TR), flat_ref.shape[0])
    fill_flat(flat_ref, 0, TR, row(cot_ref), row(left), row(right))
    shifted_copies(flat_ref, copies_ref, 0, LEN // PART)

    def body(k, carry):
        at = pl.multiple_of(FIRST + k * 3 * PART, 16)
        hg_ref[pl.ds(at, 3 * PART), :] = back_rows(copies_ref, at, 3 * PART, [back_ref[0], back_ref[1], back_ref[2]])
        return carry

    lax.fori_loop(0, 3, body, 0)

    wide = wide_ref[...]

    def rows_of(groups):
        groups = [dot(group, wide) for group in groups]
        return lambda i: groups[i // 4][:, i % 4 * C : (i % 4 + 1) * C]

    centre = rows_of([s_ref[:, g * 128 : (g + 1) * 128] for g in range(SG)])
    left = rows_of([jnp.where(even_lon, b_ref[g], a_ref[g]) for g in range(SG)])
    right = rows_of([jnp.where(even_lon, a_ref[g], b_ref[g]) for g in range(SG)])
    fill_flat(flat_ref, 0, TR, centre, left, right)
    shifted_copies(flat_ref, x_ref, 0, LEN // PART)

    def pre_body(k, carry):
        at = pl.multiple_of(FIRST + k * 3 * PART, 16)
        pre_ref[pl.ds(at, 3 * PART), :] = conv_rows(x_ref, at, 3 * PART, taps(w1_ref, (0, 1, 2)))
        return carry

    lax.fori_loop(0, 3, pre_body, 0)


def taps(w_ref, order):
    return [w_ref[r].reshape(3 * C, C) for r in order]


def transpose_flat(own_ref, out_ref):
    out_ref[...] = own_ref[...].T


def mid(where, cot, s, a, b, back, wide, w_first):
    vmem = pl.BlockSpec(memory_space=pltpu.VMEM)
    return pl.pallas_call(
        mid_kernel,
        in_specs=[pl.BlockSpec(memory_space=pltpu.SMEM)] + [vmem] * 7,
        out_specs=[vmem] * 3,
        out_shape=[
            jax.ShapeDtypeStruct((LEN, C), F32),
            jax.ShapeDtypeStruct((LEN, 3 * C), BF16),
            jax.ShapeDtypeStruct((LEN, C), F32),
        ],
        scratch_shapes=[pltpu.VMEM((LEN + 16, C), F32), pltpu.VMEM((LEN, 3 * C), BF16)],
        compiler_params=pltpu.CompilerParams(vmem_limit_bytes=24 << 20),
        cost_estimate=pl.CostEstimate(flops=2 * 2736 * 1152 * 256, bytes_accessed=4 << 20, transcendentals=0),
        name="mid",
    )(where, cot, s, a, b, back, wide, w_first)


def main_kernel(where_ref, cot_ref, s_ref, a_ref, b_ref, c_ref, d_ref,
                wide_ref, w1_ref, w2_ref, back1_ref, back2_ref, cot_t_ref, hg_in, x_in, pre_in,
                field_ref, keep_ref, send_ref, hg_ref, x_ref, pre_ref,
                red_ref, flat_ref, h_ref, own_ref, own_t_ref, eg_ref):
    even_lon, even_lat = evens(where_ref)
    north = where_ref[0] == 0
    south = where_ref[0] == where_ref[2] - 1
    north_row, south_row = jnp.where(north, 2, 0), jnp.where(south, 0, 2)
    pad, centre, tail = slice(0, 16), slice(16, 16 + TC), slice(16 + TC, 32 + TC)

    def edge(k):
        up = jnp.where(even_lat, d_ref[k], c_ref[k])
        down = jnp.where(even_lat, c_ref[k], d_ref[k])
        left = lambda i: jnp.where(even_lon, b_ref[i], a_ref[i])
        right = lambda i: jnp.where(even_lon, a_ref[i], b_ref[i])
        return up, down, left, right

    up0, down0, left, right = edge(1)
    up1, down1, _, _ = edge(2)

    def cot_rows(part, inner):
        near_up, far_up = jnp.where(north, up0[part], up1[part]), jnp.where(north, up1[part], up0[part])
        near_down, far_down = jnp.where(south, down1[part], down0[part]), jnp.where(south, down0[part], down1[part])
        outer = {-1: near_up, -2: far_up, TR: near_down, TR + 1: far_down}
        return lambda i: (outer[i] if i in outer else inner(i)).astype(F32)

    rows = (
        cot_rows(centre, lambda i: cot_ref[i]),
        cot_rows(pad, lambda i: left(SG + i)),
        cot_rows(tail, lambda i: right(SG + i)),
    )
    fill_flat(flat_ref, -2, 2, *rows)
    fill_flat(flat_ref, TR - 2, TR + 2, *rows)
    shifted_copies(flat_ref, h_ref, 0, 2)
    shifted_copies(flat_ref, h_ref, place(TR - 2) - 32, 2)
    at = place(-1) - 16
    got = back_rows(h_ref, at, PART, [back2_ref[north_row], back2_ref[1], back2_ref[2]])
    hg_ref[at + 8 : at + PART - 8] = got[8:-8]
    at = place(TR - 1) - 16
    got = back_rows(h_ref, at, PART, [back2_ref[0], back2_ref[1], back2_ref[south_row]])
    hg_ref[at + 8 : at + PART - 8] = got[8:-8]

    wide = wide_ref[...]
    up, down, left, right = edge(0)

    def embed_rows(part, first, last):
        block = lambda rows, k: rows[:, k * C : (k + 1) * C]
        up_, down_ = dot(up[part], wide), dot(down[part], wide)
        first, last = dot(first, wide), dot(last, wide)
        outer = {
            -1: jnp.where(north, block(up_, 0), block(up_, 3)),
            -2: jnp.where(north, block(up_, 1), block(up_, 2)),
            TR: jnp.where(south, block(down_, 3), block(down_, 0)),
            TR + 1: jnp.where(south, block(down_, 2), block(down_, 1)),
        }
        return lambda i: outer[i] if i in outer else block(first, i) if i < 4 else block(last, i - TR + 4)

    rows = (
        embed_rows(centre, s_ref[:, :128], s_ref[:, -128:]),
        embed_rows(pad, left(0), left(SG - 1)),
        embed_rows(tail, right(0), right(SG - 1)),
    )
    clear_flat(flat_ref, 0, 8)
    fill_flat(flat_ref, -2, 1, *rows)
    fill_flat(flat_ref, TR - 1, TR + 2, *rows)
    clear_flat(flat_ref, 8 + place(TR + 2), flat_ref.shape[0])
    shifted_copies(flat_ref, x_ref, 0, 1)
    shifted_copies(flat_ref, x_ref, place(TR) - 16, 1)

    for at in (place(-1) - 16, place(TR - 1) - 16):
        got = conv_rows(x_ref, at, PART, taps(w1_ref, (0, 1, 2)))
        pre_ref[at + 8 : at + PART - 8] = got[8:-8]

    def pole_pre(at):
        got = conv_rows(x_ref, at, PITCH + 16, taps(w1_ref, (2, 1, 0)))
        pre_ref[at + 8 : at + PITCH + 8] = got[8:-8]

    @pl.when(north)
    def _():
        pole_pre(place(-1) - 16)

    @pl.when(south)
    def _():
        pole_pre(place(TR) - 16)

    flat_ref[8 + FIRST - 16 : 8 + FIRST] = jnp.zeros((16, C), F32)
    flat_ref[8 + FIRST + 9 * PART : 24 + FIRST + 9 * PART] = jnp.zeros((16, C), F32)

    def hidden_body(k, carry):
        at = pl.multiple_of(FIRST + k * PART, 16)
        pre = pre_ref[pl.ds(at, PART), :]
        flat_ref[pl.ds(at + 8, PART), :] = pre / (1.0 + jnp.exp(-pre))
        return carry

    lax.fori_loop(0, 9, hidden_body, 0)
    shifted_copies(flat_ref, h_ref, FIRST, 9)

    def field_body(k, carry):
        at = pl.multiple_of(OWN + k * WIDE * PITCH, 16)
        got = conv_rows(h_ref, at, WIDE * PITCH, taps(w2_ref, (0, 1, 2))).astype(BF16)
        for u in range(WIDE):
            field_ref[WIDE * k + u] = got[u * PITCH : u * PITCH + TC]
        return carry

    lax.fori_loop(0, TR // WIDE, field_body, 0)

    def weight_grad(src_ref, grad_t_ref, half):
        for r in range(3):
            at = OWN + (r - 1) * PITCH
            got = dot(grad_t_ref[...], src_ref[at : at + TR * PITCH]).astype(BF16)
            for s in range(3):
                to = (3 * r + s) * C
                red_ref[half, to : to + C] = got[:, s * C : (s + 1) * C]

    weight_grad(h_ref, cot_t_ref, 0)

    def grad_body(k, carry):
        at = pl.multiple_of(FIRST + k * PART, 16)
        pre = pre_ref[pl.ds(at, PART), :]
        sig = 1.0 / (1.0 + jnp.exp(-pre))
        flat_ref[pl.ds(at + 8, PART), :] = hg_ref[pl.ds(at, PART), :] * (sig * (1.0 + pre * (1.0 - sig)))
        return carry

    lax.fori_loop(0, 9, grad_body, 0)
    shifted_copies(flat_ref, h_ref, FIRST, 9)
    for i in range(TR):
        at = 8 + place(i)
        own_ref[i * PITCH : i * PITCH + TC] = flat_ref[at : at + TC].astype(BF16)
        own_ref[i * PITCH + TC : (i + 1) * PITCH] = jnp.zeros((PITCH - TC, C), BF16)
    transpose_flat(own_ref, own_t_ref)
    weight_grad(x_ref, own_t_ref, 1)


    def eg_body(k, carry):
        at = pl.multiple_of(OWN + k * WIDE * PITCH, 16)
        got = back_rows(h_ref, at, WIDE * PITCH, [back1_ref[0], back1_ref[1], back1_ref[2]])
        eg_ref[pl.ds(pl.multiple_of(k * WIDE * PITCH, 16), WIDE * PITCH), :] = got.astype(BF16)
        return carry

    lax.fori_loop(0, TR // WIDE, eg_body, 0)

    @pl.when(north)
    def _():
        got = back_rows(h_ref, OWN, PITCH, [back1_ref[2], back1_ref[1], back1_ref[2]])
        eg_ref[:PITCH] = got.astype(BF16)

    @pl.when(south)
    def _():
        got = back_rows(h_ref, place(TR - 1), PITCH, [back1_ref[0], back1_ref[1], back1_ref[0]])
        eg_ref[(TR - 1) * PITCH :] = got.astype(BF16)

    total = jnp.zeros((FEAT, C), F32)
    for g in range(TR // 4):
        s_t = s_ref[:, g * 128 : (g + 1) * 128].T
        for k in range(4):
            i = 4 * g + k
            total += dot(s_t[k * FEAT : (k + 1) * FEAT], eg_ref[i * PITCH : i * PITCH + TC])
    red_ref[0, 9 * C :] = jnp.zeros((FEAT, C), BF16)
    red_ref[1, 9 * C :] = total.astype(BF16)
    core = where_ref[1] % 2
    keep_ref[...] = red_ref[core]
    send_ref[...] = red_ref[1 - core]


def main(where, cot, s, halo, wide, w_first, w_second, back1, back2, cot_t, hg, x, pre):
    vmem = pl.BlockSpec(memory_space=pltpu.VMEM)
    return pl.pallas_call(
        main_kernel,
        in_specs=[pl.BlockSpec(memory_space=pltpu.SMEM)] + [vmem] * 15,
        out_specs=[vmem] * 6,
        out_shape=[
            jax.ShapeDtypeStruct((TR, TC, C), BF16),
            jax.ShapeDtypeStruct((HALF, C), BF16),
            jax.ShapeDtypeStruct((HALF, C), BF16),
            jax.ShapeDtypeStruct(hg.shape, hg.dtype),
            jax.ShapeDtypeStruct(x.shape, x.dtype),
            jax.ShapeDtypeStruct(pre.shape, pre.dtype),
        ],
        input_output_aliases={13: 3, 14: 4, 15: 5},
        scratch_shapes=[
            pltpu.VMEM((2, HALF, C), BF16),
            pltpu.VMEM((LEN + 16, C), F32),
            pltpu.VMEM((LEN, 3 * C), BF16),
            pltpu.VMEM((TR * PITCH, C), BF16),
            pltpu.VMEM((C, TR * PITCH), BF16),
            pltpu.VMEM((TR * PITCH, C), BF16),
        ],
        compiler_params=pltpu.CompilerParams(vmem_limit_bytes=32 << 20),
        cost_estimate=pl.CostEstimate(flops=8 << 30, bytes_accessed=6 << 20, transcendentals=1 << 20),
        name="main",
    )(where, cot, s, *halo, wide, w_first, w_second, back1, back2, cot_t, hg, x, pre)


def turn_kernel(own_ref, out_ref):
    for k in range(9):
        out_ref[k] = own_ref[k * C : (k + 1) * C].T


def turn(own):
    vmem = pl.BlockSpec(memory_space=pltpu.VMEM)
    return pl.pallas_call(
        turn_kernel,
        in_specs=[vmem],
        out_specs=vmem,
        out_shape=jax.ShapeDtypeStruct((9, C, C), BF16),
        compiler_params=pltpu.CompilerParams(vmem_limit_bytes=8 << 20),
        cost_estimate=pl.CostEstimate(flops=1 << 20, bytes_accessed=1 << 20, transcendentals=0),
        name="turn",
    )(own)


def unpack_kernel(where_ref, own_ref, turned_ref, other_ref, embed_ref, first_ref, second_ref):
    even = where_ref[1] % 2 == 0
    for r in range(3):
        for s in range(3):
            k = 3 * r + s
            mine, other = turned_ref[k], other_ref[k * C : (k + 1) * C].T
            first_ref[r, s] = jnp.where(even, other, mine).astype(F32)
            second_ref[r, s] = jnp.where(even, mine, other).astype(F32)
    embed = jnp.where(even, other_ref[9 * C : 9 * C + FEAT], own_ref[9 * C : 9 * C + FEAT])
    embed_ref[...] = embed[: embed_ref.shape[0]].astype(F32)


def unpack(where, own, turned, other, values):
    vmem = pl.BlockSpec(memory_space=pltpu.VMEM)
    return pl.pallas_call(
        unpack_kernel,
        in_specs=[pl.BlockSpec(memory_space=pltpu.SMEM), vmem, vmem, vmem],
        out_specs=[vmem] * 3,
        out_shape=[
            jax.ShapeDtypeStruct((values, C), F32),
            jax.ShapeDtypeStruct((3, 3, C, C), F32),
            jax.ShapeDtypeStruct((3, 3, C, C), F32),
        ],
        compiler_params=pltpu.CompilerParams(vmem_limit_bytes=16 << 20),
        name="unpack",
    )(where, own, turned, other)


def swaps(bands, sectors):
    number = lambda lat, lon: lat * sectors + lon % sectors

    def across(lat, lon):
        if lat % 2:
            return number(lat + 1, lon) if lat < bands - 1 else number(lat, lon + sectors // 2)
        return number(lat - 1, lon) if lat > 0 else number(lat, lon + sectors // 2)

    def swap(of):
        pairs = [(number(i, j), of(i, j)) for i in range(bands) for j in range(sectors)]
        return lambda x: lax.ppermute(x, ALL, pairs)

    return (
        swap(lambda i, j: number(i, j ^ 1)),
        swap(lambda i, j: number(i, j + 1 if j % 2 else j - 1)),
        swap(lambda i, j: number(i ^ 1, j)),
        swap(across),
    )


def per_device(obs_values, tile_ids, obs_rows, obs_cols, w_embed, w_first, w_second, cotangent):
    bands, sectors = lax.axis_size("lat"), lax.axis_size("lon")
    owners = bands * sectors
    count, values = obs_values.shape
    where = jnp.stack(
        [lax.axis_index("lat"), lax.axis_index("lon"), jnp.int32(bands), jnp.int32(sectors)]
    ).astype(jnp.int32)
    swap_a, swap_b, swap_c, swap_d = swaps(bands, sectors)
    packed = pack(tile_ids.T, obs_rows.reshape(1, count), obs_cols.reshape(1, count), obs_values.T)
    got = lax.all_to_all(packed, ALL, 0, 0, tiled=True)
    cot_t, wide, back1, back2 = prep(cotangent, w_embed, w_first, w_second)
    s, a, b = setconv(where, got, cotangent)
    a, b = swap_a(a), swap_b(b)
    c, d = join(where, a, b, s, cotangent)
    hg, x, pre = mid(where, cotangent, s, a, b, back2, wide, w_first)
    halo = (a, b, swap_c(c), swap_d(d))
    field, keep, send, _, _, _ = main(where, cotangent, s, halo, wide, w_first, w_second, back1, back2, cot_t, hg, x, pre)

    chips = owners // 2
    groups = [[2 * k + core for k in range(chips)] for core in range(2)]
    half = keep.astype(F32) + swap_a(send).astype(F32)
    half = jnp.pad(half.astype(BF16), ((0, chips * RED - HALF), (0, 0))).reshape(chips, RED, C)
    parts = lax.all_to_all(half, ALL, 0, 0, axis_index_groups=groups, tiled=True)
    summed = jnp.sum(parts.astype(F32), axis=0).astype(BF16)
    spread = jnp.broadcast_to(summed[None], (chips, RED, C))
    own = lax.all_to_all(spread, ALL, 0, 0, axis_index_groups=groups, tiled=True).reshape(chips * RED, C)
    other = swap_a(own)
    grad_embed, grad_first, grad_second = unpack(where, own, turn(own), other, values)
    return (field, grad_embed, grad_first, grad_second)


def solution(mesh):
    in_specs = (
        P(ALL, None),
        P(ALL, None),
        P(ALL),
        P(ALL),
        P(),
        P(),
        P(),
        P("lat", "lon", None),
    )
    out_specs = (P("lat", "lon", None), P(), P(), P())
    return jax.shard_map(
        per_device, mesh=mesh, in_specs=in_specs, out_specs=out_specs, check_vma=False
    )
```

```python
import functools
import math
import jax
import jax.numpy as jnp
from jax import lax
from jax.experimental import pallas as pl
from jax.experimental.pallas import tpu as pltpu
from jax.sharding import PartitionSpec as P

F32 = jnp.float32
BF16 = jnp.bfloat16
spread_cells = 1.0
ALL = ("lat", "lon")

TR, TC, C = 16, 128, 128
PITCH = TC + 16
LEN = 3040
PART = 304
FIRST = PITCH
OWN = 16 + 2 * PITCH
FEAT = 32
SENT = 28
RED = 24
HALF = 9 * C + FEAT
SG = TR * FEAT // 128
WIDE = 8


def dot(a, b):
    return jnp.dot(a, b, preferred_element_type=F32)


def dot_nt(a, b):
    return lax.dot_general(a, b, (((1,), (1,)), ((), ())), preferred_element_type=F32)


def place(i):
    return 16 + (i + 2) * PITCH


def pack_kernel(ids_hbm, rows_hbm, cols_hbm, vals_hbm, out_ref,
                ids_ref, rows_ref, cols_ref, vals_ref, q_ref, v_ref, pair_ref, even_ref, odd_ref, sems):
    step = pl.program_id(0)
    count = ids_ref.shape[1]
    owners = out_ref.shape[0] * pl.num_programs(0)
    sub = 256
    part = 2048
    pairs = out_ref.shape[0] // 2

    @pl.when(step == 0)
    def _():
        moves = [
            pltpu.make_async_copy(a, b, sems.at[k])
            for k, (a, b) in enumerate(
                [(ids_hbm, ids_ref), (rows_hbm, rows_ref), (cols_hbm, cols_ref), (vals_hbm, vals_ref)]
            )
        ]
        for move in moves:
            move.start()
        owner = lax.broadcasted_iota(jnp.int32, (owners, sub), 0)
        slot = lax.broadcasted_iota(jnp.int32, (sub, sub), 0)
        upto = slot <= lax.broadcasted_iota(jnp.int32, (sub, sub), 1)
        upto = jnp.concatenate(
            [jnp.where(upto, 1.0, 0.0).astype(BF16), jnp.ones((sub, 128), BF16)], axis=1
        )
        slot = slot.astype(F32).astype(BF16)
        one, none = jnp.ones((sub, sub), BF16), jnp.zeros((sub, sub), BF16)

        def rows_of_16(row, rows):
            return jnp.concatenate([jnp.broadcast_to(row, (16, sub)).astype(BF16)] * (rows // 16), axis=0)

        for move in moves:
            move.wait()

        def body(k, carry):
            for u in range(8):
                at = pl.ds(pl.multiple_of(k * 8 * sub + u * sub, sub), sub)
                ids = ids_ref[:, at]
                hot = owner == ids
                counted = dot(jnp.where(hot, 1.0, 0.0).astype(BF16), upto)
                before = counted[:, :sub] + jnp.concatenate([carry, carry], axis=1)
                rank = jnp.sum(jnp.where(hot, before, 0.0), axis=0, keepdims=True) - 1.0
                key = rank + ((ids & 1) * 128).astype(F32)
                q_ref[:, at] = jnp.where(slot == rows_of_16(key, sub), one, none)
                pair_ref[:, at] = rows_of_16((ids >> 1).astype(F32), pairs)
                rows, cols = rows_ref[:, at], cols_ref[:, at]
                rows_hi, cols_hi = rows.astype(BF16).astype(F32), cols.astype(BF16).astype(F32)
                tail = jnp.concatenate(
                    [rows_hi, rows - rows_hi, cols_hi, cols - cols_hi, jnp.zeros((4, sub), F32)], axis=0
                )
                v_ref[:, at] = jnp.concatenate([vals_ref[:, at].astype(F32), tail], axis=0)
                carry = carry + counted[:, sub:]
            return carry

        lax.fori_loop(0, count // sub // 8, body, jnp.zeros((owners, 128), F32))

    wanted = lax.broadcasted_iota(jnp.int32, (pairs, part), 0) + step * pairs
    wanted = wanted.astype(F32).astype(BF16)
    none = jnp.zeros((pairs, part), BF16)
    for k in range(count // part):
        at = pl.ds(k * part, part)
        mine = pair_ref[:, at] == wanted
        left = jnp.concatenate(
            [
                jnp.where(mine, jnp.broadcast_to(v_ref[f : f + 1, at], (pairs, part)).astype(BF16), none)
                for f in range(SENT)
            ],
            axis=0,
        )
        term = dot_nt(left, q_ref[:, at])
        for half, acc in enumerate((even_ref, odd_ref)):
            piece = term[:, half * 128 : (half + 1) * 128]
            if k == 0:
                acc[...] = piece
            else:
                acc[...] += piece
    rest = jnp.zeros((FEAT - SENT, 128), F32)
    for p in range(pairs):
        for half, acc in enumerate((even_ref, odd_ref)):
            got = jnp.concatenate([acc[pl.ds(p, SENT, stride=pairs), :], rest], axis=0)
            out_ref[2 * p + half] = got.astype(BF16)


def pack(ids, rows, cols, values):
    count = ids.shape[1]
    owners = 128
    steps = 4
    return pl.pallas_call(
        pack_kernel,
        grid=(steps,),
        in_specs=[pl.BlockSpec(memory_space=pl.ANY)] * 4,
        out_specs=pl.BlockSpec((owners // steps, FEAT, 128), lambda i: (i, 0, 0)),
        out_shape=jax.ShapeDtypeStruct((owners, FEAT, 128), BF16),
        scratch_shapes=[
            pltpu.VMEM(ids.shape, ids.dtype),
            pltpu.VMEM(rows.shape, rows.dtype),
            pltpu.VMEM(cols.shape, cols.dtype),
            pltpu.VMEM(values.shape, values.dtype),
            pltpu.VMEM((256, count), BF16),
            pltpu.VMEM((FEAT, count), F32),
            pltpu.VMEM((owners // steps // 2, count), BF16),
            pltpu.VMEM((owners // steps // 2 * SENT, 128), F32),
            pltpu.VMEM((owners // steps // 2 * SENT, 128), F32),
            pltpu.SemaphoreType.DMA((4,)),
        ],
        compiler_params=pltpu.CompilerParams(vmem_limit_bytes=58 << 20),
        cost_estimate=pl.CostEstimate(flops=2 * 2048 * 256 * 8192, bytes_accessed=3 << 20, transcendentals=0),
        name="pack",
    )(ids, rows, cols, values)


def setconv_kernel(where_ref, got_ref, cot_ref, s_ref, a_ref, b_ref, acc_ref):
    step = pl.program_id(0)
    x = jnp.concatenate([got_ref[k] for k in range(got_ref.shape[0])], axis=1).astype(F32)
    n = x.shape[1]
    alpha = math.sqrt(0.5 / math.log(2.0)) / spread_cells
    row = (x[24:25] + x[25:26]) * alpha
    col = (x[26:27] + x[27:28]) * alpha
    row_mid = (lax.broadcasted_iota(jnp.int32, (TR, n), 0).astype(F32) + 0.5) * alpha
    col_mid = (lax.broadcasted_iota(jnp.int32, (TC, n), 0).astype(F32) + 0.5) * alpha
    row_weight = jnp.exp2(-jnp.square(row - row_mid))
    col_weight = jnp.exp2(-jnp.square(col - col_mid)).astype(BF16)
    values = x[:24]
    weighted = jnp.concatenate([values * row_weight[i : i + 1] for i in range(TR)], axis=0).astype(BF16)
    term = dot_nt(weighted, col_weight)

    @pl.when(step == 0)
    def _():
        acc_ref[...] = term

    @pl.when(step > 0)
    def _():
        acc_ref[...] += term

    @pl.when(step == pl.num_programs(0) - 1)
    def _():
        none = jnp.zeros((FEAT - 24, TC), F32)
        for g in range(TR // 4):
            rows = []
            for i in range(4 * g, 4 * g + 4):
                rows += [acc_ref[24 * i : 24 * i + 24], none]
            s_ref[:, g * 128 : (g + 1) * 128] = jnp.concatenate(rows, axis=0).T.astype(BF16)
        even_lon, _ = evens(where_ref)
        for g in range(SG):
            left, right = s_ref[:16, g * 128 : (g + 1) * 128], s_ref[TC - 16 :, g * 128 : (g + 1) * 128]
            a_ref[g] = jnp.where(even_lon, right, left)
            b_ref[g] = jnp.where(even_lon, left, right)
        left, right = cot_ref[:, :16, :], cot_ref[:, TC - 16 :, :]
        a_ref[SG:] = jnp.where(even_lon, right, left)
        b_ref[SG:] = jnp.where(even_lon, left, right)


def setconv(where, got, cot):
    steps = 1
    fixed = lambda *shape: pl.BlockSpec(shape, lambda i: (0,) * len(shape))
    lanes = TR * FEAT
    shapes = [(TC, lanes), (SG + TR, 16, C), (SG + TR, 16, C)]
    return pl.pallas_call(
        setconv_kernel,
        grid=(steps,),
        in_specs=[
            pl.BlockSpec(memory_space=pltpu.SMEM),
            pl.BlockSpec((got.shape[0] // steps, FEAT, 128), lambda i: (i, 0, 0)),
            fixed(*cot.shape),
        ],
        out_specs=[fixed(*s) for s in shapes],
        out_shape=[jax.ShapeDtypeStruct(s, BF16) for s in shapes],
        scratch_shapes=[pltpu.VMEM((TR * 24, TC), F32)],
        compiler_params=pltpu.CompilerParams(vmem_limit_bytes=16 << 20),
        cost_estimate=pl.CostEstimate(
            flops=2 * 384 * 256 * 16384, bytes_accessed=2 << 20, transcendentals=144 * 16384
        ),
        name="setconv",
    )(where, got, cot)


def join_kernel(where_ref, a_ref, b_ref, s_ref, cot_ref, c_out, d_out):
    even_lon, even_lat = evens(where_ref)
    right = jnp.where(even_lon, a_ref[...], b_ref[...])
    left = jnp.where(even_lon, b_ref[...], a_ref[...])
    centre = slice(16, 16 + TC)
    for out, first in ((c_out, ~even_lat), (d_out, even_lat)):
        out[0, :16] = jnp.where(first, left[0], left[SG - 1])
        out[0, centre] = jnp.where(first, s_ref[:, :128], s_ref[:, -128:])
        out[0, 16 + TC :] = jnp.where(first, right[0], right[SG - 1])
        out[1:, :16] = jnp.where(first, left[SG : SG + 2], left[-2:])
        out[1:, centre] = jnp.where(first, cot_ref[:2], cot_ref[TR - 2 :])
        out[1:, 16 + TC :] = jnp.where(first, right[SG : SG + 2], right[-2:])


def join(where, a, b, s, cot):
    vmem = pl.BlockSpec(memory_space=pltpu.VMEM)
    return pl.pallas_call(
        join_kernel,
        in_specs=[pl.BlockSpec(memory_space=pltpu.SMEM)] + [vmem] * 4,
        out_specs=[vmem] * 2,
        out_shape=[jax.ShapeDtypeStruct((3, TC + 32, C), BF16)] * 2,
        cost_estimate=pl.CostEstimate(flops=0, bytes_accessed=1 << 18, transcendentals=0),
        compiler_params=pltpu.CompilerParams(vmem_limit_bytes=8 << 20),
        name="join",
    )(where, a, b, s, cot)


def shifted_copies(flat_ref, out_ref, begin, parts):
    def body(k, carry):
        at = pl.multiple_of(begin + k * PART, 16)
        for s in range(3):
            out_ref[pl.ds(at, PART), s * C : (s + 1) * C] = flat_ref[pl.ds(at + 7 + s, PART), :].astype(BF16)
        return carry

    lax.fori_loop(0, parts, body, 0)


def three_rows(src_ref, at, rows):
    return jnp.concatenate(
        [src_ref[pl.ds(at + (r - 1) * PITCH, rows), :] for r in range(3)], axis=1
    )


def conv_rows(src_ref, at, rows, weights):
    return dot(three_rows(src_ref, at, rows), jnp.concatenate(weights, axis=0))


def back_rows(src_ref, at, rows, weights):
    return dot_nt(three_rows(src_ref, at, rows), jnp.concatenate(weights, axis=1))


def fill_flat(flat_ref, begin, end, centre, left, right):
    first = lax.broadcasted_iota(jnp.int32, (16, C), 0) < 8
    flat_ref[place(begin) - 8 : place(begin) + 8] = left(begin)
    for i in range(begin, end):
        at = 8 + place(i)
        flat_ref[at : at + TC] = centre(i)
        after = jnp.where(first, right(i), left(i + 1)) if i < end - 1 else right(i)
        flat_ref[at + TC : at + PITCH] = after


def clear_flat(flat_ref, begin, end):
    flat_ref[begin:end] = jnp.zeros((end - begin, C), F32)


def evens(where_ref):
    return where_ref[1] % 2 == 0, where_ref[0] % 2 == 0


def arrange_back(w_ref, out_ref):
    for r in range(3):
        for s in range(3):
            out_ref[r, :, s * C : (s + 1) * C] = w_ref[2 - r, 2 - s]


def prep_kernel(cot_ref, embed_ref, w1_ref, w2_ref, cot_t_ref, wide_ref, back1_ref, back2_ref, own_ref):
    for i in range(TR):
        own_ref[i * PITCH : i * PITCH + TC] = cot_ref[i]
        own_ref[i * PITCH + TC : (i + 1) * PITCH] = jnp.zeros((PITCH - TC, C), BF16)
    transpose_flat(own_ref, cot_t_ref)
    values = embed_ref.shape[0]
    padded = jnp.concatenate([embed_ref[...].astype(F32), jnp.zeros((FEAT - values, C), F32)], axis=0).astype(BF16)
    wide_ref[...] = jnp.zeros_like(wide_ref)
    for k in range(4):
        wide_ref[k * FEAT : (k + 1) * FEAT, k * C : (k + 1) * C] = padded
    arrange_back(w1_ref, back1_ref)
    arrange_back(w2_ref, back2_ref)


def prep(cot, w_embed, w_first, w_second):
    vmem = pl.BlockSpec(memory_space=pltpu.VMEM)
    return pl.pallas_call(
        prep_kernel,
        in_specs=[vmem] * 4,
        out_specs=[vmem] * 4,
        out_shape=[
            jax.ShapeDtypeStruct((C, TR * PITCH), BF16),
            jax.ShapeDtypeStruct((4 * FEAT, 4 * C), BF16),
            jax.ShapeDtypeStruct((3, C, 3 * C), BF16),
            jax.ShapeDtypeStruct((3, C, 3 * C), BF16),
        ],
        scratch_shapes=[pltpu.VMEM((TR * PITCH, C), BF16)],
        compiler_params=pltpu.CompilerParams(vmem_limit_bytes=16 << 20),
        cost_estimate=pl.CostEstimate(flops=1 << 20, bytes_accessed=4 << 20, transcendentals=0),
        name="prep",
    )(cot, w_embed, w_first, w_second)


def mid_kernel(where_ref, cot_ref, s_ref, a_ref, b_ref, back_ref, wide_ref, w1_ref,
               hg_ref, x_ref, pre_ref, flat_ref, copies_ref):
    even_lon, _ = evens(where_ref)
    left = jnp.where(even_lon, b_ref[SG:], a_ref[SG:])
    right = jnp.where(even_lon, a_ref[SG:], b_ref[SG:])
    row = lambda rows: lambda i: rows[i].astype(F32)
    clear_flat(flat_ref, 0, place(0) - 8)
    clear_flat(flat_ref, 8 + place(TR), flat_ref.shape[0])
    fill_flat(flat_ref, 0, TR, row(cot_ref), row(left), row(right))
    shifted_copies(flat_ref, copies_ref, 0, LEN // PART)

    def body(k, carry):
        at = pl.multiple_of(FIRST + k * 3 * PART, 16)
        hg_ref[pl.ds(at, 3 * PART), :] = back_rows(copies_ref, at, 3 * PART, [back_ref[0], back_ref[1], back_ref[2]])
        return carry

    lax.fori_loop(0, 3, body, 0)

    wide = wide_ref[...]

    def rows_of(groups):
        groups = [dot(group, wide) for group in groups]
        return lambda i: groups[i // 4][:, i % 4 * C : (i % 4 + 1) * C]

    centre = rows_of([s_ref[:, g * 128 : (g + 1) * 128] for g in range(SG)])
    left = rows_of([jnp.where(even_lon, b_ref[g], a_ref[g]) for g in range(SG)])
    right = rows_of([jnp.where(even_lon, a_ref[g], b_ref[g]) for g in range(SG)])
    fill_flat(flat_ref, 0, TR, centre, left, right)
    shifted_copies(flat_ref, x_ref, 0, LEN // PART)

    def pre_body(k, carry):
        at = pl.multiple_of(FIRST + k * 3 * PART, 16)
        pre_ref[pl.ds(at, 3 * PART), :] = conv_rows(x_ref, at, 3 * PART, taps(w1_ref, (0, 1, 2)))
        return carry

    lax.fori_loop(0, 3, pre_body, 0)


def taps(w_ref, order):
    return [w_ref[r].reshape(3 * C, C) for r in order]


def transpose_flat(own_ref, out_ref):
    out_ref[...] = own_ref[...].T


def mid(where, cot, s, a, b, back, wide, w_first):
    vmem = pl.BlockSpec(memory_space=pltpu.VMEM)
    return pl.pallas_call(
        mid_kernel,
        in_specs=[pl.BlockSpec(memory_space=pltpu.SMEM)] + [vmem] * 7,
        out_specs=[vmem] * 3,
        out_shape=[
            jax.ShapeDtypeStruct((LEN, C), F32),
            jax.ShapeDtypeStruct((LEN, 3 * C), BF16),
            jax.ShapeDtypeStruct((LEN, C), F32),
        ],
        scratch_shapes=[pltpu.VMEM((LEN + 16, C), F32), pltpu.VMEM((LEN, 3 * C), BF16)],
        compiler_params=pltpu.CompilerParams(vmem_limit_bytes=24 << 20),
        cost_estimate=pl.CostEstimate(flops=2 * 2736 * 1152 * 256, bytes_accessed=4 << 20, transcendentals=0),
        name="mid",
    )(where, cot, s, a, b, back, wide, w_first)


def main_kernel(where_ref, cot_ref, s_ref, a_ref, b_ref, c_ref, d_ref,
                wide_ref, w1_ref, w2_ref, back1_ref, back2_ref, cot_t_ref, hg_in, x_in, pre_in,
                field_ref, keep_ref, send_ref, hg_ref, x_ref, pre_ref,
                red_ref, flat_ref, h_ref, own_ref, own_t_ref, eg_ref):
    even_lon, even_lat = evens(where_ref)
    north = where_ref[0] == 0
    south = where_ref[0] == where_ref[2] - 1
    north_row, south_row = jnp.where(north, 2, 0), jnp.where(south, 0, 2)
    pad, centre, tail = slice(0, 16), slice(16, 16 + TC), slice(16 + TC, 32 + TC)

    def edge(k):
        up = jnp.where(even_lat, d_ref[k], c_ref[k])
        down = jnp.where(even_lat, c_ref[k], d_ref[k])
        left = lambda i: jnp.where(even_lon, b_ref[i], a_ref[i])
        right = lambda i: jnp.where(even_lon, a_ref[i], b_ref[i])
        return up, down, left, right

    up0, down0, left, right = edge(1)
    up1, down1, _, _ = edge(2)

    def cot_rows(part, inner):
        near_up, far_up = jnp.where(north, up0[part], up1[part]), jnp.where(north, up1[part], up0[part])
        near_down, far_down = jnp.where(south, down1[part], down0[part]), jnp.where(south, down0[part], down1[part])
        outer = {-1: near_up, -2: far_up, TR: near_down, TR + 1: far_down}
        return lambda i: (outer[i] if i in outer else inner(i)).astype(F32)

    rows = (
        cot_rows(centre, lambda i: cot_ref[i]),
        cot_rows(pad, lambda i: left(SG + i)),
        cot_rows(tail, lambda i: right(SG + i)),
    )
    fill_flat(flat_ref, -2, 2, *rows)
    fill_flat(flat_ref, TR - 2, TR + 2, *rows)
    shifted_copies(flat_ref, h_ref, 0, 2)
    shifted_copies(flat_ref, h_ref, place(TR - 2) - 32, 2)
    at = place(-1) - 16
    got = back_rows(h_ref, at, PART, [back2_ref[north_row], back2_ref[1], back2_ref[2]])
    hg_ref[at + 8 : at + PART - 8] = got[8:-8]
    at = place(TR - 1) - 16
    got = back_rows(h_ref, at, PART, [back2_ref[0], back2_ref[1], back2_ref[south_row]])
    hg_ref[at + 8 : at + PART - 8] = got[8:-8]

    wide = wide_ref[...]
    up, down, left, right = edge(0)

    def embed_rows(part, first, last):
        block = lambda rows, k: rows[:, k * C : (k + 1) * C]
        up_, down_ = dot(up[part], wide), dot(down[part], wide)
        first, last = dot(first, wide), dot(last, wide)
        outer = {
            -1: jnp.where(north, block(up_, 0), block(up_, 3)),
            -2: jnp.where(north, block(up_, 1), block(up_, 2)),
            TR: jnp.where(south, block(down_, 3), block(down_, 0)),
            TR + 1: jnp.where(south, block(down_, 2), block(down_, 1)),
        }
        return lambda i: outer[i] if i in outer else block(first, i) if i < 4 else block(last, i - TR + 4)

    rows = (
        embed_rows(centre, s_ref[:, :128], s_ref[:, -128:]),
        embed_rows(pad, left(0), left(SG - 1)),
        embed_rows(tail, right(0), right(SG - 1)),
    )
    clear_flat(flat_ref, 0, 8)
    fill_flat(flat_ref, -2, 1, *rows)
    fill_flat(flat_ref, TR - 1, TR + 2, *rows)
    clear_flat(flat_ref, 8 + place(TR + 2), flat_ref.shape[0])
    shifted_copies(flat_ref, x_ref, 0, 1)
    shifted_copies(flat_ref, x_ref, place(TR) - 16, 1)

    for at in (place(-1) - 16, place(TR - 1) - 16):
        got = conv_rows(x_ref, at, PART, taps(w1_ref, (0, 1, 2)))
        pre_ref[at + 8 : at + PART - 8] = got[8:-8]

    def pole_pre(at):
        got = conv_rows(x_ref, at, PITCH + 16, taps(w1_ref, (2, 1, 0)))
        pre_ref[at + 8 : at + PITCH + 8] = got[8:-8]

    @pl.when(north)
    def _():
        pole_pre(place(-1) - 16)

    @pl.when(south)
    def _():
        pole_pre(place(TR) - 16)

    flat_ref[8 + FIRST - 16 : 8 + FIRST] = jnp.zeros((16, C), F32)
    flat_ref[8 + FIRST + 9 * PART : 24 + FIRST + 9 * PART] = jnp.zeros((16, C), F32)

    def hidden_body(k, carry):
        at = pl.multiple_of(FIRST + k * PART, 16)
        pre = pre_ref[pl.ds(at, PART), :]
        flat_ref[pl.ds(at + 8, PART), :] = pre / (1.0 + jnp.exp(-pre))
        return carry

    lax.fori_loop(0, 9, hidden_body, 0)
    shifted_copies(flat_ref, h_ref, FIRST, 9)

    def field_body(k, carry):
        at = pl.multiple_of(OWN + k * WIDE * PITCH, 16)
        got = conv_rows(h_ref, at, WIDE * PITCH, taps(w2_ref, (0, 1, 2))).astype(BF16)
        for u in range(WIDE):
            field_ref[WIDE * k + u] = got[u * PITCH : u * PITCH + TC]
        return carry

    lax.fori_loop(0, TR // WIDE, field_body, 0)

    def weight_grad(src_ref, grad_t_ref, half):
        for r in range(3):
            at = OWN + (r - 1) * PITCH
            got = dot(grad_t_ref[...], src_ref[at : at + TR * PITCH]).astype(BF16)
            for s in range(3):
                to = (3 * r + s) * C
                red_ref[half, to : to + C] = got[:, s * C : (s + 1) * C]

    weight_grad(h_ref, cot_t_ref, 0)

    def grad_body(k, carry):
        at = pl.multiple_of(FIRST + k * PART, 16)
        pre = pre_ref[pl.ds(at, PART), :]
        sig = 1.0 / (1.0 + jnp.exp(-pre))
        flat_ref[pl.ds(at + 8, PART), :] = hg_ref[pl.ds(at, PART), :] * (sig * (1.0 + pre * (1.0 - sig)))
        return carry

    lax.fori_loop(0, 9, grad_body, 0)
    shifted_copies(flat_ref, h_ref, FIRST, 9)
    for i in range(TR):
        at = 8 + place(i)
        own_ref[i * PITCH : i * PITCH + TC] = flat_ref[at : at + TC].astype(BF16)
        own_ref[i * PITCH + TC : (i + 1) * PITCH] = jnp.zeros((PITCH - TC, C), BF16)
    transpose_flat(own_ref, own_t_ref)
    weight_grad(x_ref, own_t_ref, 1)


    def eg_body(k, carry):
        at = pl.multiple_of(OWN + k * WIDE * PITCH, 16)
        got = back_rows(h_ref, at, WIDE * PITCH, [back1_ref[0], back1_ref[1], back1_ref[2]])
        eg_ref[pl.ds(pl.multiple_of(k * WIDE * PITCH, 16), WIDE * PITCH), :] = got.astype(BF16)
        return carry

    lax.fori_loop(0, TR // WIDE, eg_body, 0)

    @pl.when(north)
    def _():
        got = back_rows(h_ref, OWN, PITCH, [back1_ref[2], back1_ref[1], back1_ref[2]])
        eg_ref[:PITCH] = got.astype(BF16)

    @pl.when(south)
    def _():
        got = back_rows(h_ref, place(TR - 1), PITCH, [back1_ref[0], back1_ref[1], back1_ref[0]])
        eg_ref[(TR - 1) * PITCH :] = got.astype(BF16)

    total = jnp.zeros((FEAT, C), F32)
    for g in range(TR // 4):
        s_t = s_ref[:, g * 128 : (g + 1) * 128].T
        for k in range(4):
            i = 4 * g + k
            total += dot(s_t[k * FEAT : (k + 1) * FEAT], eg_ref[i * PITCH : i * PITCH + TC])
    red_ref[0, 9 * C :] = jnp.zeros((FEAT, C), BF16)
    red_ref[1, 9 * C :] = total.astype(BF16)
    core = where_ref[1] % 2
    keep_ref[...] = red_ref[core]
    send_ref[...] = red_ref[1 - core]


def main(where, cot, s, halo, wide, w_first, w_second, back1, back2, cot_t, hg, x, pre):
    vmem = pl.BlockSpec(memory_space=pltpu.VMEM)
    return pl.pallas_call(
        main_kernel,
        in_specs=[pl.BlockSpec(memory_space=pltpu.SMEM)] + [vmem] * 15,
        out_specs=[vmem] * 6,
        out_shape=[
            jax.ShapeDtypeStruct((TR, TC, C), BF16),
            jax.ShapeDtypeStruct((HALF, C), BF16),
            jax.ShapeDtypeStruct((HALF, C), BF16),
            jax.ShapeDtypeStruct(hg.shape, hg.dtype),
            jax.ShapeDtypeStruct(x.shape, x.dtype),
            jax.ShapeDtypeStruct(pre.shape, pre.dtype),
        ],
        input_output_aliases={13: 3, 14: 4, 15: 5},
        scratch_shapes=[
            pltpu.VMEM((2, HALF, C), BF16),
            pltpu.VMEM((LEN + 16, C), F32),
            pltpu.VMEM((LEN, 3 * C), BF16),
            pltpu.VMEM((TR * PITCH, C), BF16),
            pltpu.VMEM((C, TR * PITCH), BF16),
            pltpu.VMEM((TR * PITCH, C), BF16),
        ],
        compiler_params=pltpu.CompilerParams(vmem_limit_bytes=32 << 20),
        cost_estimate=pl.CostEstimate(flops=8 << 30, bytes_accessed=6 << 20, transcendentals=1 << 20),
        name="main",
    )(where, cot, s, *halo, wide, w_first, w_second, back1, back2, cot_t, hg, x, pre)


def turn_kernel(own_ref, out_ref):
    for k in range(9):
        out_ref[k] = own_ref[k * C : (k + 1) * C].T


def turn(own):
    vmem = pl.BlockSpec(memory_space=pltpu.VMEM)
    return pl.pallas_call(
        turn_kernel,
        in_specs=[vmem],
        out_specs=vmem,
        out_shape=jax.ShapeDtypeStruct((9, C, C), BF16),
        compiler_params=pltpu.CompilerParams(vmem_limit_bytes=8 << 20),
        cost_estimate=pl.CostEstimate(flops=1 << 20, bytes_accessed=1 << 20, transcendentals=0),
        name="turn",
    )(own)


def unpack_kernel(where_ref, own_ref, turned_ref, other_ref, embed_ref, first_ref, second_ref):
    even = where_ref[1] % 2 == 0
    for r in range(3):
        for s in range(3):
            k = 3 * r + s
            mine, other = turned_ref[k], other_ref[k * C : (k + 1) * C].T
            first_ref[r, s] = jnp.where(even, other, mine).astype(F32)
            second_ref[r, s] = jnp.where(even, mine, other).astype(F32)
    embed = jnp.where(even, other_ref[9 * C : 9 * C + FEAT], own_ref[9 * C : 9 * C + FEAT])
    embed_ref[...] = embed[: embed_ref.shape[0]].astype(F32)


def unpack(where, own, turned, other, values):
    vmem = pl.BlockSpec(memory_space=pltpu.VMEM)
    return pl.pallas_call(
        unpack_kernel,
        in_specs=[pl.BlockSpec(memory_space=pltpu.SMEM), vmem, vmem, vmem],
        out_specs=[vmem] * 3,
        out_shape=[
            jax.ShapeDtypeStruct((values, C), F32),
            jax.ShapeDtypeStruct((3, 3, C, C), F32),
            jax.ShapeDtypeStruct((3, 3, C, C), F32),
        ],
        compiler_params=pltpu.CompilerParams(vmem_limit_bytes=16 << 20),
        name="unpack",
    )(where, own, turned, other)


def swaps(bands, sectors):
    number = lambda lat, lon: lat * sectors + lon % sectors

    def across(lat, lon):
        if lat % 2:
            return number(lat + 1, lon) if lat < bands - 1 else number(lat, lon + sectors // 2)
        return number(lat - 1, lon) if lat > 0 else number(lat, lon + sectors // 2)

    def swap(of):
        pairs = [(number(i, j), of(i, j)) for i in range(bands) for j in range(sectors)]
        return lambda x: lax.ppermute(x, ALL, pairs)

    return (
        swap(lambda i, j: number(i, j ^ 1)),
        swap(lambda i, j: number(i, j + 1 if j % 2 else j - 1)),
        swap(lambda i, j: number(i ^ 1, j)),
        swap(across),
    )


def per_device(obs_values, tile_ids, obs_rows, obs_cols, w_embed, w_first, w_second, cotangent):
    bands, sectors = lax.axis_size("lat"), lax.axis_size("lon")
    owners = bands * sectors
    count, values = obs_values.shape
    where = jnp.stack(
        [lax.axis_index("lat"), lax.axis_index("lon"), jnp.int32(bands), jnp.int32(sectors)]
    ).astype(jnp.int32)
    swap_a, swap_b, swap_c, swap_d = swaps(bands, sectors)
    packed = pack(tile_ids.T, obs_rows.reshape(1, count), obs_cols.reshape(1, count), obs_values.T)
    got = lax.all_to_all(packed, ALL, 0, 0, tiled=True)
    cot_t, wide, back1, back2 = prep(cotangent, w_embed, w_first, w_second)
    s, a, b = setconv(where, got, cotangent)
    a, b = swap_a(a), swap_b(b)
    c, d = join(where, a, b, s, cotangent)
    hg, x, pre = mid(where, cotangent, s, a, b, back2, wide, w_first)
    halo = (a, b, swap_c(c), swap_d(d))
    field, keep, send, _, _, _ = main(where, cotangent, s, halo, wide, w_first, w_second, back1, back2, cot_t, hg, x, pre)

    chips = owners // 2
    groups = [[2 * k + core for k in range(chips)] for core in range(2)]
    half = keep.astype(F32) + swap_a(send).astype(F32)
    half = jnp.pad(half.astype(BF16), ((0, chips * RED - HALF), (0, 0))).reshape(chips, RED, C)
    parts = lax.all_to_all(half, ALL, 0, 0, axis_index_groups=groups, tiled=True)
    summed = jnp.sum(parts.astype(F32), axis=0).astype(BF16)
    spread = jnp.broadcast_to(summed[None], (chips, RED, C))
    own = lax.all_to_all(spread, ALL, 0, 0, axis_index_groups=groups, tiled=True).reshape(chips * RED, C)
    other = swap_a(own)
    grad_embed, grad_first, grad_second = unpack(where, own, turn(own), other, values)
    return (field, grad_embed, grad_first, grad_second)


def solution(mesh):
    in_specs = (
        P(ALL, None),
        P(ALL, None),
        P(ALL),
        P(ALL),
        P(),
        P(),
        P(),
        P("lat", "lon", None),
    )
    out_specs = (P("lat", "lon", None), P(), P(), P())
    return jax.shard_map(
        per_device, mesh=mesh, in_specs=in_specs, out_specs=out_specs, check_vma=False
    )
```
